512 devices in a mesh: img: 2 (over core), xy: 256 (over z, y, x).
Axes of the slice: x: 4, y: 8, z: 8, core: 2. Of those that a mesh axis runs over, the one named last changes fastest.
Arguments:
- images: float32 [4, 6, 16, 512, 512], P('img', None, None, 'xy'), may hold values from -12 to 12
Outputs:
- new_images: float32 [4, 6, 16, 512, 512], P('img', None, None, 'xy')
- knots: float32 [4], replicated
The draws below stay inside these ranges and needn't reach their ends.
All inputs are finite; a program needn't handle non-finite values.
Results may differ from the reference program's by a relative error of at most 0.0009.
Values sent between devices are 32-bit elements; how exact they have to be, the bound alone decides.
No kernel may reach another device: no remote copies, remote signals or barrier semaphores. Data moves between devices by JAX's collectives and lax.ppermute only.
A program may use at most 64 MiB of HBM per device.

```python
import math
import jax
import jax.numpy as jnp
from jax import lax

COMP = 6
Z = 16
NX = 512
M = 4
NY = 512


def draw_images(key, part):
    key = jax.random.fold_in(key, 7)
    key_step, key_base, key_path, key_noise, key_rows = jax.random.split(key, 5)
    spacing = jnp.exp(jax.random.uniform(key_step, (M,), jnp.float32, math.log(0.3), math.log(3.0)))
    first = jnp.arange(M) == 0
    increments = jnp.where(first, 0.0, spacing)
    increments = 2.0 * increments / jnp.sum(increments)
    row_factors = jax.random.uniform(key_rows, (M, NY), jnp.float32, 1.0, 3.0)
    position = jnp.cumsum(increments[:, None] * row_factors, axis=0)
    shape = (COMP, Z, NY, NX)
    base = jax.random.truncated_normal(key_base, -4.0, 4.0, shape, jnp.float32)
    path = jax.random.truncated_normal(key_path, -4.0, 4.0, shape, jnp.float32)
    noise = jax.random.truncated_normal(key_noise, -4.0, 4.0, (M,) + shape, jnp.float32)
    placed = position.reshape(M, 1, 1, NY, 1)
    row_scale = row_factors.reshape(M, 1, 1, NY, 1)
    fields = 0.4 * (base[None] + placed * path[None] + 0.03 * row_scale * noise)
    return fields.astype(jnp.float32)


def setup_inputs(seed: int = 0) -> dict:
    key_of = jax.random.split(jax.random.key(seed), 2)
    return {
        "images": draw_images(jax.random.fold_in(key_of[1], 71), 0),
    }


KAPPA_PHASE = 1.0
KAPPA_SOLUTE = 0.6
BARRIER = 1.5
COUPLING = 2.0
TIME_STEP = 0.05
EQUILIBRIUM = ((0.8, 0.1), (0.1, 0.8), (0.1, 0.1), (0.45, 0.45))

def stencil(padded):
    middle = padded[:, :, :, 1:-1, :]
    laplacian = padded[:, :, :, 2:, :] + padded[:, :, :, :-2, :]
    laplacian = laplacian + jnp.roll(middle, 1, axis=4) + jnp.roll(middle, -1, axis=4)
    raised = jnp.concatenate([middle[:, :, 1:], middle[:, :, -1:]], axis=2)
    lowered = jnp.concatenate([middle[:, :, :1], middle[:, :, :-1]], axis=2)
    laplacian = laplacian + raised + lowered - 6.0 * middle
    return (middle, laplacian)

def gradient_step(middle, laplacian):
    phases = [middle[:, i] for i in range(4)]
    solutes = [middle[:, 4 + s] for s in range(2)]
    excess = []
    for s in range(2):
        value = solutes[s]
        for i in range(4):
            value = value - EQUILIBRIUM[i][s] * phases[i]
        excess.append(value)
    squares = phases[0] * phases[0] + phases[1] * phases[1] + phases[2] * phases[2] + phases[3] * phases[3]
    forces = []
    for i in range(4):
        force = -KAPPA_PHASE * laplacian[:, i] + 2.0 * BARRIER * phases[i] * (squares - phases[i] * phases[i])
        for s in range(2):
            force = force - COUPLING * EQUILIBRIUM[i][s] * excess[s]
        forces.append(force)
    for s in range(2):
        forces.append(-KAPPA_SOLUTE * laplacian[:, 4 + s] + COUPLING * excess[s])
    return middle - TIME_STEP * jnp.stack(forces, axis=1)

def spline_tables(dist_sq):
    image_count = dist_sq.shape[0] + 1
    lengths = jnp.sqrt(1.0 + dist_sq)
    knots = jnp.concatenate([jnp.zeros((1,), lengths.dtype), jnp.cumsum(lengths)])
    knots = knots / knots[-1]
    widths = knots[1:] - knots[:-1]
    targets = jnp.arange(image_count).astype(knots.dtype) / (image_count - 1)
    below = lax.optimization_barrier(jnp.sum((knots[None, :] <= targets[:, None]).astype(jnp.int32), axis=1)) - 1
    interval = jnp.clip(below, 0, image_count - 2).astype(jnp.int32)
    columns = jnp.arange(image_count).astype(jnp.int32)
    lower = (columns[None, :] == interval[:, None]).astype(knots.dtype)
    upper = (columns[None, :] == interval[:, None] + 1).astype(knots.dtype)
    width_at = lax.optimization_barrier(jnp.sum(lower[:, :-1] * widths[None, :], axis=1))
    right_knot = lax.optimization_barrier(jnp.sum(upper * knots[None, :], axis=1))
    weight_a = (right_knot - targets) / width_at
    weight_b = 1.0 - weight_a
    values = weight_a[:, None] * lower + weight_b[:, None] * upper
    bends = (weight_a ** 3 - weight_a)[:, None] * lower + (weight_b ** 3 - weight_b)[:, None] * upper
    curves = bends * (width_at * width_at / 6.0)[:, None]
    return (knots, widths, values, curves)

def solve_second(fields, widths):
    shaped = widths.reshape(-1, 1, 1, 1, 1)
    rhs = 6.0 * ((fields[2:] - fields[1:-1]) / shaped[1:] - (fields[1:-1] - fields[:-2]) / shaped[:-1])
    inner = rhs.shape[0]
    flat = rhs.reshape(inner, -1)
    zero = jnp.zeros((1,), widths.dtype)
    main_band = 2.0 * (widths[:-1] + widths[1:])
    lower_band = jnp.concatenate([zero, widths[1:inner]])
    upper_band = jnp.concatenate([widths[1:inner], zero])
    solved = lax.linalg.tridiagonal_solve(lower_band, main_band, upper_band, flat)
    solved = solved.reshape(rhs.shape)
    edge = jnp.zeros((1,) + rhs.shape[1:], rhs.dtype)
    return jnp.concatenate([edge, solved, edge], axis=0)

def contract(mixing, fields):
    return jnp.einsum('jk,kabcd->jabcd', mixing, fields, precision=lax.Precision.HIGHEST)

def reference(images):
    padded = jnp.concatenate([images[:, :, :, -1:, :], images, images[:, :, :, :1, :]], axis=3)
    middle, laplacian = stencil(padded)
    stepped = gradient_step(middle, laplacian)
    change = stepped[1:] - stepped[:-1]
    dist_sq = lax.optimization_barrier(jnp.sum(change * change, axis=(1, 2, 3, 4)))
    knots, widths, values, curves = spline_tables(dist_sq)
    second = solve_second(stepped, widths)
    new_images = contract(values, stepped) + contract(curves, second)
    return (new_images, knots)
```

```python
import jax
import jax.numpy as jnp
from jax import lax
from jax.sharding import Mesh, PartitionSpec as P

KAPPA_PHASE = 1.0
KAPPA_SOLUTE = 0.6
BARRIER = 1.5
COUPLING = 2.0
TIME_STEP = 0.05
EQUILIBRIUM = ((0.8, 0.1), (0.1, 0.8), (0.1, 0.1), (0.45, 0.45))
AXES = ("z", "y", "x")


def stencil(padded):
    middle = padded[:, :, :, 1:-1, :]
    laplacian = padded[:, :, :, 2:, :] + padded[:, :, :, :-2, :]
    laplacian = laplacian + jnp.roll(middle, 1, axis=4) + jnp.roll(middle, -1, axis=4)
    raised = jnp.concatenate([middle[:, :, 1:], middle[:, :, -1:]], axis=2)
    lowered = jnp.concatenate([middle[:, :, :1], middle[:, :, :-1]], axis=2)
    laplacian = laplacian + raised + lowered - 6.0 * middle
    return (middle, laplacian)


def gradient_step(middle, laplacian):
    phases = [middle[:, i] for i in range(4)]
    solutes = [middle[:, 4 + s] for s in range(2)]
    excess = []
    for s in range(2):
        value = solutes[s]
        for i in range(4):
            value = value - EQUILIBRIUM[i][s] * phases[i]
        excess.append(value)
    squares = (
        phases[0] * phases[0]
        + phases[1] * phases[1]
        + phases[2] * phases[2]
        + phases[3] * phases[3]
    )
    forces = []
    for i in range(4):
        force = -KAPPA_PHASE * laplacian[:, i] + 2.0 * BARRIER * phases[i] * (
            squares - phases[i] * phases[i]
        )
        for s in range(2):
            force = force - COUPLING * EQUILIBRIUM[i][s] * excess[s]
        forces.append(force)
    for s in range(2):
        forces.append(-KAPPA_SOLUTE * laplacian[:, 4 + s] + COUPLING * excess[s])
    return middle - TIME_STEP * jnp.stack(forces, axis=1)


def per_device(images):
    strips = lax.axis_size(AXES)
    up = [(i, (i + 1) % strips) for i in range(strips)]
    down = [((i + 1) % strips, i) for i in range(strips)]
    before = lax.ppermute(images[:, :, :, -1:, :], AXES, up)
    after = lax.ppermute(images[:, :, :, :1, :], AXES, down)
    padded = jnp.concatenate([before, images, after], axis=3)
    stepped = gradient_step(*stencil(padded))
    other = lax.ppermute(stepped, "img", [(0, 1), (1, 0)])
    first = lax.axis_index("img") == 0
    low = jnp.where(first, stepped, other)
    high = jnp.where(first, other, stepped)
    s = (low[0], low[1], high[0], high[1])
    gaps = [s[k + 1] - s[k] for k in range(3)]
    own = jnp.stack([jnp.sum(g * g) for g in gaps]) * 0.5
    dist_sq = lax.psum(own, ("img",) + AXES)
    lengths = jnp.sqrt(1.0 + dist_sq)
    l1, l2, l3 = lengths[0], lengths[1], lengths[2]
    total = l1 + l2 + l3
    k1, k2, k3 = l1 / total, (l1 + l2) / total, total / total
    k0 = jnp.zeros_like(k1)
    knots = (k0, k1, k2, k3)
    w = (k1, k2 - k1, k3 - k2)
    main1, main2 = 2.0 * (w[0] + w[1]), 2.0 * (w[1] + w[2])
    rhs1 = 6.0 * (gaps[1] / w[1] - gaps[0] / w[0])
    rhs2 = 6.0 * (gaps[2] / w[2] - gaps[1] / w[1])
    det = main1 * main2 - w[1] * w[1]
    second1 = (main2 * rhs1 - w[1] * rhs2) / det
    second2 = (main1 * rhs2 - w[1] * rhs1) / det
    zero = jnp.zeros_like(k1)
    new = []
    for j in range(2):
        target = jnp.where(first, j / 3.0, (j + 2) / 3.0).astype(jnp.float32)
        below = sum((k <= target).astype(jnp.int32) for k in knots) - 1
        at = jnp.clip(below, 0, 2)
        h = jnp.where(at == 0, w[0], jnp.where(at == 1, w[1], w[2]))
        right = jnp.where(at == 0, k1, jnp.where(at == 1, k2, k3))
        a = (right - target) / h
        b = 1.0 - a
        ca = (a * a * a - a) * (h * h / 6.0)
        cb = (b * b * b - b) * (h * h / 6.0)
        v = [
            jnp.where(at == k, a, zero) + jnp.where(at == k - 1, b, zero)
            for k in range(4)
        ]
        c1 = jnp.where(at == 1, ca, zero) + jnp.where(at == 0, cb, zero)
        c2 = jnp.where(at == 2, ca, zero) + jnp.where(at == 1, cb, zero)
        new.append(
            v[0] * s[0] + v[1] * s[1] + v[2] * s[2] + v[3] * s[3] + c1 * second1 + c2 * second2
        )
    return jnp.stack(new), jnp.stack(knots)


def solution(mesh):
    fine = Mesh(mesh.devices.reshape(2, 4, 8, 8), ("img",) + AXES)
    spec = P("img", None, None, AXES, None)
    return jax.shard_map(
        per_device, mesh=fine, in_specs=(spec,), out_specs=(spec, P()), check_vma=False
    )
```

```python
import jax
import jax.numpy as jnp
from jax import lax
from jax.sharding import Mesh, PartitionSpec as P

KAPPA_PHASE = 1.0
KAPPA_SOLUTE = 0.6
BARRIER = 1.5
COUPLING = 2.0
TIME_STEP = 0.05
EQUILIBRIUM = ((0.8, 0.1), (0.1, 0.8), (0.1, 0.1), (0.45, 0.45))
AXES = ("z", "y", "x")


def stencil(padded):
    middle = padded[:, :, :, 1:-1, :]
    laplacian = padded[:, :, :, 2:, :] + padded[:, :, :, :-2, :]
    laplacian = laplacian + jnp.roll(middle, 1, axis=4) + jnp.roll(middle, -1, axis=4)
    raised = jnp.concatenate([middle[:, :, 1:], middle[:, :, -1:]], axis=2)
    lowered = jnp.concatenate([middle[:, :, :1], middle[:, :, :-1]], axis=2)
    laplacian = laplacian + raised + lowered - 6.0 * middle
    return (middle, laplacian)


def gradient_step(middle, laplacian):
    phases = [middle[:, i] for i in range(4)]
    solutes = [middle[:, 4 + s] for s in range(2)]
    excess = []
    for s in range(2):
        value = solutes[s]
        for i in range(4):
            value = value - EQUILIBRIUM[i][s] * phases[i]
        excess.append(value)
    squares = (
        phases[0] * phases[0]
        + phases[1] * phases[1]
        + phases[2] * phases[2]
        + phases[3] * phases[3]
    )
    forces = []
    for i in range(4):
        force = -KAPPA_PHASE * laplacian[:, i] + 2.0 * BARRIER * phases[i] * (
            squares - phases[i] * phases[i]
        )
        for s in range(2):
            force = force - COUPLING * EQUILIBRIUM[i][s] * excess[s]
        forces.append(force)
    for s in range(2):
        forces.append(-KAPPA_SOLUTE * laplacian[:, 4 + s] + COUPLING * excess[s])
    return middle - TIME_STEP * jnp.stack(forces, axis=1)


def exchange_sum(part, axes):
    sent = jnp.broadcast_to(part, (lax.axis_size(axes),) + part.shape)
    return jnp.sum(lax.all_to_all(sent, axes, 0, 0, tiled=True), axis=0)


def per_device(images):
    strips = lax.axis_size(AXES)
    up = [(i, (i + 1) % strips) for i in range(strips)]
    down = [((i + 1) % strips, i) for i in range(strips)]
    before = lax.ppermute(images[:, :, :, -1:, :], AXES, up)
    after = lax.ppermute(images[:, :, :, :1, :], AXES, down)
    padded = jnp.concatenate([before, images, after], axis=3)
    stepped = gradient_step(*stencil(padded))
    other = lax.ppermute(stepped, "img", [(0, 1), (1, 0)])
    first = lax.axis_index("img") == 0
    low = jnp.where(first, stepped, other)
    high = jnp.where(first, other, stepped)
    s = (low[0], low[1], high[0], high[1])
    gaps = [s[k + 1] - s[k] for k in range(3)]
    own = jnp.stack([jnp.sum(g * g) for g in gaps]) * 0.5
    own = jnp.broadcast_to(jnp.pad(own, (0, 5))[:, None], (8, 128))
    own = exchange_sum(own, ("img", "x"))
    own = exchange_sum(own, ("z", "y"))
    dist_sq = own[:3, 0]
    lengths = jnp.sqrt(1.0 + dist_sq)
    l1, l2, l3 = lengths[0], lengths[1], lengths[2]
    total = l1 + l2 + l3
    k1, k2, k3 = l1 / total, (l1 + l2) / total, total / total
    k0 = jnp.zeros_like(k1)
    knots = (k0, k1, k2, k3)
    w = (k1, k2 - k1, k3 - k2)
    main1, main2 = 2.0 * (w[0] + w[1]), 2.0 * (w[1] + w[2])
    rhs1 = 6.0 * (gaps[1] / w[1] - gaps[0] / w[0])
    rhs2 = 6.0 * (gaps[2] / w[2] - gaps[1] / w[1])
    det = main1 * main2 - w[1] * w[1]
    second1 = (main2 * rhs1 - w[1] * rhs2) / det
    second2 = (main1 * rhs2 - w[1] * rhs1) / det
    zero = jnp.zeros_like(k1)
    new = []
    for j in range(2):
        target = jnp.where(first, j / 3.0, (j + 2) / 3.0).astype(jnp.float32)
        below = sum((k <= target).astype(jnp.int32) for k in knots) - 1
        at = jnp.clip(below, 0, 2)
        h = jnp.where(at == 0, w[0], jnp.where(at == 1, w[1], w[2]))
        right = jnp.where(at == 0, k1, jnp.where(at == 1, k2, k3))
        a = (right - target) / h
        b = 1.0 - a
        ca = (a * a * a - a) * (h * h / 6.0)
        cb = (b * b * b - b) * (h * h / 6.0)
        v = [
            jnp.where(at == k, a, zero) + jnp.where(at == k - 1, b, zero)
            for k in range(4)
        ]
        c1 = jnp.where(at == 1, ca, zero) + jnp.where(at == 0, cb, zero)
        c2 = jnp.where(at == 2, ca, zero) + jnp.where(at == 1, cb, zero)
        new.append(
            v[0] * s[0] + v[1] * s[1] + v[2] * s[2] + v[3] * s[3] + c1 * second1 + c2 * second2
        )
    return jnp.stack(new), jnp.stack(knots)


def solution(mesh):
    fine = Mesh(mesh.devices.reshape(2, 4, 8, 8), ("img",) + AXES)
    spec = P("img", None, None, AXES, None)
    return jax.shard_map(
        per_device, mesh=fine, in_specs=(spec,), out_specs=(spec, P()), check_vma=False
    )
```

```python
import functools
import jax
import jax.numpy as jnp
from jax import lax
from jax.experimental import pallas as pl
from jax.experimental.pallas import tpu as pltpu
from jax.sharding import Mesh, PartitionSpec as P

KAPPA_PHASE = 1.0
KAPPA_SOLUTE = 0.6
BARRIER = 1.5
COUPLING = 2.0
TIME_STEP = 0.05
EQUILIBRIUM = ((0.8, 0.1), (0.1, 0.8), (0.1, 0.1), (0.45, 0.45))
STRIP = ("z", "y", "x")
FIELDS, PLANES = 6, 16
HALF = PLANES // 2
TILE = (8, 128)
VMEM = pl.BlockSpec(memory_space=pltpu.VMEM)
PARAMS = pltpu.CompilerParams(vmem_limit_bytes=48 * 1024 * 1024)


def even_sublanes():
    return lax.broadcasted_iota(jnp.int32, TILE, 0) % 2 == 0


def pack_kernel(images, own, far, both):
    core = lax.axis_index("img")
    even = even_sublanes()
    first = jnp.full(TILE, core, jnp.int32) == 0

    def field(i, carry):
        k, f = i // FIELDS, i % FIELDS
        for z in range(HALF):
            low, high = images[k, f, z], images[k, f, z + HALF]
            row0 = jnp.where(even, low, pltpu.roll(high, 1, 0))
            row1 = jnp.where(even, pltpu.roll(low, 7, 0), high)
            mine = jnp.where(first, row0, row1)
            rest = jnp.where(first, row1, row0)
            own[k, f, z] = mine
            far[k, f, z] = rest
            both[0, k, f, z] = mine
            both[1, k, f, z] = rest
        return carry

    lax.fori_loop(0, 2 * FIELDS, field, 0)


def step_image(center, beside, halo, j, stepped, g):
    even = even_sublanes()
    lane = lax.broadcasted_iota(jnp.int32, TILE, 1)
    at_first, at_last = lane == 0, lane == 127
    for z in range(HALF):
        cells, sums = [], []
        for f in range(FIELDS):
            c = center[j, f, z]
            if z < HALF - 1:
                raised = center[j, f, z + 1]
            else:
                raised = jnp.where(even, pltpu.roll(center[j, f, 0], 7, 0), c)
            if z > 0:
                lowered = center[j, f, z - 1]
            else:
                lowered = jnp.where(even, c, pltpu.roll(center[j, f, HALF - 1], 1, 0))
            ahead = pltpu.roll(c, 127, 1)
            ahead = jnp.where(at_last, pltpu.roll(ahead, 6, 0), ahead)
            behind = pltpu.roll(c, 1, 1)
            behind = jnp.where(at_first, pltpu.roll(behind, 2, 0), behind)
            around = (beside[j, f, z] + halo[j, f, z]) + (raised + lowered) + (ahead + behind)
            cells.append(c)
            sums.append(around)
        squares = [cells[i] * cells[i] for i in range(4)]
        total = (squares[0] + squares[1]) + (squares[2] + squares[3])
        pulls = []
        for s in range(2):
            value = cells[4 + s]
            for i in range(4):
                value = value - EQUILIBRIUM[i][s] * cells[i]
            pulls.append((TIME_STEP * COUPLING) * value)
        for i in range(4):
            gain = (1.0 - 6.0 * TIME_STEP * KAPPA_PHASE) - (TIME_STEP * 2.0 * BARRIER) * (
                total - squares[i]
            )
            out = gain * cells[i] + (TIME_STEP * KAPPA_PHASE) * sums[i]
            out = out + (EQUILIBRIUM[i][0] * pulls[0] + EQUILIBRIUM[i][1] * pulls[1])
            stepped[g, i, z] = out
        for s in range(2):
            out = (1.0 - 6.0 * TIME_STEP * KAPPA_SOLUTE) * cells[4 + s]
            out = out + (TIME_STEP * KAPPA_SOLUTE) * sums[4 + s] - pulls[s]
            stepped[g, 4 + s, z] = out


def step_kernel(peers, both, sibling, halo_own, halo_sibling, stepped, part):
    core = lax.axis_index("img")

    def mine(j, carry):
        step_image(both.at[0], both.at[1], halo_own, j, stepped, 2 * core + j)
        return carry

    def theirs(j, carry):
        step_image(sibling.at[1], sibling.at[0], halo_sibling, j, stepped, 2 * (1 - core) + j)
        return carry

    lax.fori_loop(0, 2, mine, 0)
    lax.fori_loop(0, 2, theirs, 0)

    def gather(f, sums):
        new = []
        for k in range(3):
            terms = []
            for z in range(HALF):
                gap = stepped[k + 1, f, z] - stepped[k, f, z]
                terms.append(gap * gap)
            while len(terms) > 1:
                terms = [a + b for a, b in zip(terms[::2], terms[1::2])]
            new.append(sums[k] + terms[0])
        return tuple(new)

    zero = jnp.zeros(TILE, jnp.float32)
    sums = lax.fori_loop(0, FIELDS, gather, (zero, zero, zero))
    sub = lax.broadcasted_iota(jnp.int32, TILE, 0)
    out = zero
    for k in range(3):
        out = jnp.where(sub == k, jnp.sum(sums[k], axis=0, keepdims=True), out)
    for p in range(peers):
        part[p] = out


def resum_kernel(parts, out):
    total = parts[0]
    for p in range(1, parts.shape[0]):
        total = total + parts[p]
    for p in range(out.shape[0]):
        out[p] = total


def combine_kernel(parts, near, far, new, knots):
    core = lax.axis_index("img")
    even = even_sublanes()
    first = jnp.full(TILE, core, jnp.int32) == 0
    total = parts[0]
    for p in range(1, parts.shape[0]):
        total = total + parts[p]
    l1, l2, l3 = (
        jnp.sqrt(1.0 + jnp.broadcast_to(jnp.sum(total[k : k + 1], axis=1, keepdims=True), TILE))
        for k in range(3)
    )
    whole = l1 + l2 + l3
    k1, k2, k3 = l1 / whole, (l1 + l2) / whole, whole / whole
    w0, w1, w2 = k1, k2 - k1, k3 - k2
    main1, main2 = 2.0 * (w0 + w1), 2.0 * (w1 + w2)
    det = main1 * main2 - w1 * w1
    scale = 6.0 / det
    i0, i1, i2 = 1.0 / w0, 1.0 / w1, 1.0 / w2
    bend1 = (
        -main2 * i0 * scale,
        (main2 + w1) * i1 * scale,
        -w1 * i2 * scale,
    )
    bend2 = (
        w1 * i0 * scale,
        -(main1 + w1) * i1 * scale,
        main1 * i2 * scale,
    )
    zero = jnp.zeros(TILE, jnp.float32)
    values, gaps = [], []
    for j in range(2):
        target = jnp.where(first, jnp.float32(j / 3.0), jnp.float32((j + 2) / 3.0))
        below = 1 + sum((k <= target).astype(jnp.int32) for k in (k1, k2, k3)) - 1
        at = jnp.clip(below, 0, 2)
        h = jnp.where(at == 0, w0, jnp.where(at == 1, w1, w2))
        right = jnp.where(at == 0, k1, jnp.where(at == 1, k2, k3))
        a = (right - target) / h
        b = 1.0 - a
        curve = h * h * (1.0 / 6.0)
        ca, cb = (a * a * a - a) * curve, (b * b * b - b) * curve
        v = [jnp.where(at == k, a, jnp.where(at == k - 1, b, zero)) for k in range(4)]
        c1 = jnp.where(at == 1, ca, jnp.where(at == 0, cb, zero))
        c2 = jnp.where(at == 2, ca, jnp.where(at == 1, cb, zero))
        values.append(v)
        gaps.append([c1 * bend1[m] + c2 * bend2[m] for m in range(3)])
    knots[0] = jnp.float32(0.0)
    knots[1] = k1[0, 0]
    knots[2] = k2[0, 0]
    knots[3] = k3[0, 0]

    def resampled(rows, f, z):
        s = [rows[k, f, z] for k in range(4)]
        d = [s[k + 1] - s[k] for k in range(3)]
        out = []
        for j in range(2):
            v, e = values[j], gaps[j]
            straight = (v[0] * s[0] + v[1] * s[1]) + (v[2] * s[2] + v[3] * s[3])
            out.append(straight + (e[0] * d[0] + e[1] * d[1] + e[2] * d[2]))
        return out

    def field(f, carry):
        for z in range(HALF):
            mine, rest = resampled(near, f, z), resampled(far, f, z)
            for j in range(2):
                row0 = jnp.where(first, mine[j], rest[j])
                row1 = jnp.where(first, rest[j], mine[j])
                new[j, f, z] = jnp.where(even, row0, pltpu.roll(row1, 1, 0))
                new[j, f, z + HALF] = jnp.where(even, pltpu.roll(row0, 7, 0), row1)
        return carry

    lax.fori_loop(0, FIELDS, field, 0)


def in_vmem(x):
    return pltpu.with_memory_space_constraint(x, pltpu.VMEM)


def vmem(*shape):
    return pltpu.VMEM(shape, jnp.float32)


def resum(parts, peers):
    return pl.pallas_call(
        resum_kernel,
        out_shape=vmem(peers, *TILE),
        in_specs=[VMEM],
        out_specs=VMEM,
        compiler_params=PARAMS,
    )(in_vmem(parts))


def exchange(parts, axes):
    return lax.all_to_all(parts, axes, 0, 0, tiled=True)


def per_device(images):
    cores, strips = lax.axis_size("img"), lax.axis_size(STRIP)
    everyone = ("img",) + STRIP
    tiles = images.reshape(2, FIELDS, PLANES, 2, 4, 128).transpose(0, 1, 2, 4, 3, 5)
    tiles = tiles.reshape(2, FIELDS, PLANES, *TILE)
    packed = (2, FIELDS, HALF) + TILE
    own, far, both = pl.pallas_call(
        pack_kernel,
        out_shape=(vmem(*packed), vmem(*packed), vmem(2, *packed)),
        in_specs=[VMEM],
        out_specs=(VMEM, VMEM, VMEM),
        compiler_params=PARAMS,
    )(tiles)
    right = [(i + 1) % strips for i in range(strips)]
    left = [(i - 1) % strips for i in range(strips)]
    same = [(i, right[i]) for i in range(strips)]
    same += [(strips + i, strips + left[i]) for i in range(strips)]
    cross = [(i, strips + left[i]) for i in range(strips)]
    cross += [(strips + i, right[i]) for i in range(strips)]
    halo_own = lax.ppermute(far, everyone, same)
    halo_sibling = lax.ppermute(own, everyone, cross)
    swap = [(0, 1), (1, 0)]
    sibling = lax.ppermute(both, "img", swap)
    groups = (("img", "z"), ("y",), ("x",))
    sizes = [lax.axis_size(g) for g in groups]
    near, parts = pl.pallas_call(
        functools.partial(step_kernel, sizes[0]),
        out_shape=(vmem(4, *packed[1:]), vmem(sizes[0], *TILE)),
        in_specs=[VMEM] * 4,
        out_specs=(VMEM, VMEM),
        compiler_params=PARAMS,
    )(in_vmem(both), in_vmem(sibling), in_vmem(halo_own), in_vmem(halo_sibling))
    rest = lax.ppermute(near, "img", swap)
    parts = exchange(parts, groups[0])
    parts = exchange(resum(parts, sizes[1]), groups[1])
    parts = exchange(resum(parts, sizes[2]), groups[2])
    new, knots = pl.pallas_call(
        combine_kernel,
        out_shape=(
            jax.ShapeDtypeStruct((2, FIELDS, PLANES) + TILE, jnp.float32),
            jax.ShapeDtypeStruct((4,), jnp.float32),
        ),
        in_specs=[VMEM] * 3,
        out_specs=(VMEM, pl.BlockSpec(memory_space=pltpu.SMEM)),
        compiler_params=PARAMS,
    )(in_vmem(parts), in_vmem(near), in_vmem(rest))
    new = new.reshape(2, FIELDS, PLANES, 4, 2, 128).transpose(0, 1, 2, 4, 3, 5)
    return new.reshape(2, FIELDS, PLANES, 2, 512), knots


def solution(mesh):
    sizes = (4, 8, 8) if mesh.devices.size == 512 else (1, 1, mesh.devices.size // 2)
    fine = Mesh(mesh.devices.reshape(2, *sizes), ("img",) + STRIP)
    spec = P("img", None, None, STRIP, None)
    return jax.shard_map(
        per_device, mesh=fine, in_specs=(spec,), out_specs=(spec, P()), check_vma=False
    )
```

```python
import jax
import jax.numpy as jnp
from jax import lax
from jax.experimental import pallas as pl
from jax.experimental.pallas import tpu as pltpu
from jax.sharding import Mesh, PartitionSpec as P

KAPPA_PHASE = 1.0
KAPPA_SOLUTE = 0.6
BARRIER = 1.5
COUPLING = 2.0
TIME_STEP = 0.05
EQUILIBRIUM = ((0.8, 0.1), (0.1, 0.8), (0.1, 0.1), (0.45, 0.45))
STRIP = ("z", "y2", "y1", "y0", "x")
FIELDS, PLANES = 6, 16
HALF = PLANES // 2
CELLS = 4 * FIELDS * HALF
TILE = (8, 128)
VMEM = pl.BlockSpec(memory_space=pltpu.VMEM)
PARAMS = pltpu.CompilerParams(vmem_limit_bytes=48 * 1024 * 1024)


def cell(k, f, z):
    return (k * FIELDS + f) * HALF + z


def even_sublanes():
    return lax.broadcasted_iota(jnp.int32, TILE, 0) % 2 == 0


def pack_kernel(images, own, far):
    core = lax.axis_index("img")
    even = even_sublanes()
    first = jnp.full(TILE, core, jnp.int32) == 0

    def field(i, carry):
        k, f = i // FIELDS, i % FIELDS
        for z in range(HALF):
            low, high = images[k, f, z], images[k, f, z + HALF]
            row0 = jnp.where(even, low, pltpu.roll(high, 1, 0))
            row1 = jnp.where(even, pltpu.roll(low, 7, 0), high)
            own[k, f, z] = jnp.where(first, row0, row1)
            far[k, f, z] = jnp.where(first, row1, row0)
        return carry

    lax.fori_loop(0, 2 * FIELDS, field, 0)


def step_image(center, beside, halo, j, stepped, g):
    even = even_sublanes()
    lane = lax.broadcasted_iota(jnp.int32, TILE, 1)
    at_first, at_last = lane == 0, lane == 127
    for z in range(HALF):
        cells, sums = [], []
        for f in range(FIELDS):
            c = center[j, f, z]
            if z < HALF - 1:
                raised = center[j, f, z + 1]
            else:
                raised = jnp.where(even, pltpu.roll(center[j, f, 0], 7, 0), c)
            if z > 0:
                lowered = center[j, f, z - 1]
            else:
                lowered = jnp.where(even, c, pltpu.roll(center[j, f, HALF - 1], 1, 0))
            ahead = pltpu.roll(c, 127, 1)
            ahead = jnp.where(at_last, pltpu.roll(ahead, 6, 0), ahead)
            behind = pltpu.roll(c, 1, 1)
            behind = jnp.where(at_first, pltpu.roll(behind, 2, 0), behind)
            around = (beside[j, f, z] + halo[j, f, z]) + (raised + lowered) + (ahead + behind)
            cells.append(c)
            sums.append(around)
        squares = [cells[i] * cells[i] for i in range(4)]
        total = (squares[0] + squares[1]) + (squares[2] + squares[3])
        pulls = []
        for s in range(2):
            value = cells[4 + s]
            for i in range(4):
                value = value - EQUILIBRIUM[i][s] * cells[i]
            pulls.append((TIME_STEP * COUPLING) * value)
        for i in range(4):
            gain = (1.0 - 6.0 * TIME_STEP * KAPPA_PHASE) - (TIME_STEP * 2.0 * BARRIER) * (
                total - squares[i]
            )
            out = gain * cells[i] + (TIME_STEP * KAPPA_PHASE) * sums[i]
            out = out + (EQUILIBRIUM[i][0] * pulls[0] + EQUILIBRIUM[i][1] * pulls[1])
            stepped[cell(g, i, z)] = out
        for s in range(2):
            out = (1.0 - 6.0 * TIME_STEP * KAPPA_SOLUTE) * cells[4 + s]
            out = out + (TIME_STEP * KAPPA_SOLUTE) * sums[4 + s] - pulls[s]
            stepped[cell(g, 4 + s, z)] = out


def step_kernel(own, far, sib_far, sib_own, halo_own, halo_sibling, stepped):
    core = lax.axis_index("img")

    def mine(j, carry):
        step_image(own, far, halo_own, j, stepped, 2 * core + j)
        return carry

    def theirs(j, carry):
        step_image(sib_own, sib_far, halo_sibling, j, stepped, 2 * (1 - core) + j)
        return carry

    lax.fori_loop(0, 2, mine, 0)
    lax.fori_loop(0, 2, theirs, 0)

    def gather(f, sums):
        new = []
        for k in range(3):
            terms = []
            for z in range(HALF):
                gap = stepped[cell(k + 1, f, z)] - stepped[cell(k, f, z)]
                terms.append(gap * gap)
            while len(terms) > 1:
                terms = [a + b for a, b in zip(terms[::2], terms[1::2])]
            new.append(sums[k] + terms[0])
        return tuple(new)

    zero = jnp.zeros(TILE, jnp.float32)
    sums = lax.fori_loop(0, FIELDS, gather, (zero, zero, zero))
    sub = lax.broadcasted_iota(jnp.int32, TILE, 0)
    out = zero
    for k in range(3):
        out = jnp.where(sub == k, jnp.sum(sums[k], axis=0, keepdims=True), out)
    stepped[CELLS] = out


def combine_kernel(parts, near, far, new, knots):
    core = lax.axis_index("img")
    even = even_sublanes()
    first = jnp.full(TILE, core, jnp.int32) == 0
    total = parts[...]
    l1, l2, l3 = (
        jnp.sqrt(1.0 + jnp.broadcast_to(jnp.sum(total[k : k + 1], axis=1, keepdims=True), TILE))
        for k in range(3)
    )
    whole = l1 + l2 + l3
    k1, k2, k3 = l1 / whole, (l1 + l2) / whole, whole / whole
    w0, w1, w2 = k1, k2 - k1, k3 - k2
    main1, main2 = 2.0 * (w0 + w1), 2.0 * (w1 + w2)
    det = main1 * main2 - w1 * w1
    scale = 6.0 / det
    i0, i1, i2 = 1.0 / w0, 1.0 / w1, 1.0 / w2
    bend1 = (
        -main2 * i0 * scale,
        (main2 + w1) * i1 * scale,
        -w1 * i2 * scale,
    )
    bend2 = (
        w1 * i0 * scale,
        -(main1 + w1) * i1 * scale,
        main1 * i2 * scale,
    )
    zero = jnp.zeros(TILE, jnp.float32)
    values, gaps = [], []
    for j in range(2):
        target = jnp.where(first, jnp.float32(j / 3.0), jnp.float32((j + 2) / 3.0))
        below = 1 + sum((k <= target).astype(jnp.int32) for k in (k1, k2, k3)) - 1
        at = jnp.clip(below, 0, 2)
        h = jnp.where(at == 0, w0, jnp.where(at == 1, w1, w2))
        right = jnp.where(at == 0, k1, jnp.where(at == 1, k2, k3))
        a = (right - target) / h
        b = 1.0 - a
        curve = h * h * (1.0 / 6.0)
        ca, cb = (a * a * a - a) * curve, (b * b * b - b) * curve
        v = [jnp.where(at == k, a, jnp.where(at == k - 1, b, zero)) for k in range(4)]
        c1 = jnp.where(at == 1, ca, jnp.where(at == 0, cb, zero))
        c2 = jnp.where(at == 2, ca, jnp.where(at == 1, cb, zero))
        values.append(v)
        gaps.append([c1 * bend1[m] + c2 * bend2[m] for m in range(3)])
    knots[0] = jnp.float32(0.0)
    knots[1] = k1[0, 0]
    knots[2] = k2[0, 0]
    knots[3] = k3[0, 0]

    def resampled(rows, f, z):
        s = [rows[cell(k, f, z)] for k in range(4)]
        d = [s[k + 1] - s[k] for k in range(3)]
        out = []
        for j in range(2):
            v, e = values[j], gaps[j]
            straight = (v[0] * s[0] + v[1] * s[1]) + (v[2] * s[2] + v[3] * s[3])
            out.append(straight + (e[0] * d[0] + e[1] * d[1] + e[2] * d[2]))
        return out

    def field(f, carry):
        for z in range(HALF):
            mine, rest = resampled(near, f, z), resampled(far, f, z)
            for j in range(2):
                row0 = jnp.where(first, mine[j], rest[j])
                row1 = jnp.where(first, rest[j], mine[j])
                new[j, f, z] = jnp.where(even, row0, pltpu.roll(row1, 1, 0))
                new[j, f, z + HALF] = jnp.where(even, pltpu.roll(row0, 7, 0), row1)
        return carry

    lax.fori_loop(0, FIELDS, field, 0)


def in_vmem(x):
    return pltpu.with_memory_space_constraint(x, pltpu.VMEM)


def vmem(*shape):
    return pltpu.VMEM(shape, jnp.float32)


def sum_tiles(part, everyone):
    count = lax.axis_size(everyone)
    for axis in ("y0", "y1", "y2"):
        part = lax.psum(part, axis)
    for step in (1, 2, 4, 64, 128):
        pairs = [(i, i ^ step) for i in range(count)]
        part = part + lax.ppermute(part, everyone, pairs)
    return part


def per_device(images):
    everyone = ("img",) + STRIP
    strips = lax.axis_size(STRIP)
    tiles = images.reshape(2, FIELDS, PLANES, 2, 4, 128).transpose(0, 1, 2, 4, 3, 5)
    tiles = tiles.reshape(2, FIELDS, PLANES, *TILE)
    packed = (2, FIELDS, HALF) + TILE
    own, far = pl.pallas_call(
        pack_kernel,
        out_shape=(vmem(*packed), vmem(*packed)),
        in_specs=[VMEM],
        out_specs=(VMEM, VMEM),
        compiler_params=PARAMS,
    )(tiles)
    right = [(i + 1) % strips for i in range(strips)]
    left = [(i - 1) % strips for i in range(strips)]
    same = [(i, right[i]) for i in range(strips)]
    same += [(strips + i, strips + left[i]) for i in range(strips)]
    cross = [(i, strips + left[i]) for i in range(strips)]
    cross += [(strips + i, right[i]) for i in range(strips)]
    halo_own = lax.ppermute(far, everyone, same)
    halo_sibling = lax.ppermute(own, everyone, cross)
    swap = [(0, 1), (1, 0)]
    sib_far = lax.ppermute(own, "img", swap)
    sib_own = lax.ppermute(far, "img", swap)
    inputs = (own, far, sib_far, sib_own, halo_own, halo_sibling)
    near = pl.pallas_call(
        step_kernel,
        out_shape=vmem(CELLS + 1, *TILE),
        in_specs=[VMEM] * 6,
        out_specs=VMEM,
        compiler_params=PARAMS,
    )(*map(in_vmem, inputs))
    rest = lax.ppermute(near, "img", swap)
    parts = sum_tiles(near[CELLS] + rest[CELLS], everyone)
    new, knots = pl.pallas_call(
        combine_kernel,
        out_shape=(
            jax.ShapeDtypeStruct((2, FIELDS, PLANES) + TILE, jnp.float32),
            jax.ShapeDtypeStruct((4,), jnp.float32),
        ),
        in_specs=[VMEM] * 3,
        out_specs=(VMEM, pl.BlockSpec(memory_space=pltpu.SMEM)),
        compiler_params=PARAMS,
    )(in_vmem(parts), in_vmem(near), in_vmem(rest))
    new = new.reshape(2, FIELDS, PLANES, 4, 2, 128).transpose(0, 1, 2, 4, 3, 5)
    return new.reshape(2, FIELDS, PLANES, 2, 512), knots


def solution(mesh):
    fine = Mesh(mesh.devices.reshape(2, 4, 2, 2, 2, 8), ("img",) + STRIP)
    spec = P("img", None, None, STRIP, None)
    return jax.shard_map(
        per_device, mesh=fine, in_specs=(spec,), out_specs=(spec, P()), check_vma=False
    )
```

```python
import jax
import jax.numpy as jnp
from jax import lax
from jax.experimental import pallas as pl
from jax.experimental.pallas import tpu as pltpu
from jax.sharding import Mesh, PartitionSpec as P

KAPPA_PHASE = 1.0
KAPPA_SOLUTE = 0.6
BARRIER = 1.5
COUPLING = 2.0
TIME_STEP = 0.05
EQUILIBRIUM = ((0.8, 0.1), (0.1, 0.8), (0.1, 0.1), (0.45, 0.45))
STRIP = ("z", "yh", "yl", "x")
FIELDS, PLANES = 6, 16
HALF = PLANES // 2
CELLS = 4 * FIELDS * HALF
TILE = (8, 128)
VMEM = pl.BlockSpec(memory_space=pltpu.VMEM)
PARAMS = pltpu.CompilerParams(vmem_limit_bytes=48 * 1024 * 1024)


def cell(k, f, z):
    return (k * FIELDS + f) * HALF + z


def even_sublanes():
    return lax.broadcasted_iota(jnp.int32, TILE, 0) % 2 == 0


def pack_kernel(images, own, far, own_copy, far_copy):
    core = lax.axis_index("img")
    even = even_sublanes()
    first = jnp.full(TILE, core, jnp.int32) == 0

    def field(i, carry):
        k, f = i // FIELDS, i % FIELDS
        for z in range(HALF):
            low, high = images[k, f, z], images[k, f, z + HALF]
            row0 = jnp.where(even, low, pltpu.roll(high, 1, 0))
            row1 = jnp.where(even, pltpu.roll(low, 7, 0), high)
            mine = jnp.where(first, row0, row1)
            rest = jnp.where(first, row1, row0)
            own[k, f, z] = mine
            far[k, f, z] = rest
            own_copy[k, f, z] = mine
            far_copy[k, f, z] = rest
        return carry

    lax.fori_loop(0, 2 * FIELDS, field, 0)


def step_image(center, beside, halo, j, stepped, g):
    even = even_sublanes()
    lane = lax.broadcasted_iota(jnp.int32, TILE, 1)
    at_first, at_last = lane == 0, lane == 127
    for z in range(HALF):
        cells, sums = [], []
        for f in range(FIELDS):
            c = center[j, f, z]
            if z < HALF - 1:
                raised = center[j, f, z + 1]
            else:
                raised = jnp.where(even, pltpu.roll(center[j, f, 0], 7, 0), c)
            if z > 0:
                lowered = center[j, f, z - 1]
            else:
                lowered = jnp.where(even, c, pltpu.roll(center[j, f, HALF - 1], 1, 0))
            ahead = pltpu.roll(c, 127, 1)
            ahead = jnp.where(at_last, pltpu.roll(ahead, 6, 0), ahead)
            behind = pltpu.roll(c, 1, 1)
            behind = jnp.where(at_first, pltpu.roll(behind, 2, 0), behind)
            around = (beside[j, f, z] + halo[j, f, z]) + (raised + lowered) + (ahead + behind)
            cells.append(c)
            sums.append(around)
        squares = [cells[i] * cells[i] for i in range(4)]
        total = (squares[0] + squares[1]) + (squares[2] + squares[3])
        pulls = []
        for s in range(2):
            value = cells[4 + s]
            for i in range(4):
                value = value - EQUILIBRIUM[i][s] * cells[i]
            pulls.append((TIME_STEP * COUPLING) * value)
        for i in range(4):
            gain = (1.0 - 6.0 * TIME_STEP * KAPPA_PHASE) - (TIME_STEP * 2.0 * BARRIER) * (
                total - squares[i]
            )
            out = gain * cells[i] + (TIME_STEP * KAPPA_PHASE) * sums[i]
            out = out + (EQUILIBRIUM[i][0] * pulls[0] + EQUILIBRIUM[i][1] * pulls[1])
            stepped[cell(g, i, z)] = out
        for s in range(2):
            out = (1.0 - 6.0 * TIME_STEP * KAPPA_SOLUTE) * cells[4 + s]
            out = out + (TIME_STEP * KAPPA_SOLUTE) * sums[4 + s] - pulls[s]
            stepped[cell(g, 4 + s, z)] = out


def step_kernel(own, far, sib_far, sib_own, halo_own, halo_sibling, stepped):
    core = lax.axis_index("img")

    def mine(j, carry):
        step_image(own, far, halo_own, j, stepped, 2 * core + j)
        return carry

    def theirs(j, carry):
        step_image(sib_own, sib_far, halo_sibling, j, stepped, 2 * (1 - core) + j)
        return carry

    lax.fori_loop(0, 2, mine, 0)
    lax.fori_loop(0, 2, theirs, 0)

    def gather(f, sums):
        new = []
        for k in range(3):
            terms = []
            for z in range(HALF):
                gap = stepped[cell(k + 1, f, z)] - stepped[cell(k, f, z)]
                terms.append(gap * gap)
            while len(terms) > 1:
                terms = [a + b for a, b in zip(terms[::2], terms[1::2])]
            new.append(sums[k] + terms[0])
        return tuple(new)

    zero = jnp.zeros(TILE, jnp.float32)
    sums = lax.fori_loop(0, FIELDS, gather, (zero, zero, zero))
    sub = lax.broadcasted_iota(jnp.int32, TILE, 0)
    out = zero
    for k in range(3):
        out = jnp.where(sub == k, jnp.sum(sums[k], axis=0, keepdims=True), out)
    stepped[CELLS] = out


def combine_kernel(parts, near, far, new, knots):
    core = lax.axis_index("img")
    even = even_sublanes()
    first = jnp.full(TILE, core, jnp.int32) == 0
    total = parts[0]
    for p in range(1, parts.shape[0]):
        total = total + parts[p]
    l1, l2, l3 = (
        jnp.sqrt(1.0 + jnp.broadcast_to(jnp.sum(total[k : k + 1], axis=1, keepdims=True), TILE))
        for k in range(3)
    )
    whole = l1 + l2 + l3
    k1, k2, k3 = l1 / whole, (l1 + l2) / whole, whole / whole
    w0, w1, w2 = k1, k2 - k1, k3 - k2
    main1, main2 = 2.0 * (w0 + w1), 2.0 * (w1 + w2)
    det = main1 * main2 - w1 * w1
    scale = 6.0 / det
    i0, i1, i2 = 1.0 / w0, 1.0 / w1, 1.0 / w2
    bend1 = (
        -main2 * i0 * scale,
        (main2 + w1) * i1 * scale,
        -w1 * i2 * scale,
    )
    bend2 = (
        w1 * i0 * scale,
        -(main1 + w1) * i1 * scale,
        main1 * i2 * scale,
    )
    zero = jnp.zeros(TILE, jnp.float32)
    values, gaps = [], []
    for j in range(2):
        target = jnp.where(first, jnp.float32(j / 3.0), jnp.float32((j + 2) / 3.0))
        below = 1 + sum((k <= target).astype(jnp.int32) for k in (k1, k2, k3)) - 1
        at = jnp.clip(below, 0, 2)
        h = jnp.where(at == 0, w0, jnp.where(at == 1, w1, w2))
        right = jnp.where(at == 0, k1, jnp.where(at == 1, k2, k3))
        a = (right - target) / h
        b = 1.0 - a
        curve = h * h * (1.0 / 6.0)
        ca, cb = (a * a * a - a) * curve, (b * b * b - b) * curve
        v = [jnp.where(at == k, a, jnp.where(at == k - 1, b, zero)) for k in range(4)]
        c1 = jnp.where(at == 1, ca, jnp.where(at == 0, cb, zero))
        c2 = jnp.where(at == 2, ca, jnp.where(at == 1, cb, zero))
        values.append(v)
        gaps.append([c1 * bend1[m] + c2 * bend2[m] for m in range(3)])
    knots[0] = jnp.float32(0.0)
    knots[1] = k1[0, 0]
    knots[2] = k2[0, 0]
    knots[3] = k3[0, 0]

    def resampled(rows, f, z):
        s = [rows[cell(k, f, z)] for k in range(4)]
        d = [s[k + 1] - s[k] for k in range(3)]
        out = []
        for j in range(2):
            v, e = values[j], gaps[j]
            straight = (v[0] * s[0] + v[1] * s[1]) + (v[2] * s[2] + v[3] * s[3])
            out.append(straight + (e[0] * d[0] + e[1] * d[1] + e[2] * d[2]))
        return out

    def field(f, carry):
        for z in range(HALF):
            mine, rest = resampled(near, f, z), resampled(far, f, z)
            for j in range(2):
                row0 = jnp.where(first, mine[j], rest[j])
                row1 = jnp.where(first, rest[j], mine[j])
                new[j, f, z] = jnp.where(even, row0, pltpu.roll(row1, 1, 0))
                new[j, f, z + HALF] = jnp.where(even, pltpu.roll(row0, 7, 0), row1)
        return carry

    lax.fori_loop(0, FIELDS, field, 0)


def in_vmem(x):
    return pltpu.with_memory_space_constraint(x, pltpu.VMEM)


def vmem(*shape):
    return pltpu.VMEM(shape, jnp.float32)


def add_kernel(near, rest, out):
    total = near[CELLS] + rest[CELLS]
    for p in range(out.shape[0]):
        out[p] = total


def resum_kernel(parts, out):
    total = parts[0]
    for p in range(1, parts.shape[0]):
        total = total + parts[p]
    for p in range(out.shape[0]):
        out[p] = total


def spread(kernel, peers, *inputs):
    return pl.pallas_call(
        kernel,
        out_shape=vmem(peers, *TILE),
        in_specs=[VMEM] * len(inputs),
        out_specs=VMEM,
        compiler_params=PARAMS,
    )(*map(in_vmem, inputs))


def per_device(images):
    everyone = ("img",) + STRIP
    strips = lax.axis_size(STRIP)
    tiles = images.reshape(2, FIELDS, PLANES, 2, 4, 128).transpose(0, 1, 2, 4, 3, 5)
    tiles = tiles.reshape(2, FIELDS, PLANES, *TILE)
    packed = (2, FIELDS, HALF) + TILE
    own, far, own_copy, far_copy = pl.pallas_call(
        pack_kernel,
        out_shape=(vmem(*packed),) * 4,
        in_specs=[VMEM],
        out_specs=(VMEM,) * 4,
        compiler_params=PARAMS,
    )(tiles)
    right = [(i + 1) % strips for i in range(strips)]
    left = [(i - 1) % strips for i in range(strips)]
    same = [(i, right[i]) for i in range(strips)]
    same += [(strips + i, strips + left[i]) for i in range(strips)]
    cross = [(i, strips + left[i]) for i in range(strips)]
    cross += [(strips + i, right[i]) for i in range(strips)]
    halo_own = lax.ppermute(far_copy, everyone, same)
    halo_sibling = lax.ppermute(own_copy, everyone, cross)
    swap = [(0, 1), (1, 0)]
    sib_far = lax.ppermute(own, "img", swap)
    sib_own = lax.ppermute(far, "img", swap)
    inputs = (own, far, sib_far, sib_own, halo_own, halo_sibling)
    near = pl.pallas_call(
        step_kernel,
        out_shape=vmem(CELLS + 1, *TILE),
        in_specs=[VMEM] * 6,
        out_specs=VMEM,
        compiler_params=PARAMS,
    )(*map(in_vmem, inputs))
    rest = lax.ppermute(near, "img", swap)
    groups = (("z", "yh"), ("yl", "x"))
    parts = spread(add_kernel, lax.axis_size(groups[0]), near, rest)
    parts = lax.all_to_all(parts, groups[0], 0, 0, tiled=True)
    parts = spread(resum_kernel, lax.axis_size(groups[1]), parts)
    parts = lax.all_to_all(parts, groups[1], 0, 0, tiled=True)
    new, knots = pl.pallas_call(
        combine_kernel,
        out_shape=(
            jax.ShapeDtypeStruct((2, FIELDS, PLANES) + TILE, jnp.float32),
            jax.ShapeDtypeStruct((4,), jnp.float32),
        ),
        in_specs=[VMEM] * 3,
        out_specs=(VMEM, pl.BlockSpec(memory_space=pltpu.SMEM)),
        compiler_params=PARAMS,
    )(in_vmem(parts), in_vmem(near), in_vmem(rest))
    new = new.reshape(2, FIELDS, PLANES, 4, 2, 128).transpose(0, 1, 2, 4, 3, 5)
    return new.reshape(2, FIELDS, PLANES, 2, 512), knots


def solution(mesh):
    fine = Mesh(mesh.devices.reshape(2, 4, 4, 2, 8), ("img",) + STRIP)
    spec = P("img", None, None, STRIP, None)
    return jax.shard_map(
        per_device, mesh=fine, in_specs=(spec,), out_specs=(spec, P()), check_vma=False
    )
```

```python
import jax
import jax.numpy as jnp
from jax import lax
from jax.experimental import pallas as pl
from jax.experimental.pallas import tpu as pltpu
from jax.sharding import Mesh, PartitionSpec as P

KAPPA_PHASE = 1.0
KAPPA_SOLUTE = 0.6
BARRIER = 1.5
COUPLING = 2.0
TIME_STEP = 0.05
EQUILIBRIUM = ((0.8, 0.1), (0.1, 0.8), (0.1, 0.1), (0.45, 0.45))
STRIP = ("z", "y", "x")
FIELDS, PLANES = 6, 16
HALF = PLANES // 2
CELLS = 4 * FIELDS * HALF
TILE = (8, 128)
VMEM = pl.BlockSpec(memory_space=pltpu.VMEM)
PARAMS = pltpu.CompilerParams(vmem_limit_bytes=48 * 1024 * 1024)


def cell(k, f, z):
    return (k * FIELDS + f) * HALF + z


def even_sublanes():
    return lax.broadcasted_iota(jnp.int32, TILE, 0) % 2 == 0


def pack_kernel(images, own, far, own_copy, far_copy):
    core = lax.axis_index("img")
    even = even_sublanes()
    first = jnp.full(TILE, core, jnp.int32) == 0

    def field(i, carry):
        k, f = i // FIELDS, i % FIELDS
        for z in range(HALF):
            low, high = images[k, f, z], images[k, f, z + HALF]
            row0 = jnp.where(even, low, pltpu.roll(high, 1, 0))
            row1 = jnp.where(even, pltpu.roll(low, 7, 0), high)
            mine = jnp.where(first, row0, row1)
            rest = jnp.where(first, row1, row0)
            own[k, f, z] = mine
            far[k, f, z] = rest
            own_copy[k, f, z] = mine
            far_copy[k, f, z] = rest
        return carry

    lax.fori_loop(0, 2 * FIELDS, field, 0)


def step_image(center, beside, halo, j, stepped, g):
    even = even_sublanes()
    lane = lax.broadcasted_iota(jnp.int32, TILE, 1)
    at_first, at_last = lane == 0, lane == 127
    for z in range(HALF):
        cells, sums = [], []
        for f in range(FIELDS):
            c = center[j, f, z]
            if z < HALF - 1:
                raised = center[j, f, z + 1]
            else:
                raised = jnp.where(even, pltpu.roll(center[j, f, 0], 7, 0), c)
            if z > 0:
                lowered = center[j, f, z - 1]
            else:
                lowered = jnp.where(even, c, pltpu.roll(center[j, f, HALF - 1], 1, 0))
            ahead = pltpu.roll(c, 127, 1)
            ahead = jnp.where(at_last, pltpu.roll(ahead, 6, 0), ahead)
            behind = pltpu.roll(c, 1, 1)
            behind = jnp.where(at_first, pltpu.roll(behind, 2, 0), behind)
            around = (beside[j, f, z] + halo[j, f, z]) + (raised + lowered) + (ahead + behind)
            cells.append(c)
            sums.append(around)
        squares = [cells[i] * cells[i] for i in range(4)]
        total = (squares[0] + squares[1]) + (squares[2] + squares[3])
        pulls = []
        for s in range(2):
            value = cells[4 + s]
            for i in range(4):
                value = value - EQUILIBRIUM[i][s] * cells[i]
            pulls.append((TIME_STEP * COUPLING) * value)
        for i in range(4):
            gain = (1.0 - 6.0 * TIME_STEP * KAPPA_PHASE) - (TIME_STEP * 2.0 * BARRIER) * (
                total - squares[i]
            )
            out = gain * cells[i] + (TIME_STEP * KAPPA_PHASE) * sums[i]
            out = out + (EQUILIBRIUM[i][0] * pulls[0] + EQUILIBRIUM[i][1] * pulls[1])
            stepped[cell(g, i, z)] = out
        for s in range(2):
            out = (1.0 - 6.0 * TIME_STEP * KAPPA_SOLUTE) * cells[4 + s]
            out = out + (TIME_STEP * KAPPA_SOLUTE) * sums[4 + s] - pulls[s]
            stepped[cell(g, 4 + s, z)] = out


def step_kernel(own, far, sib_far, sib_own, halo_own, halo_sibling, stepped):
    core = lax.axis_index("img")

    def mine(j, carry):
        step_image(own, far, halo_own, j, stepped, 2 * core + j)
        return carry

    def theirs(j, carry):
        step_image(sib_own, sib_far, halo_sibling, j, stepped, 2 * (1 - core) + j)
        return carry

    lax.fori_loop(0, 2, mine, 0)
    lax.fori_loop(0, 2, theirs, 0)

    def gather(f, sums):
        new = []
        for k in range(3):
            terms = []
            for z in range(HALF):
                gap = stepped[cell(k + 1, f, z)] - stepped[cell(k, f, z)]
                terms.append(gap * gap)
            while len(terms) > 1:
                terms = [a + b for a, b in zip(terms[::2], terms[1::2])]
            new.append(sums[k] + terms[0])
        return tuple(new)

    zero = jnp.zeros(TILE, jnp.float32)
    sums = lax.fori_loop(0, FIELDS, gather, (zero, zero, zero))
    lane = lax.broadcasted_iota(jnp.int32, TILE, 1)
    out = zero
    for k in range(3):
        out = jnp.where(lane == k, jnp.sum(sums[k]), out)
    stepped[CELLS] = out


def combine_kernel(parts, near, far, new, knots):
    core = lax.axis_index("img")
    even = even_sublanes()
    first = jnp.full(TILE, core, jnp.int32) == 0
    terms = [parts[p] for p in range(parts.shape[0])]
    while len(terms) > 1:
        terms = [a + b for a, b in zip(terms[::2], terms[1::2])]
    lane = lax.broadcasted_iota(jnp.int32, TILE, 1)
    l1, l2, l3 = (
        jnp.sqrt(1.0 + jnp.full(TILE, jnp.sum(jnp.where(lane == k, terms[0], 0.0))))
        for k in range(3)
    )
    whole = l1 + l2 + l3
    k1, k2, k3 = l1 / whole, (l1 + l2) / whole, whole / whole
    w0, w1, w2 = k1, k2 - k1, k3 - k2
    main1, main2 = 2.0 * (w0 + w1), 2.0 * (w1 + w2)
    det = main1 * main2 - w1 * w1
    scale = 6.0 / det
    i0, i1, i2 = 1.0 / w0, 1.0 / w1, 1.0 / w2
    bend1 = (
        -main2 * i0 * scale,
        (main2 + w1) * i1 * scale,
        -w1 * i2 * scale,
    )
    bend2 = (
        w1 * i0 * scale,
        -(main1 + w1) * i1 * scale,
        main1 * i2 * scale,
    )
    zero = jnp.zeros(TILE, jnp.float32)
    values, gaps = [], []
    for j in range(2):
        target = jnp.where(first, jnp.float32(j / 3.0), jnp.float32((j + 2) / 3.0))
        below = 1 + sum((k <= target).astype(jnp.int32) for k in (k1, k2, k3)) - 1
        at = jnp.clip(below, 0, 2)
        h = jnp.where(at == 0, w0, jnp.where(at == 1, w1, w2))
        right = jnp.where(at == 0, k1, jnp.where(at == 1, k2, k3))
        a = (right - target) / h
        b = 1.0 - a
        curve = h * h * (1.0 / 6.0)
        ca, cb = (a * a * a - a) * curve, (b * b * b - b) * curve
        v = [jnp.where(at == k, a, jnp.where(at == k - 1, b, zero)) for k in range(4)]
        c1 = jnp.where(at == 1, ca, jnp.where(at == 0, cb, zero))
        c2 = jnp.where(at == 2, ca, jnp.where(at == 1, cb, zero))
        values.append(v)
        gaps.append([c1 * bend1[m] + c2 * bend2[m] for m in range(3)])
    knots[0] = jnp.float32(0.0)
    knots[1] = k1[0, 0]
    knots[2] = k2[0, 0]
    knots[3] = k3[0, 0]

    def resampled(rows, f, z):
        s = [rows[cell(k, f, z)] for k in range(4)]
        d = [s[k + 1] - s[k] for k in range(3)]
        out = []
        for j in range(2):
            v, e = values[j], gaps[j]
            straight = (v[0] * s[0] + v[1] * s[1]) + (v[2] * s[2] + v[3] * s[3])
            out.append(straight + (e[0] * d[0] + e[1] * d[1] + e[2] * d[2]))
        return out

    def field(f, carry):
        for z in range(HALF):
            mine, rest = resampled(near, f, z), resampled(far, f, z)
            for j in range(2):
                row0 = jnp.where(first, mine[j], rest[j])
                row1 = jnp.where(first, rest[j], mine[j])
                new[j, f, z] = jnp.where(even, row0, pltpu.roll(row1, 1, 0))
                new[j, f, z + HALF] = jnp.where(even, pltpu.roll(row0, 7, 0), row1)
        return carry

    lax.fori_loop(0, FIELDS, field, 0)


def in_vmem(x):
    return pltpu.with_memory_space_constraint(x, pltpu.VMEM)


def vmem(*shape):
    return pltpu.VMEM(shape, jnp.float32)


def add_kernel(near, rest, out):
    total = near[CELLS, 0:1, :] + rest[CELLS, 0:1, :]

    def row(p, carry):
        out[p] = total
        return carry

    lax.fori_loop(0, out.shape[0], row, 0, unroll=8)


def spread(kernel, peers, *inputs):
    return pl.pallas_call(
        kernel,
        out_shape=vmem(peers, 1, TILE[1]),
        in_specs=[VMEM] * len(inputs),
        out_specs=VMEM,
        compiler_params=PARAMS,
    )(*map(in_vmem, inputs))


def per_device(images):
    everyone = ("img",) + STRIP
    strips = lax.axis_size(STRIP)
    tiles = images.reshape(2, FIELDS, PLANES, 2, 4, 128).transpose(0, 1, 2, 4, 3, 5)
    tiles = tiles.reshape(2, FIELDS, PLANES, *TILE)
    packed = (2, FIELDS, HALF) + TILE
    own, far, own_copy, far_copy = pl.pallas_call(
        pack_kernel,
        out_shape=(vmem(*packed),) * 4,
        in_specs=[VMEM],
        out_specs=(VMEM,) * 4,
        compiler_params=PARAMS,
    )(tiles)
    right = [(i + 1) % strips for i in range(strips)]
    left = [(i - 1) % strips for i in range(strips)]
    same = [(i, right[i]) for i in range(strips)]
    same += [(strips + i, strips + left[i]) for i in range(strips)]
    cross = [(i, strips + left[i]) for i in range(strips)]
    cross += [(strips + i, right[i]) for i in range(strips)]
    halo_own = lax.ppermute(far_copy, everyone, same)
    halo_sibling = lax.ppermute(own_copy, everyone, cross)
    swap = [(0, 1), (1, 0)]
    sib_far = lax.ppermute(own, "img", swap)
    sib_own = lax.ppermute(far, "img", swap)
    inputs = (own, far, sib_far, sib_own, halo_own, halo_sibling)
    near = pl.pallas_call(
        step_kernel,
        out_shape=vmem(CELLS + 1, *TILE),
        in_specs=[VMEM] * 6,
        out_specs=VMEM,
        compiler_params=PARAMS,
    )(*map(in_vmem, inputs))
    rest = lax.ppermute(near, "img", swap)
    parts = spread(add_kernel, strips, near, rest)
    parts = lax.all_to_all(parts, STRIP, 0, 0, tiled=True)
    parts = parts.reshape(strips // TILE[0], *TILE)
    new, knots = pl.pallas_call(
        combine_kernel,
        out_shape=(
            jax.ShapeDtypeStruct((2, FIELDS, PLANES) + TILE, jnp.float32),
            jax.ShapeDtypeStruct((4,), jnp.float32),
        ),
        in_specs=[VMEM] * 3,
        out_specs=(VMEM, pl.BlockSpec(memory_space=pltpu.SMEM)),
        compiler_params=PARAMS,
    )(in_vmem(parts), in_vmem(near), in_vmem(rest))
    new = new.reshape(2, FIELDS, PLANES, 4, 2, 128).transpose(0, 1, 2, 4, 3, 5)
    return new.reshape(2, FIELDS, PLANES, 2, 512), knots


def solution(mesh):
    fine = Mesh(mesh.devices.reshape(2, 4, 8, 8), ("img",) + STRIP)
    spec = P("img", None, None, STRIP, None)
    return jax.shard_map(
        per_device, mesh=fine, in_specs=(spec,), out_specs=(spec, P()), check_vma=False
    )
```

```python
import jax
import jax.numpy as jnp
from jax import lax
from jax.experimental import pallas as pl
from jax.experimental.pallas import tpu as pltpu
from jax.sharding import Mesh, PartitionSpec as P

KAPPA_PHASE = 1.0
KAPPA_SOLUTE = 0.6
BARRIER = 1.5
COUPLING = 2.0
TIME_STEP = 0.05
EQUILIBRIUM = ((0.8, 0.1), (0.1, 0.8), (0.1, 0.1), (0.45, 0.45))
STRIP = ("z", "y", "x")
FIELDS, PLANES = 6, 16
HALF = PLANES // 2
CELLS = 4 * FIELDS * HALF
TILE = (8, 128)
VMEM = pl.BlockSpec(memory_space=pltpu.VMEM)
PARAMS = pltpu.CompilerParams(vmem_limit_bytes=48 * 1024 * 1024)


def cell(k, f, z):
    return (k * FIELDS + f) * HALF + z


def even_sublanes():
    return lax.broadcasted_iota(jnp.int32, TILE, 0) % 2 == 0


def pack_kernel(images, own, far, own_copy, far_copy):
    core = lax.axis_index("img")
    even = even_sublanes()
    first = jnp.full(TILE, core, jnp.int32) == 0

    def field(i, carry):
        k, f = i // FIELDS, i % FIELDS
        for z in range(HALF):
            low, high = images[k, f, z], images[k, f, z + HALF]
            row0 = jnp.where(even, low, pltpu.roll(high, 1, 0))
            row1 = jnp.where(even, pltpu.roll(low, 7, 0), high)
            mine = jnp.where(first, row0, row1)
            rest = jnp.where(first, row1, row0)
            own[k, f, z] = mine
            far[k, f, z] = rest
            own_copy[k, f, z] = mine
            far_copy[k, f, z] = rest
        return carry

    lax.fori_loop(0, 2 * FIELDS, field, 0)


def step_image(center, beside, halo, j, stepped, g):
    even = even_sublanes()
    lane = lax.broadcasted_iota(jnp.int32, TILE, 1)
    at_first, at_last = lane == 0, lane == 127
    for z in range(HALF):
        cells, sums = [], []
        for f in range(FIELDS):
            c = center[j, f, z]
            if z < HALF - 1:
                raised = center[j, f, z + 1]
            else:
                raised = jnp.where(even, pltpu.roll(center[j, f, 0], 7, 0), c)
            if z > 0:
                lowered = center[j, f, z - 1]
            else:
                lowered = jnp.where(even, c, pltpu.roll(center[j, f, HALF - 1], 1, 0))
            ahead = pltpu.roll(c, 127, 1)
            ahead = jnp.where(at_last, pltpu.roll(ahead, 6, 0), ahead)
            behind = pltpu.roll(c, 1, 1)
            behind = jnp.where(at_first, pltpu.roll(behind, 2, 0), behind)
            around = (beside[j, f, z] + halo[j, f, z]) + (raised + lowered) + (ahead + behind)
            cells.append(c)
            sums.append(around)
        squares = [cells[i] * cells[i] for i in range(4)]
        total = (squares[0] + squares[1]) + (squares[2] + squares[3])
        pulls = []
        for s in range(2):
            value = cells[4 + s]
            for i in range(4):
                value = value - EQUILIBRIUM[i][s] * cells[i]
            pulls.append((TIME_STEP * COUPLING) * value)
        for i in range(4):
            gain = (1.0 - 6.0 * TIME_STEP * KAPPA_PHASE) - (TIME_STEP * 2.0 * BARRIER) * (
                total - squares[i]
            )
            out = gain * cells[i] + (TIME_STEP * KAPPA_PHASE) * sums[i]
            out = out + (EQUILIBRIUM[i][0] * pulls[0] + EQUILIBRIUM[i][1] * pulls[1])
            stepped[cell(g, i, z)] = out
        for s in range(2):
            out = (1.0 - 6.0 * TIME_STEP * KAPPA_SOLUTE) * cells[4 + s]
            out = out + (TIME_STEP * KAPPA_SOLUTE) * sums[4 + s] - pulls[s]
            stepped[cell(g, 4 + s, z)] = out


def step_kernel(own, far, sib_far, sib_own, halo_own, halo_sibling, stepped, part):
    core = lax.axis_index("img")

    def mine(j, carry):
        step_image(own, far, halo_own, j, stepped, 2 * core + j)
        return carry

    def theirs(j, carry):
        step_image(sib_own, sib_far, halo_sibling, j, stepped, 2 * (1 - core) + j)
        return carry

    lax.fori_loop(0, 2, mine, 0)
    lax.fori_loop(0, 2, theirs, 0)

    def gather(f, sums):
        new = []
        for k in range(3):
            terms = []
            for z in range(HALF):
                gap = stepped[cell(k + 1, f, z)] - stepped[cell(k, f, z)]
                terms.append(gap * gap)
            while len(terms) > 1:
                terms = [a + b for a, b in zip(terms[::2], terms[1::2])]
            new.append(sums[k] + terms[0])
        return tuple(new)

    zero = jnp.zeros(TILE, jnp.float32)
    sums = lax.fori_loop(0, FIELDS, gather, (zero, zero, zero))
    lane = lax.broadcasted_iota(jnp.int32, TILE, 1)
    out = zero
    for k in range(3):
        out = jnp.where(lane == k, jnp.sum(sums[k]), out)
    part[0] = out[0:1]


def combine_kernel(parts, near, far, new, knots):
    core = lax.axis_index("img")
    even = even_sublanes()
    first = jnp.full(TILE, core, jnp.int32) == 0
    terms = [parts[p] for p in range(parts.shape[0])]
    while len(terms) > 1:
        terms = [a + b for a, b in zip(terms[::2], terms[1::2])]
    lane = lax.broadcasted_iota(jnp.int32, TILE, 1)
    l1, l2, l3 = (
        jnp.sqrt(1.0 + jnp.full(TILE, jnp.sum(jnp.where(lane == k, terms[0], 0.0))))
        for k in range(3)
    )
    whole = l1 + l2 + l3
    k1, k2, k3 = l1 / whole, (l1 + l2) / whole, whole / whole
    w0, w1, w2 = k1, k2 - k1, k3 - k2
    main1, main2 = 2.0 * (w0 + w1), 2.0 * (w1 + w2)
    det = main1 * main2 - w1 * w1
    scale = 6.0 / det
    i0, i1, i2 = 1.0 / w0, 1.0 / w1, 1.0 / w2
    bend1 = (
        -main2 * i0 * scale,
        (main2 + w1) * i1 * scale,
        -w1 * i2 * scale,
    )
    bend2 = (
        w1 * i0 * scale,
        -(main1 + w1) * i1 * scale,
        main1 * i2 * scale,
    )
    zero = jnp.zeros(TILE, jnp.float32)
    values, gaps = [], []
    for j in range(2):
        target = jnp.where(first, jnp.float32(j / 3.0), jnp.float32((j + 2) / 3.0))
        below = 1 + sum((k <= target).astype(jnp.int32) for k in (k1, k2, k3)) - 1
        at = jnp.clip(below, 0, 2)
        h = jnp.where(at == 0, w0, jnp.where(at == 1, w1, w2))
        right = jnp.where(at == 0, k1, jnp.where(at == 1, k2, k3))
        a = (right - target) / h
        b = 1.0 - a
        curve = h * h * (1.0 / 6.0)
        ca, cb = (a * a * a - a) * curve, (b * b * b - b) * curve
        v = [jnp.where(at == k, a, jnp.where(at == k - 1, b, zero)) for k in range(4)]
        c1 = jnp.where(at == 1, ca, jnp.where(at == 0, cb, zero))
        c2 = jnp.where(at == 2, ca, jnp.where(at == 1, cb, zero))
        values.append(v)
        gaps.append([c1 * bend1[m] + c2 * bend2[m] for m in range(3)])
    knots[0] = jnp.float32(0.0)
    knots[1] = k1[0, 0]
    knots[2] = k2[0, 0]
    knots[3] = k3[0, 0]

    def resampled(rows, f, z):
        s = [rows[cell(k, f, z)] for k in range(4)]
        d = [s[k + 1] - s[k] for k in range(3)]
        out = []
        for j in range(2):
            v, e = values[j], gaps[j]
            straight = (v[0] * s[0] + v[1] * s[1]) + (v[2] * s[2] + v[3] * s[3])
            out.append(straight + (e[0] * d[0] + e[1] * d[1] + e[2] * d[2]))
        return out

    def field(f, carry):
        for z in range(HALF):
            mine, rest = resampled(near, f, z), resampled(far, f, z)
            for j in range(2):
                row0 = jnp.where(first, mine[j], rest[j])
                row1 = jnp.where(first, rest[j], mine[j])
                new[j, f, z] = jnp.where(even, row0, pltpu.roll(row1, 1, 0))
                new[j, f, z + HALF] = jnp.where(even, pltpu.roll(row0, 7, 0), row1)
        return carry

    lax.fori_loop(0, FIELDS, field, 0)


def in_vmem(x):
    return pltpu.with_memory_space_constraint(x, pltpu.VMEM)


def vmem(*shape):
    return pltpu.VMEM(shape, jnp.float32)


def per_device(images):
    everyone = ("img",) + STRIP
    strips = lax.axis_size(STRIP)
    tiles = images.reshape(2, FIELDS, PLANES, 2, 4, 128).transpose(0, 1, 2, 4, 3, 5)
    tiles = tiles.reshape(2, FIELDS, PLANES, *TILE)
    packed = (2, FIELDS, HALF) + TILE
    own, far, own_copy, far_copy = pl.pallas_call(
        pack_kernel,
        out_shape=(vmem(*packed),) * 4,
        in_specs=[VMEM],
        out_specs=(VMEM,) * 4,
        compiler_params=PARAMS,
    )(tiles)
    right = [(i + 1) % strips for i in range(strips)]
    left = [(i - 1) % strips for i in range(strips)]
    same = [(i, right[i]) for i in range(strips)]
    same += [(strips + i, strips + left[i]) for i in range(strips)]
    cross = [(i, strips + left[i]) for i in range(strips)]
    cross += [(strips + i, right[i]) for i in range(strips)]
    halo_own = lax.ppermute(far_copy, everyone, same)
    halo_sibling = lax.ppermute(own_copy, everyone, cross)
    swap = [(0, 1), (1, 0)]
    sib_far = lax.ppermute(own, "img", swap)
    sib_own = lax.ppermute(far, "img", swap)
    inputs = (own, far, sib_far, sib_own, halo_own, halo_sibling)
    near, part = pl.pallas_call(
        step_kernel,
        out_shape=(vmem(CELLS, *TILE), jax.ShapeDtypeStruct((1, 1, TILE[1]), jnp.float32)),
        in_specs=[VMEM] * 6,
        out_specs=(VMEM, VMEM),
        compiler_params=PARAMS,
    )(*map(in_vmem, inputs))
    rest = lax.ppermute(near, "img", swap)
    parts = lax.all_gather(part, STRIP + ("img",), axis=0, tiled=True)
    parts = parts.reshape(-1, *TILE)
    new, knots = pl.pallas_call(
        combine_kernel,
        out_shape=(
            jax.ShapeDtypeStruct((2, FIELDS, PLANES) + TILE, jnp.float32),
            jax.ShapeDtypeStruct((4,), jnp.float32),
        ),
        in_specs=[VMEM] * 3,
        out_specs=(VMEM, pl.BlockSpec(memory_space=pltpu.SMEM)),
        compiler_params=PARAMS,
    )(parts, in_vmem(near), in_vmem(rest))
    new = new.reshape(2, FIELDS, PLANES, 4, 2, 128).transpose(0, 1, 2, 4, 3, 5)
    return new.reshape(2, FIELDS, PLANES, 2, 512), knots


def solution(mesh):
    fine = Mesh(mesh.devices.reshape(2, 8, 8, 4), ("img",) + STRIP)
    spec = P("img", None, None, STRIP, None)
    return jax.shard_map(
        per_device, mesh=fine, in_specs=(spec,), out_specs=(spec, P()), check_vma=False
    )
```

```python
import jax
import jax.numpy as jnp
from jax import lax
from jax.experimental import pallas as pl
from jax.experimental.pallas import tpu as pltpu
from jax.sharding import Mesh, PartitionSpec as P

KAPPA_PHASE = 1.0
KAPPA_SOLUTE = 0.6
BARRIER = 1.5
COUPLING = 2.0
TIME_STEP = 0.05
EQUILIBRIUM = ((0.8, 0.1), (0.1, 0.8), (0.1, 0.1), (0.45, 0.45))
STRIP = ("z", "y", "x")
FIELDS, PLANES = 6, 16
HALF = PLANES // 2
CELLS = 4 * FIELDS * HALF
TILE = (8, 128)
VMEM = pl.BlockSpec(memory_space=pltpu.VMEM)
PARAMS = pltpu.CompilerParams(vmem_limit_bytes=48 * 1024 * 1024)


def cell(k, f, z):
    return (k * FIELDS + f) * HALF + z


def even_sublanes():
    return lax.broadcasted_iota(jnp.int32, TILE, 0) % 2 == 0


def pack_kernel(images, own, far, own_copy, far_copy):
    core = lax.axis_index("img")
    even = even_sublanes()
    first = jnp.full(TILE, core, jnp.int32) == 0

    def field(i, carry):
        k, f = i // FIELDS, i % FIELDS
        for z in range(HALF):
            low, high = images[k, f, z], images[k, f, z + HALF]
            row0 = jnp.where(even, low, pltpu.roll(high, 1, 0))
            row1 = jnp.where(even, pltpu.roll(low, 7, 0), high)
            mine = jnp.where(first, row0, row1)
            rest = jnp.where(first, row1, row0)
            own[k, f, z] = mine
            far[k, f, z] = rest
            own_copy[k, f, z] = mine
            far_copy[k, f, z] = rest
        return carry

    lax.fori_loop(0, 2 * FIELDS, field, 0)


def step_image(center, beside, halo, j, stepped, g):
    even = even_sublanes()
    lane = lax.broadcasted_iota(jnp.int32, TILE, 1)
    at_first, at_last = lane == 0, lane == 127
    for z in range(HALF):
        cells, sums = [], []
        for f in range(FIELDS):
            c = center[j, f, z]
            if z < HALF - 1:
                raised = center[j, f, z + 1]
            else:
                raised = jnp.where(even, pltpu.roll(center[j, f, 0], 7, 0), c)
            if z > 0:
                lowered = center[j, f, z - 1]
            else:
                lowered = jnp.where(even, c, pltpu.roll(center[j, f, HALF - 1], 1, 0))
            ahead = pltpu.roll(c, 127, 1)
            ahead = jnp.where(at_last, pltpu.roll(ahead, 6, 0), ahead)
            behind = pltpu.roll(c, 1, 1)
            behind = jnp.where(at_first, pltpu.roll(behind, 2, 0), behind)
            around = (beside[j, f, z] + halo[j, f, z]) + (raised + lowered) + (ahead + behind)
            cells.append(c)
            sums.append(around)
        squares = [cells[i] * cells[i] for i in range(4)]
        total = (squares[0] + squares[1]) + (squares[2] + squares[3])
        pulls = []
        for s in range(2):
            value = cells[4 + s]
            for i in range(4):
                value = value - EQUILIBRIUM[i][s] * cells[i]
            pulls.append((TIME_STEP * COUPLING) * value)
        for i in range(4):
            gain = (1.0 - 6.0 * TIME_STEP * KAPPA_PHASE) - (TIME_STEP * 2.0 * BARRIER) * (
                total - squares[i]
            )
            out = gain * cells[i] + (TIME_STEP * KAPPA_PHASE) * sums[i]
            out = out + (EQUILIBRIUM[i][0] * pulls[0] + EQUILIBRIUM[i][1] * pulls[1])
            stepped[cell(g, i, z)] = out
        for s in range(2):
            out = (1.0 - 6.0 * TIME_STEP * KAPPA_SOLUTE) * cells[4 + s]
            out = out + (TIME_STEP * KAPPA_SOLUTE) * sums[4 + s] - pulls[s]
            stepped[cell(g, 4 + s, z)] = out


def step_kernel(own, far, sib_far, sib_own, halo_own, halo_sibling, stepped, part):
    core = lax.axis_index("img")

    def mine(j, carry):
        step_image(own, far, halo_own, j, stepped, 2 * core + j)
        return carry

    def theirs(j, carry):
        step_image(sib_own, sib_far, halo_sibling, j, stepped, 2 * (1 - core) + j)
        return carry

    lax.fori_loop(0, 2, mine, 0)
    lax.fori_loop(0, 2, theirs, 0)

    def gather(f, sums):
        new = []
        for k in range(3):
            terms = []
            for z in range(HALF):
                gap = stepped[cell(k + 1, f, z)] - stepped[cell(k, f, z)]
                terms.append(gap * gap)
            while len(terms) > 1:
                terms = [a + b for a, b in zip(terms[::2], terms[1::2])]
            new.append(sums[k] + terms[0])
        return tuple(new)

    zero = jnp.zeros(TILE, jnp.float32)
    sums = lax.fori_loop(0, FIELDS, gather, (zero, zero, zero))
    lane = lax.broadcasted_iota(jnp.int32, TILE, 1)
    out = zero
    for k in range(3):
        out = jnp.where(lane == k, jnp.sum(sums[k]), out)
    total = out[0:1]

    def row(p, carry):
        part[p] = total
        return carry

    lax.fori_loop(0, part.shape[0], row, 0, unroll=16)


def combine_kernel(parts, near, far, new, knots):
    core = lax.axis_index("img")
    even = even_sublanes()
    first = jnp.full(TILE, core, jnp.int32) == 0
    terms = [parts[p] for p in range(parts.shape[0])]
    while len(terms) > 1:
        terms = [a + b for a, b in zip(terms[::2], terms[1::2])]
    lane = lax.broadcasted_iota(jnp.int32, TILE, 1)
    l1, l2, l3 = (
        jnp.sqrt(1.0 + jnp.full(TILE, jnp.sum(jnp.where(lane == k, terms[0], 0.0))))
        for k in range(3)
    )
    whole = l1 + l2 + l3
    k1, k2, k3 = l1 / whole, (l1 + l2) / whole, whole / whole
    w0, w1, w2 = k1, k2 - k1, k3 - k2
    main1, main2 = 2.0 * (w0 + w1), 2.0 * (w1 + w2)
    det = main1 * main2 - w1 * w1
    scale = 6.0 / det
    i0, i1, i2 = 1.0 / w0, 1.0 / w1, 1.0 / w2
    bend1 = (
        -main2 * i0 * scale,
        (main2 + w1) * i1 * scale,
        -w1 * i2 * scale,
    )
    bend2 = (
        w1 * i0 * scale,
        -(main1 + w1) * i1 * scale,
        main1 * i2 * scale,
    )
    zero = jnp.zeros(TILE, jnp.float32)
    values, gaps = [], []
    for j in range(2):
        target = jnp.where(first, jnp.float32(j / 3.0), jnp.float32((j + 2) / 3.0))
        below = 1 + sum((k <= target).astype(jnp.int32) for k in (k1, k2, k3)) - 1
        at = jnp.clip(below, 0, 2)
        h = jnp.where(at == 0, w0, jnp.where(at == 1, w1, w2))
        right = jnp.where(at == 0, k1, jnp.where(at == 1, k2, k3))
        a = (right - target) / h
        b = 1.0 - a
        curve = h * h * (1.0 / 6.0)
        ca, cb = (a * a * a - a) * curve, (b * b * b - b) * curve
        v = [jnp.where(at == k, a, jnp.where(at == k - 1, b, zero)) for k in range(4)]
        c1 = jnp.where(at == 1, ca, jnp.where(at == 0, cb, zero))
        c2 = jnp.where(at == 2, ca, jnp.where(at == 1, cb, zero))
        values.append(v)
        gaps.append([c1 * bend1[m] + c2 * bend2[m] for m in range(3)])
    knots[0] = jnp.float32(0.0)
    knots[1] = k1[0, 0]
    knots[2] = k2[0, 0]
    knots[3] = k3[0, 0]

    def resampled(rows, f, z):
        s = [rows[cell(k, f, z)] for k in range(4)]
        d = [s[k + 1] - s[k] for k in range(3)]
        out = []
        for j in range(2):
            v, e = values[j], gaps[j]
            straight = (v[0] * s[0] + v[1] * s[1]) + (v[2] * s[2] + v[3] * s[3])
            out.append(straight + (e[0] * d[0] + e[1] * d[1] + e[2] * d[2]))
        return out

    def field(f, carry):
        for z in range(HALF):
            mine, rest = resampled(near, f, z), resampled(far, f, z)
            for j in range(2):
                row0 = jnp.where(first, mine[j], rest[j])
                row1 = jnp.where(first, rest[j], mine[j])
                new[j, f, z] = jnp.where(even, row0, pltpu.roll(row1, 1, 0))
                new[j, f, z + HALF] = jnp.where(even, pltpu.roll(row0, 7, 0), row1)
        return carry

    lax.fori_loop(0, FIELDS, field, 0)


def in_vmem(x):
    return pltpu.with_memory_space_constraint(x, pltpu.VMEM)


def vmem(*shape):
    return pltpu.VMEM(shape, jnp.float32)


def per_device(images):
    everyone = ("img",) + STRIP
    strips = lax.axis_size(STRIP)
    tiles = images.reshape(2, FIELDS, PLANES, 2, 4, 128).transpose(0, 1, 2, 4, 3, 5)
    tiles = tiles.reshape(2, FIELDS, PLANES, *TILE)
    packed = (2, FIELDS, HALF) + TILE
    own, far, own_copy, far_copy = pl.pallas_call(
        pack_kernel,
        out_shape=(vmem(*packed),) * 4,
        in_specs=[VMEM],
        out_specs=(VMEM,) * 4,
        compiler_params=PARAMS,
    )(tiles)
    right = [(i + 1) % strips for i in range(strips)]
    left = [(i - 1) % strips for i in range(strips)]
    same = [(i, right[i]) for i in range(strips)]
    same += [(strips + i, strips + left[i]) for i in range(strips)]
    cross = [(i, strips + left[i]) for i in range(strips)]
    cross += [(strips + i, right[i]) for i in range(strips)]
    halo_own = lax.ppermute(far_copy, everyone, same)
    halo_sibling = lax.ppermute(own_copy, everyone, cross)
    swap = [(0, 1), (1, 0)]
    sib_far = lax.ppermute(own, "img", swap)
    sib_own = lax.ppermute(far, "img", swap)
    inputs = (own, far, sib_far, sib_own, halo_own, halo_sibling)
    near, part = pl.pallas_call(
        step_kernel,
        out_shape=(vmem(CELLS, *TILE), vmem(2 * strips, 1, TILE[1])),
        in_specs=[VMEM] * 6,
        out_specs=(VMEM, VMEM),
        compiler_params=PARAMS,
    )(*map(in_vmem, inputs))
    rest = lax.ppermute(near, "img", swap)
    parts = lax.all_to_all(part, everyone, 0, 0, tiled=True)
    parts = parts.reshape(-1, *TILE)
    new, knots = pl.pallas_call(
        combine_kernel,
        out_shape=(
            jax.ShapeDtypeStruct((2, FIELDS, PLANES) + TILE, jnp.float32),
            jax.ShapeDtypeStruct((4,), jnp.float32),
        ),
        in_specs=[VMEM] * 3,
        out_specs=(VMEM, pl.BlockSpec(memory_space=pltpu.SMEM)),
        compiler_params=PARAMS,
    )(in_vmem(parts), in_vmem(near), in_vmem(rest))
    new = new.reshape(2, FIELDS, PLANES, 4, 2, 128).transpose(0, 1, 2, 4, 3, 5)
    return new.reshape(2, FIELDS, PLANES, 2, 512), knots


def solution(mesh):
    fine = Mesh(mesh.devices.reshape(2, 8, 8, 4), ("img",) + STRIP)
    spec = P("img", None, None, STRIP, None)
    return jax.shard_map(
        per_device, mesh=fine, in_specs=(spec,), out_specs=(spec, P()), check_vma=False
    )
```

```python
import jax
import jax.numpy as jnp
from jax import lax
from jax.experimental import pallas as pl
from jax.experimental.pallas import tpu as pltpu
from jax.sharding import Mesh, PartitionSpec as P

KAPPA_PHASE = 1.0
KAPPA_SOLUTE = 0.6
BARRIER = 1.5
COUPLING = 2.0
TIME_STEP = 0.05
EQUILIBRIUM = ((0.8, 0.1), (0.1, 0.8), (0.1, 0.1), (0.45, 0.45))
STRIP = ("z", "y", "x")
FIELDS, PLANES = 6, 16
HALF = PLANES // 2
CELLS = 4 * FIELDS * HALF
TILE = (8, 128)
VMEM = pl.BlockSpec(memory_space=pltpu.VMEM)
PARAMS = pltpu.CompilerParams(vmem_limit_bytes=48 * 1024 * 1024)


def cell(k, f, z):
    return (k * FIELDS + f) * HALF + z


def even_sublanes():
    return lax.broadcasted_iota(jnp.int32, TILE, 0) % 2 == 0


def pack_kernel(images, own, far, own_copy, far_copy):
    core = lax.axis_index("img")
    even = even_sublanes()
    first = jnp.full(TILE, core, jnp.int32) == 0

    def field(i, carry):
        k, f = i // FIELDS, i % FIELDS
        for z in range(HALF):
            low, high = images[k, f, z], images[k, f, z + HALF]
            row0 = jnp.where(even, low, pltpu.roll(high, 1, 0))
            row1 = jnp.where(even, pltpu.roll(low, 7, 0), high)
            mine = jnp.where(first, row0, row1)
            rest = jnp.where(first, row1, row0)
            own[k, f, z] = mine
            far[k, f, z] = rest
            own_copy[k, f, z] = mine
            far_copy[k, f, z] = rest
        return carry

    lax.fori_loop(0, 2 * FIELDS, field, 0)


def step_image(center, beside, halo, j, stepped, g):
    even = even_sublanes()
    lane = lax.broadcasted_iota(jnp.int32, TILE, 1)
    at_first, at_last = lane == 0, lane == 127
    for z in range(HALF):
        cells, sums = [], []
        for f in range(FIELDS):
            c = center[j, f, z]
            if z < HALF - 1:
                raised = center[j, f, z + 1]
            else:
                raised = jnp.where(even, pltpu.roll(center[j, f, 0], 7, 0), c)
            if z > 0:
                lowered = center[j, f, z - 1]
            else:
                lowered = jnp.where(even, c, pltpu.roll(center[j, f, HALF - 1], 1, 0))
            ahead = pltpu.roll(c, 127, 1)
            ahead = jnp.where(at_last, pltpu.roll(ahead, 6, 0), ahead)
            behind = pltpu.roll(c, 1, 1)
            behind = jnp.where(at_first, pltpu.roll(behind, 2, 0), behind)
            around = (beside[j, f, z] + halo[j, f, z]) + (raised + lowered) + (ahead + behind)
            cells.append(c)
            sums.append(around)
        squares = [cells[i] * cells[i] for i in range(4)]
        total = (squares[0] + squares[1]) + (squares[2] + squares[3])
        pulls = []
        for s in range(2):
            value = cells[4 + s]
            for i in range(4):
                value = value - EQUILIBRIUM[i][s] * cells[i]
            pulls.append((TIME_STEP * COUPLING) * value)
        for i in range(4):
            gain = (1.0 - 6.0 * TIME_STEP * KAPPA_PHASE) - (TIME_STEP * 2.0 * BARRIER) * (
                total - squares[i]
            )
            out = gain * cells[i] + (TIME_STEP * KAPPA_PHASE) * sums[i]
            out = out + (EQUILIBRIUM[i][0] * pulls[0] + EQUILIBRIUM[i][1] * pulls[1])
            stepped[cell(g, i, z)] = out
        for s in range(2):
            out = (1.0 - 6.0 * TIME_STEP * KAPPA_SOLUTE) * cells[4 + s]
            out = out + (TIME_STEP * KAPPA_SOLUTE) * sums[4 + s] - pulls[s]
            stepped[cell(g, 4 + s, z)] = out


def step_kernel(own, far, sib_far, sib_own, halo_own, halo_sibling, stepped, part):
    core = lax.axis_index("img")

    def mine(j, carry):
        step_image(own, far, halo_own, j, stepped, 2 * core + j)
        return carry

    def theirs(j, carry):
        step_image(sib_own, sib_far, halo_sibling, j, stepped, 2 * (1 - core) + j)
        return carry

    lax.fori_loop(0, 2, mine, 0)
    lax.fori_loop(0, 2, theirs, 0)

    def gather(f, sums):
        new = []
        for k in range(3):
            terms = []
            for z in range(HALF):
                gap = stepped[cell(k + 1, f, z)] - stepped[cell(k, f, z)]
                terms.append(gap * gap)
            while len(terms) > 1:
                terms = [a + b for a, b in zip(terms[::2], terms[1::2])]
            new.append(sums[k] + terms[0])
        return tuple(new)

    zero = jnp.zeros(TILE, jnp.float32)
    sums = lax.fori_loop(0, FIELDS, gather, (zero, zero, zero))
    lane = lax.broadcasted_iota(jnp.int32, TILE, 1)
    out = zero
    for k in range(3):
        out = jnp.where(lane == k, jnp.sum(sums[k]), out)
    total = out[0:1]

    def row(p, carry):
        part[p] = total
        return carry

    lax.fori_loop(0, part.shape[0], row, 0, unroll=16)


def combine_kernel(parts, near, far, new, knots):
    core = lax.axis_index("img")
    even = even_sublanes()
    first = jnp.full(TILE, core, jnp.int32) == 0
    terms = [parts[p] for p in range(parts.shape[0])]
    while len(terms) > 1:
        terms = [a + b for a, b in zip(terms[::2], terms[1::2])]
    lane = lax.broadcasted_iota(jnp.int32, TILE, 1)
    l1, l2, l3 = (
        jnp.sqrt(1.0 + jnp.full(TILE, jnp.sum(jnp.where(lane == k, terms[0], 0.0))))
        for k in range(3)
    )
    whole = l1 + l2 + l3
    k1, k2, k3 = l1 / whole, (l1 + l2) / whole, whole / whole
    w0, w1, w2 = k1, k2 - k1, k3 - k2
    main1, main2 = 2.0 * (w0 + w1), 2.0 * (w1 + w2)
    det = main1 * main2 - w1 * w1
    scale = 6.0 / det
    i0, i1, i2 = 1.0 / w0, 1.0 / w1, 1.0 / w2
    bend1 = (
        -main2 * i0 * scale,
        (main2 + w1) * i1 * scale,
        -w1 * i2 * scale,
    )
    bend2 = (
        w1 * i0 * scale,
        -(main1 + w1) * i1 * scale,
        main1 * i2 * scale,
    )
    zero = jnp.zeros(TILE, jnp.float32)
    values, gaps = [], []
    for j in range(2):
        target = jnp.where(first, jnp.float32(j / 3.0), jnp.float32((j + 2) / 3.0))
        below = 1 + sum((k <= target).astype(jnp.int32) for k in (k1, k2, k3)) - 1
        at = jnp.clip(below, 0, 2)
        h = jnp.where(at == 0, w0, jnp.where(at == 1, w1, w2))
        right = jnp.where(at == 0, k1, jnp.where(at == 1, k2, k3))
        a = (right - target) / h
        b = 1.0 - a
        curve = h * h * (1.0 / 6.0)
        ca, cb = (a * a * a - a) * curve, (b * b * b - b) * curve
        v = [jnp.where(at == k, a, jnp.where(at == k - 1, b, zero)) for k in range(4)]
        c1 = jnp.where(at == 1, ca, jnp.where(at == 0, cb, zero))
        c2 = jnp.where(at == 2, ca, jnp.where(at == 1, cb, zero))
        values.append(v)
        gaps.append([c1 * bend1[m] + c2 * bend2[m] for m in range(3)])
    knots[0] = jnp.float32(0.0)
    knots[1] = k1[0, 0]
    knots[2] = k2[0, 0]
    knots[3] = k3[0, 0]

    def resampled(rows, f, z):
        s = [rows[cell(k, f, z)] for k in range(4)]
        d = [s[k + 1] - s[k] for k in range(3)]
        out = []
        for j in range(2):
            v, e = values[j], gaps[j]
            straight = (v[0] * s[0] + v[1] * s[1]) + (v[2] * s[2] + v[3] * s[3])
            out.append(straight + (e[0] * d[0] + e[1] * d[1] + e[2] * d[2]))
        return out

    def field(f, carry):
        for z in range(HALF):
            mine, rest = resampled(near, f, z), resampled(far, f, z)
            for j in range(2):
                row0 = jnp.where(first, mine[j], rest[j])
                row1 = jnp.where(first, rest[j], mine[j])
                new[j, f, z] = jnp.where(even, row0, pltpu.roll(row1, 1, 0))
                new[j, f, z + HALF] = jnp.where(even, pltpu.roll(row0, 7, 0), row1)
        return carry

    lax.fori_loop(0, FIELDS, field, 0)


def in_vmem(x):
    return pltpu.with_memory_space_constraint(x, pltpu.VMEM)


def vmem(*shape):
    return pltpu.VMEM(shape, jnp.float32)


def per_device(images):
    everyone = ("img",) + STRIP
    strips = lax.axis_size(STRIP)
    tiles = images.reshape(2, FIELDS, PLANES, 2, 4, 128).transpose(0, 1, 2, 4, 3, 5)
    tiles = tiles.reshape(2, FIELDS, PLANES, *TILE)
    packed = (2, FIELDS, HALF) + TILE
    own, far, own_copy, far_copy = pl.pallas_call(
        pack_kernel,
        out_shape=(vmem(*packed),) * 4,
        in_specs=[VMEM],
        out_specs=(VMEM,) * 4,
        compiler_params=PARAMS,
    )(tiles)
    right = [(i + 1) % strips for i in range(strips)]
    left = [(i - 1) % strips for i in range(strips)]
    same = [(i, right[i]) for i in range(strips)]
    same += [(strips + i, strips + left[i]) for i in range(strips)]
    cross = [(i, strips + left[i]) for i in range(strips)]
    cross += [(strips + i, right[i]) for i in range(strips)]
    halo_own = lax.ppermute(far_copy, everyone, same)
    halo_sibling = lax.ppermute(own_copy, everyone, cross)
    swap = [(0, 1), (1, 0)]
    sib_far = lax.ppermute(own, "img", swap)
    sib_own = lax.ppermute(far, "img", swap)
    inputs = (own, far, sib_far, sib_own, halo_own, halo_sibling)
    near, part = pl.pallas_call(
        step_kernel,
        out_shape=(vmem(CELLS, *TILE), pltpu.HBM((2 * strips, 1, TILE[1]), jnp.float32)),
        in_specs=[VMEM] * 6,
        out_specs=(VMEM, VMEM),
        compiler_params=PARAMS,
    )(*map(in_vmem, inputs))
    rest = lax.ppermute(near, "img", swap)
    parts = lax.all_to_all(part, everyone, 0, 0, tiled=True)
    parts = parts.reshape(-1, *TILE)
    new, knots = pl.pallas_call(
        combine_kernel,
        out_shape=(
            jax.ShapeDtypeStruct((2, FIELDS, PLANES) + TILE, jnp.float32),
            jax.ShapeDtypeStruct((4,), jnp.float32),
        ),
        in_specs=[VMEM] * 3,
        out_specs=(VMEM, pl.BlockSpec(memory_space=pltpu.SMEM)),
        compiler_params=PARAMS,
    )(in_vmem(parts), in_vmem(near), in_vmem(rest))
    new = new.reshape(2, FIELDS, PLANES, 4, 2, 128).transpose(0, 1, 2, 4, 3, 5)
    return new.reshape(2, FIELDS, PLANES, 2, 512), knots


def solution(mesh):
    fine = Mesh(mesh.devices.reshape(2, 8, 8, 4), ("img",) + STRIP)
    spec = P("img", None, None, STRIP, None)
    return jax.shard_map(
        per_device, mesh=fine, in_specs=(spec,), out_specs=(spec, P()), check_vma=False
    )
```

```python
import jax
import jax.numpy as jnp
from jax import lax
from jax.experimental import pallas as pl
from jax.experimental.pallas import tpu as pltpu
from jax.sharding import Mesh, PartitionSpec as P

KAPPA_PHASE = 1.0
KAPPA_SOLUTE = 0.6
BARRIER = 1.5
COUPLING = 2.0
TIME_STEP = 0.05
EQUILIBRIUM = ((0.8, 0.1), (0.1, 0.8), (0.1, 0.1), (0.45, 0.45))
STRIP = ("z", "y", "x")
FIELDS, PLANES = 6, 16
HALF = PLANES // 2
CELLS = 4 * FIELDS * HALF
TILE = (8, 128)
VMEM = pl.BlockSpec(memory_space=pltpu.VMEM)
PARAMS = pltpu.CompilerParams(vmem_limit_bytes=48 * 1024 * 1024)


def cell(k, f, z):
    return (k * FIELDS + f) * HALF + z


def even_sublanes():
    return lax.broadcasted_iota(jnp.int32, TILE, 0) % 2 == 0


def pack_kernel(images, own, far, own_copy, far_copy):
    core = lax.axis_index("img")
    even = even_sublanes()
    first = jnp.full(TILE, core, jnp.int32) == 0

    def field(i, carry):
        k, f = i // FIELDS, i % FIELDS
        for z in range(HALF):
            low, high = images[k, f, z], images[k, f, z + HALF]
            row0 = jnp.where(even, low, pltpu.roll(high, 1, 0))
            row1 = jnp.where(even, pltpu.roll(low, 7, 0), high)
            mine = jnp.where(first, row0, row1)
            rest = jnp.where(first, row1, row0)
            own[k, f, z] = mine
            far[k, f, z] = rest
            own_copy[k, f, z] = mine
            far_copy[k, f, z] = rest
        return carry

    lax.fori_loop(0, 2 * FIELDS, field, 0)


def step_image(center, beside, halo, j, stepped, g):
    even = even_sublanes()
    lane = lax.broadcasted_iota(jnp.int32, TILE, 1)
    at_first, at_last = lane == 0, lane == 127
    for z in range(HALF):
        cells, sums = [], []
        for f in range(FIELDS):
            c = center[j, f, z]
            if z < HALF - 1:
                raised = center[j, f, z + 1]
            else:
                raised = jnp.where(even, pltpu.roll(center[j, f, 0], 7, 0), c)
            if z > 0:
                lowered = center[j, f, z - 1]
            else:
                lowered = jnp.where(even, c, pltpu.roll(center[j, f, HALF - 1], 1, 0))
            ahead = pltpu.roll(c, 127, 1)
            ahead = jnp.where(at_last, pltpu.roll(ahead, 6, 0), ahead)
            behind = pltpu.roll(c, 1, 1)
            behind = jnp.where(at_first, pltpu.roll(behind, 2, 0), behind)
            around = (beside[j, f, z] + halo[j, f, z]) + (raised + lowered) + (ahead + behind)
            cells.append(c)
            sums.append(around)
        squares = [cells[i] * cells[i] for i in range(4)]
        total = (squares[0] + squares[1]) + (squares[2] + squares[3])
        pulls = []
        for s in range(2):
            value = cells[4 + s]
            for i in range(4):
                value = value - EQUILIBRIUM[i][s] * cells[i]
            pulls.append((TIME_STEP * COUPLING) * value)
        for i in range(4):
            gain = (1.0 - 6.0 * TIME_STEP * KAPPA_PHASE) - (TIME_STEP * 2.0 * BARRIER) * (
                total - squares[i]
            )
            out = gain * cells[i] + (TIME_STEP * KAPPA_PHASE) * sums[i]
            out = out + (EQUILIBRIUM[i][0] * pulls[0] + EQUILIBRIUM[i][1] * pulls[1])
            stepped[cell(g, i, z)] = out
        for s in range(2):
            out = (1.0 - 6.0 * TIME_STEP * KAPPA_SOLUTE) * cells[4 + s]
            out = out + (TIME_STEP * KAPPA_SOLUTE) * sums[4 + s] - pulls[s]
            stepped[cell(g, 4 + s, z)] = out


def step_row(mine, theirs, stepped):
    core = lax.axis_index("img")

    def one(j, carry):
        step_image(*mine, j, stepped, 2 * core + j)
        return carry

    def other(j, carry):
        step_image(*theirs, j, stepped, 2 * (1 - core) + j)
        return carry

    lax.fori_loop(0, 2, one, 0)
    lax.fori_loop(0, 2, other, 0)


def gap_sums(stepped):
    def gather(f, sums):
        new = []
        for k in range(3):
            terms = []
            for z in range(HALF):
                gap = stepped[cell(k + 1, f, z)] - stepped[cell(k, f, z)]
                terms.append(gap * gap)
            while len(terms) > 1:
                terms = [a + b for a, b in zip(terms[::2], terms[1::2])]
            new.append(sums[k] + terms[0])
        return tuple(new)

    zero = jnp.zeros(TILE, jnp.float32)
    return lax.fori_loop(0, FIELDS, gather, (zero, zero, zero))


def near_kernel(own, far, sib_own, sib_far, halo_own, halo_sib, stepped, sums):
    step_row((own, far, halo_own), (sib_own, sib_far, halo_sib), stepped)
    for k, tile in enumerate(gap_sums(stepped)):
        sums[k] = tile


def far_kernel(own, far, sib_own, sib_far, halo_own, halo_sib, sums, stepped, rows):
    step_row((far, own, halo_own), (sib_far, sib_own, halo_sib), stepped)
    lane = lax.broadcasted_iota(jnp.int32, (1, TILE[1]), 1)
    out = jnp.zeros((1, TILE[1]), jnp.float32)
    for k, tile in enumerate(gap_sums(stepped)):
        out = jnp.where(lane == k, jnp.sum(tile + sums[k]), out)

    def row(p, carry):
        rows[p] = out
        return carry

    lax.fori_loop(0, rows.shape[0], row, 0, unroll=16)


def combine_kernel(parts, near, far, new, knots):
    core = lax.axis_index("img")
    even = even_sublanes()
    first = jnp.full(TILE, core, jnp.int32) == 0
    terms = [parts[p] for p in range(parts.shape[0])]
    while len(terms) > 1:
        terms = [a + b for a, b in zip(terms[::2], terms[1::2])]
    lane = lax.broadcasted_iota(jnp.int32, TILE, 1)
    l1, l2, l3 = (
        jnp.sqrt(1.0 + jnp.full(TILE, jnp.sum(jnp.where(lane == k, terms[0], 0.0))))
        for k in range(3)
    )
    whole = l1 + l2 + l3
    k1, k2, k3 = l1 / whole, (l1 + l2) / whole, whole / whole
    w0, w1, w2 = k1, k2 - k1, k3 - k2
    main1, main2 = 2.0 * (w0 + w1), 2.0 * (w1 + w2)
    det = main1 * main2 - w1 * w1
    scale = 6.0 / det
    i0, i1, i2 = 1.0 / w0, 1.0 / w1, 1.0 / w2
    bend1 = (
        -main2 * i0 * scale,
        (main2 + w1) * i1 * scale,
        -w1 * i2 * scale,
    )
    bend2 = (
        w1 * i0 * scale,
        -(main1 + w1) * i1 * scale,
        main1 * i2 * scale,
    )
    zero = jnp.zeros(TILE, jnp.float32)
    values, gaps = [], []
    for j in range(2):
        target = jnp.where(first, jnp.float32(j / 3.0), jnp.float32((j + 2) / 3.0))
        below = 1 + sum((k <= target).astype(jnp.int32) for k in (k1, k2, k3)) - 1
        at = jnp.clip(below, 0, 2)
        h = jnp.where(at == 0, w0, jnp.where(at == 1, w1, w2))
        right = jnp.where(at == 0, k1, jnp.where(at == 1, k2, k3))
        a = (right - target) / h
        b = 1.0 - a
        curve = h * h * (1.0 / 6.0)
        ca, cb = (a * a * a - a) * curve, (b * b * b - b) * curve
        v = [jnp.where(at == k, a, jnp.where(at == k - 1, b, zero)) for k in range(4)]
        c1 = jnp.where(at == 1, ca, jnp.where(at == 0, cb, zero))
        c2 = jnp.where(at == 2, ca, jnp.where(at == 1, cb, zero))
        values.append(v)
        gaps.append([c1 * bend1[m] + c2 * bend2[m] for m in range(3)])
    knots[0] = jnp.float32(0.0)
    knots[1] = k1[0, 0]
    knots[2] = k2[0, 0]
    knots[3] = k3[0, 0]

    def resampled(rows, f, z):
        s = [rows[cell(k, f, z)] for k in range(4)]
        d = [s[k + 1] - s[k] for k in range(3)]
        out = []
        for j in range(2):
            v, e = values[j], gaps[j]
            straight = (v[0] * s[0] + v[1] * s[1]) + (v[2] * s[2] + v[3] * s[3])
            out.append(straight + (e[0] * d[0] + e[1] * d[1] + e[2] * d[2]))
        return out

    def field(f, carry):
        for z in range(HALF):
            mine, rest = resampled(near, f, z), resampled(far, f, z)
            for j in range(2):
                row0 = jnp.where(first, mine[j], rest[j])
                row1 = jnp.where(first, rest[j], mine[j])
                new[j, f, z] = jnp.where(even, row0, pltpu.roll(row1, 1, 0))
                new[j, f, z + HALF] = jnp.where(even, pltpu.roll(row0, 7, 0), row1)
        return carry

    lax.fori_loop(0, FIELDS, field, 0)


def in_vmem(x):
    return pltpu.with_memory_space_constraint(x, pltpu.VMEM)


def vmem(*shape):
    return pltpu.VMEM(shape, jnp.float32)


def per_device(images):
    everyone = ("img",) + STRIP
    strips = lax.axis_size(STRIP)
    tiles = images.reshape(2, FIELDS, PLANES, 2, 4, 128).transpose(0, 1, 2, 4, 3, 5)
    tiles = tiles.reshape(2, FIELDS, PLANES, *TILE)
    packed = (2, FIELDS, HALF) + TILE
    own, far, own_copy, far_copy = pl.pallas_call(
        pack_kernel,
        out_shape=(vmem(*packed),) * 4,
        in_specs=[VMEM],
        out_specs=(VMEM,) * 4,
        compiler_params=PARAMS,
    )(tiles)
    right = [(i + 1) % strips for i in range(strips)]
    left = [(i - 1) % strips for i in range(strips)]
    same = [(i, right[i]) for i in range(strips)]
    same += [(strips + i, strips + left[i]) for i in range(strips)]
    cross = [(i, strips + left[i]) for i in range(strips)]
    cross += [(strips + i, right[i]) for i in range(strips)]
    halo_own = lax.ppermute(far_copy, everyone, same)
    halo_sibling = lax.ppermute(own_copy, everyone, cross)
    swap = [(0, 1), (1, 0)]
    sib_far = lax.ppermute(own, "img", swap)
    sib_own = lax.ppermute(far, "img", swap)
    passed_own = lax.ppermute(halo_sibling, "img", swap)
    passed_sibling = lax.ppermute(halo_own, "img", swap)
    cost = pl.CostEstimate(flops=3_000_000, bytes_accessed=3_000_000, transcendentals=0)
    rows = (own, far, sib_own, sib_far)
    near, sums = pl.pallas_call(
        near_kernel,
        out_shape=(vmem(CELLS, *TILE), vmem(3, *TILE)),
        in_specs=[VMEM] * 6,
        out_specs=(VMEM, VMEM),
        compiler_params=PARAMS,
        cost_estimate=cost,
    )(*map(in_vmem, rows + (halo_own, halo_sibling)))
    rest, parts = pl.pallas_call(
        far_kernel,
        out_shape=(vmem(CELLS, *TILE), vmem(strips, 1, TILE[1])),
        in_specs=[VMEM] * 7,
        out_specs=(VMEM, VMEM),
        compiler_params=PARAMS,
        cost_estimate=cost,
    )(*map(in_vmem, rows + (passed_own, passed_sibling, sums)))
    parts = lax.all_to_all(parts, STRIP, 0, 0, tiled=True)
    parts = parts.reshape(strips // TILE[0], *TILE)
    new, knots = pl.pallas_call(
        combine_kernel,
        out_shape=(
            jax.ShapeDtypeStruct((2, FIELDS, PLANES) + TILE, jnp.float32),
            jax.ShapeDtypeStruct((4,), jnp.float32),
        ),
        in_specs=[VMEM] * 3,
        out_specs=(VMEM, pl.BlockSpec(memory_space=pltpu.SMEM)),
        compiler_params=PARAMS,
    )(in_vmem(parts), in_vmem(near), in_vmem(rest))
    new = new.reshape(2, FIELDS, PLANES, 4, 2, 128).transpose(0, 1, 2, 4, 3, 5)
    return new.reshape(2, FIELDS, PLANES, 2, 512), knots


def solution(mesh):
    fine = Mesh(mesh.devices.reshape(2, 8, 8, 4), ("img",) + STRIP)
    spec = P("img", None, None, STRIP, None)
    return jax.shard_map(
        per_device, mesh=fine, in_specs=(spec,), out_specs=(spec, P()), check_vma=False
    )
```

```python
import jax
import jax.numpy as jnp
from jax import lax
from jax.experimental import pallas as pl
from jax.experimental.pallas import tpu as pltpu
from jax.sharding import Mesh, PartitionSpec as P

KAPPA_PHASE = 1.0
KAPPA_SOLUTE = 0.6
BARRIER = 1.5
COUPLING = 2.0
TIME_STEP = 0.05
EQUILIBRIUM = ((0.8, 0.1), (0.1, 0.8), (0.1, 0.1), (0.45, 0.45))
STRIP = ("z", "y", "x")
FIELDS, PLANES = 6, 16
HALF = PLANES // 2
CELLS = 4 * FIELDS * HALF
TILE = (8, 128)
VMEM = pl.BlockSpec(memory_space=pltpu.VMEM)
PARAMS = pltpu.CompilerParams(vmem_limit_bytes=48 * 1024 * 1024)


def cell(k, f, z):
    return (k * FIELDS + f) * HALF + z


def even_sublanes():
    return lax.broadcasted_iota(jnp.int32, TILE, 0) % 2 == 0


def pack_kernel(images, own, far, far_copy, own_copy):
    core = lax.axis_index("img")
    even = even_sublanes()
    first = jnp.full(TILE, core, jnp.int32) == 0

    def field(i, carry):
        k, f = i // FIELDS, i % FIELDS
        for z in range(HALF):
            low, high = images[k, f, z], images[k, f, z + HALF]
            row0 = jnp.where(even, low, pltpu.roll(high, 1, 0))
            row1 = jnp.where(even, pltpu.roll(low, 7, 0), high)
            mine = jnp.where(first, row0, row1)
            rest = jnp.where(first, row1, row0)
            own[k, f, z] = mine
            far[k, f, z] = rest
            own_copy[k, f, z] = mine
            far_copy[k, f, z] = rest
        return carry

    lax.fori_loop(0, 2 * FIELDS, field, 0)


def step_image(center, beside, halo, j, stepped, g):
    even = even_sublanes()
    lane = lax.broadcasted_iota(jnp.int32, TILE, 1)
    at_first, at_last = lane == 0, lane == 127
    for z in range(HALF):
        cells, sums = [], []
        for f in range(FIELDS):
            c = center[j, f, z]
            if z < HALF - 1:
                raised = center[j, f, z + 1]
            else:
                raised = jnp.where(even, pltpu.roll(center[j, f, 0], 7, 0), c)
            if z > 0:
                lowered = center[j, f, z - 1]
            else:
                lowered = jnp.where(even, c, pltpu.roll(center[j, f, HALF - 1], 1, 0))
            ahead = pltpu.roll(c, 127, 1)
            ahead = jnp.where(at_last, pltpu.roll(ahead, 6, 0), ahead)
            behind = pltpu.roll(c, 1, 1)
            behind = jnp.where(at_first, pltpu.roll(behind, 2, 0), behind)
            around = (beside[j, f, z] + halo[j, f, z]) + (raised + lowered) + (ahead + behind)
            cells.append(c)
            sums.append(around)
        squares = [cells[i] * cells[i] for i in range(4)]
        total = (squares[0] + squares[1]) + (squares[2] + squares[3])
        pulls = []
        for s in range(2):
            value = cells[4 + s]
            for i in range(4):
                value = value - EQUILIBRIUM[i][s] * cells[i]
            pulls.append((TIME_STEP * COUPLING) * value)
        for i in range(4):
            gain = (1.0 - 6.0 * TIME_STEP * KAPPA_PHASE) - (TIME_STEP * 2.0 * BARRIER) * (
                total - squares[i]
            )
            out = gain * cells[i] + (TIME_STEP * KAPPA_PHASE) * sums[i]
            out = out + (EQUILIBRIUM[i][0] * pulls[0] + EQUILIBRIUM[i][1] * pulls[1])
            stepped[cell(g, i, z)] = out
        for s in range(2):
            out = (1.0 - 6.0 * TIME_STEP * KAPPA_SOLUTE) * cells[4 + s]
            out = out + (TIME_STEP * KAPPA_SOLUTE) * sums[4 + s] - pulls[s]
            stepped[cell(g, 4 + s, z)] = out


def step_row(mine, theirs, stepped):
    core = lax.axis_index("img")

    def one(j, carry):
        step_image(*mine, j, stepped, 2 * core + j)
        return carry

    def other(j, carry):
        step_image(*theirs, j, stepped, 2 * (1 - core) + j)
        return carry

    lax.fori_loop(0, 2, one, 0)
    lax.fori_loop(0, 2, other, 0)


def gap_sums(stepped):
    def gather(f, sums):
        new = []
        for k in range(3):
            terms = []
            for z in range(HALF):
                gap = stepped[cell(k + 1, f, z)] - stepped[cell(k, f, z)]
                terms.append(gap * gap)
            while len(terms) > 1:
                terms = [a + b for a, b in zip(terms[::2], terms[1::2])]
            new.append(sums[k] + terms[0])
        return tuple(new)

    zero = jnp.zeros(TILE, jnp.float32)
    return lax.fori_loop(0, FIELDS, gather, (zero, zero, zero))


def near_kernel(own, far, sib_own, sib_far, halo_own, halo_sib, stepped, sums):
    step_row((own, far, halo_own), (sib_own, sib_far, halo_sib), stepped)
    for k, tile in enumerate(gap_sums(stepped)):
        sums[k] = tile


def far_kernel(own, far, sib_own, sib_far, halo_sib, halo_own, sums, stepped, rows):
    step_row((far, own, halo_own), (sib_far, sib_own, halo_sib), stepped)
    lane = lax.broadcasted_iota(jnp.int32, (1, TILE[1]), 1)
    out = jnp.zeros((1, TILE[1]), jnp.float32)
    for k, tile in enumerate(gap_sums(stepped)):
        out = jnp.where(lane == k, jnp.sum(tile + sums[k]), out)

    def row(p, carry):
        rows[p] = out
        return carry

    lax.fori_loop(0, rows.shape[0], row, 0, unroll=16)


def combine_kernel(parts, near, far, new, knots):
    core = lax.axis_index("img")
    even = even_sublanes()
    first = jnp.full(TILE, core, jnp.int32) == 0
    terms = [parts[p] for p in range(parts.shape[0])]
    while len(terms) > 1:
        terms = [a + b for a, b in zip(terms[::2], terms[1::2])]
    lane = lax.broadcasted_iota(jnp.int32, TILE, 1)
    l1, l2, l3 = (
        jnp.sqrt(1.0 + jnp.full(TILE, jnp.sum(jnp.where(lane == k, terms[0], 0.0))))
        for k in range(3)
    )
    whole = l1 + l2 + l3
    k1, k2, k3 = l1 / whole, (l1 + l2) / whole, whole / whole
    w0, w1, w2 = k1, k2 - k1, k3 - k2
    main1, main2 = 2.0 * (w0 + w1), 2.0 * (w1 + w2)
    det = main1 * main2 - w1 * w1
    scale = 6.0 / det
    i0, i1, i2 = 1.0 / w0, 1.0 / w1, 1.0 / w2
    bend1 = (
        -main2 * i0 * scale,
        (main2 + w1) * i1 * scale,
        -w1 * i2 * scale,
    )
    bend2 = (
        w1 * i0 * scale,
        -(main1 + w1) * i1 * scale,
        main1 * i2 * scale,
    )
    zero = jnp.zeros(TILE, jnp.float32)
    values, gaps = [], []
    for j in range(2):
        target = jnp.where(first, jnp.float32(j / 3.0), jnp.float32((j + 2) / 3.0))
        below = 1 + sum((k <= target).astype(jnp.int32) for k in (k1, k2, k3)) - 1
        at = jnp.clip(below, 0, 2)
        h = jnp.where(at == 0, w0, jnp.where(at == 1, w1, w2))
        right = jnp.where(at == 0, k1, jnp.where(at == 1, k2, k3))
        a = (right - target) / h
        b = 1.0 - a
        curve = h * h * (1.0 / 6.0)
        ca, cb = (a * a * a - a) * curve, (b * b * b - b) * curve
        v = [jnp.where(at == k, a, jnp.where(at == k - 1, b, zero)) for k in range(4)]
        c1 = jnp.where(at == 1, ca, jnp.where(at == 0, cb, zero))
        c2 = jnp.where(at == 2, ca, jnp.where(at == 1, cb, zero))
        values.append(v)
        gaps.append([c1 * bend1[m] + c2 * bend2[m] for m in range(3)])
    knots[0] = jnp.float32(0.0)
    knots[1] = k1[0, 0]
    knots[2] = k2[0, 0]
    knots[3] = k3[0, 0]

    def resampled(rows, f, z):
        s = [rows[cell(k, f, z)] for k in range(4)]
        d = [s[k + 1] - s[k] for k in range(3)]
        out = []
        for j in range(2):
            v, e = values[j], gaps[j]
            straight = (v[0] * s[0] + v[1] * s[1]) + (v[2] * s[2] + v[3] * s[3])
            out.append(straight + (e[0] * d[0] + e[1] * d[1] + e[2] * d[2]))
        return out

    def field(f, carry):
        for z in range(HALF):
            mine, rest = resampled(near, f, z), resampled(far, f, z)
            for j in range(2):
                row0 = jnp.where(first, mine[j], rest[j])
                row1 = jnp.where(first, rest[j], mine[j])
                new[j, f, z] = jnp.where(even, row0, pltpu.roll(row1, 1, 0))
                new[j, f, z + HALF] = jnp.where(even, pltpu.roll(row0, 7, 0), row1)
        return carry

    lax.fori_loop(0, FIELDS, field, 0)


def in_vmem(x):
    return pltpu.with_memory_space_constraint(x, pltpu.VMEM)


def vmem(*shape):
    return pltpu.VMEM(shape, jnp.float32)


def per_device(images):
    everyone = ("img",) + STRIP
    strips = lax.axis_size(STRIP)
    tiles = images.reshape(2, FIELDS, PLANES, 2, 4, 128).transpose(0, 1, 2, 4, 3, 5)
    tiles = tiles.reshape(2, FIELDS, PLANES, *TILE)
    packed = (2, FIELDS, HALF) + TILE
    own, far, far_copy, own_copy = pl.pallas_call(
        pack_kernel,
        out_shape=(vmem(*packed),) * 4,
        in_specs=[VMEM],
        out_specs=(VMEM,) * 4,
        compiler_params=PARAMS,
    )(tiles)
    right = [(i + 1) % strips for i in range(strips)]
    left = [(i - 1) % strips for i in range(strips)]
    same = [(i, right[i]) for i in range(strips)]
    same += [(strips + i, strips + left[i]) for i in range(strips)]
    cross = [(i, strips + left[i]) for i in range(strips)]
    cross += [(strips + i, right[i]) for i in range(strips)]
    halo_own = lax.ppermute(far_copy, everyone, same)
    halo_sibling = lax.ppermute(own_copy, everyone, cross)
    swap = [(0, 1), (1, 0)]
    sib_far = lax.ppermute(own, "img", swap)
    sib_own = lax.ppermute(far, "img", swap)
    passed_sibling = lax.ppermute(halo_own, "img", swap)
    passed_own = lax.ppermute(halo_sibling, "img", swap)
    cost = pl.CostEstimate(flops=3_000_000, bytes_accessed=3_000_000, transcendentals=0)
    rows = (own, far, sib_own, sib_far)
    near, sums = pl.pallas_call(
        near_kernel,
        out_shape=(vmem(CELLS, *TILE), vmem(3, *TILE)),
        in_specs=[VMEM] * 6,
        out_specs=(VMEM, VMEM),
        compiler_params=PARAMS,
        cost_estimate=cost,
    )(*map(in_vmem, rows + (halo_own, halo_sibling)))
    rest, parts = pl.pallas_call(
        far_kernel,
        out_shape=(vmem(CELLS, *TILE), vmem(strips, 1, TILE[1])),
        in_specs=[VMEM] * 7,
        out_specs=(VMEM, VMEM),
        compiler_params=PARAMS,
        cost_estimate=cost,
    )(*map(in_vmem, rows + (passed_sibling, passed_own, sums)))
    parts = lax.all_to_all(parts, STRIP, 0, 0, tiled=True)
    parts = parts.reshape(strips // TILE[0], *TILE)
    new, knots = pl.pallas_call(
        combine_kernel,
        out_shape=(
            jax.ShapeDtypeStruct((2, FIELDS, PLANES) + TILE, jnp.float32),
            jax.ShapeDtypeStruct((4,), jnp.float32),
        ),
        in_specs=[VMEM] * 3,
        out_specs=(VMEM, pl.BlockSpec(memory_space=pltpu.SMEM)),
        compiler_params=PARAMS,
    )(in_vmem(parts), in_vmem(near), in_vmem(rest))
    new = new.reshape(2, FIELDS, PLANES, 4, 2, 128).transpose(0, 1, 2, 4, 3, 5)
    return new.reshape(2, FIELDS, PLANES, 2, 512), knots


def solution(mesh):
    fine = Mesh(mesh.devices.reshape(2, 8, 8, 4), ("img",) + STRIP)
    spec = P("img", None, None, STRIP, None)
    return jax.shard_map(
        per_device, mesh=fine, in_specs=(spec,), out_specs=(spec, P()), check_vma=False
    )
```

```python
import jax
import jax.numpy as jnp
from jax import lax
from jax.experimental import pallas as pl
from jax.experimental.pallas import tpu as pltpu
from jax.sharding import Mesh, PartitionSpec as P

KAPPA_PHASE = 1.0
KAPPA_SOLUTE = 0.6
BARRIER = 1.5
COUPLING = 2.0
TIME_STEP = 0.05
EQUILIBRIUM = ((0.8, 0.1), (0.1, 0.8), (0.1, 0.1), (0.45, 0.45))
STRIP = ("z", "y", "x")
FIELDS, PLANES = 6, 16
HALF = PLANES // 2
CELLS = 4 * FIELDS * HALF
TILE = (8, 128)
VMEM = pl.BlockSpec(memory_space=pltpu.VMEM)
PARAMS = pltpu.CompilerParams(vmem_limit_bytes=48 * 1024 * 1024)


def cell(k, f, z):
    return (k * FIELDS + f) * HALF + z


def even_sublanes():
    return lax.broadcasted_iota(jnp.int32, TILE, 0) % 2 == 0


def pack_kernel(source, own, far, far_copy, own_copy, images, arrived):
    core = lax.axis_index("img")
    even = even_sublanes()
    first = jnp.full(TILE, core, jnp.int32) == 0

    def fetch(k, f):
        return pltpu.make_async_copy(source.at[k, f], images.at[k, f], arrived.at[k, f])

    for k in range(2):
        for f in range(FIELDS):
            fetch(k, f).start()

    def field(i, carry):
        k, f = i // FIELDS, i % FIELDS
        fetch(k, f).wait()
        for z in range(HALF):
            low, high = images[k, f, z], images[k, f, z + HALF]
            row0 = jnp.where(even, low, pltpu.roll(high, 1, 0))
            row1 = jnp.where(even, pltpu.roll(low, 7, 0), high)
            mine = jnp.where(first, row0, row1)
            rest = jnp.where(first, row1, row0)
            own[k, f, z] = mine
            far[k, f, z] = rest
            own_copy[k, f, z] = mine
            far_copy[k, f, z] = rest
        return carry

    lax.fori_loop(0, 2 * FIELDS, field, 0)


def step_image(center, beside, halo, j, stepped, g):
    even = even_sublanes()
    lane = lax.broadcasted_iota(jnp.int32, TILE, 1)
    at_first, at_last = lane == 0, lane == 127
    for z in range(HALF):
        cells, sums = [], []
        for f in range(FIELDS):
            c = center[j, f, z]
            if z < HALF - 1:
                raised = center[j, f, z + 1]
            else:
                raised = jnp.where(even, pltpu.roll(center[j, f, 0], 7, 0), c)
            if z > 0:
                lowered = center[j, f, z - 1]
            else:
                lowered = jnp.where(even, c, pltpu.roll(center[j, f, HALF - 1], 1, 0))
            ahead = pltpu.roll(c, 127, 1)
            ahead = jnp.where(at_last, pltpu.roll(ahead, 6, 0), ahead)
            behind = pltpu.roll(c, 1, 1)
            behind = jnp.where(at_first, pltpu.roll(behind, 2, 0), behind)
            around = (beside[j, f, z] + halo[j, f, z]) + (raised + lowered) + (ahead + behind)
            cells.append(c)
            sums.append(around)
        squares = [cells[i] * cells[i] for i in range(4)]
        total = (squares[0] + squares[1]) + (squares[2] + squares[3])
        pulls = []
        for s in range(2):
            value = cells[4 + s]
            for i in range(4):
                value = value - EQUILIBRIUM[i][s] * cells[i]
            pulls.append((TIME_STEP * COUPLING) * value)
        for i in range(4):
            gain = (1.0 - 6.0 * TIME_STEP * KAPPA_PHASE) - (TIME_STEP * 2.0 * BARRIER) * (
                total - squares[i]
            )
            out = gain * cells[i] + (TIME_STEP * KAPPA_PHASE) * sums[i]
            out = out + (EQUILIBRIUM[i][0] * pulls[0] + EQUILIBRIUM[i][1] * pulls[1])
            stepped[cell(g, i, z)] = out
        for s in range(2):
            out = (1.0 - 6.0 * TIME_STEP * KAPPA_SOLUTE) * cells[4 + s]
            out = out + (TIME_STEP * KAPPA_SOLUTE) * sums[4 + s] - pulls[s]
            stepped[cell(g, 4 + s, z)] = out


def step_row(mine, theirs, stepped):
    core = lax.axis_index("img")

    def one(j, carry):
        step_image(*mine, j, stepped, 2 * core + j)
        return carry

    def other(j, carry):
        step_image(*theirs, j, stepped, 2 * (1 - core) + j)
        return carry

    lax.fori_loop(0, 2, one, 0)
    lax.fori_loop(0, 2, other, 0)


def gap_sums(stepped):
    def gather(f, sums):
        new = []
        for k in range(3):
            terms = []
            for z in range(HALF):
                gap = stepped[cell(k + 1, f, z)] - stepped[cell(k, f, z)]
                terms.append(gap * gap)
            while len(terms) > 1:
                terms = [a + b for a, b in zip(terms[::2], terms[1::2])]
            new.append(sums[k] + terms[0])
        return tuple(new)

    zero = jnp.zeros(TILE, jnp.float32)
    return lax.fori_loop(0, FIELDS, gather, (zero, zero, zero))


def near_kernel(own, far, sib_own, sib_far, halo_own, halo_sib, stepped, sums):
    step_row((own, far, halo_own), (sib_own, sib_far, halo_sib), stepped)
    for k, tile in enumerate(gap_sums(stepped)):
        sums[k] = tile


def far_kernel(own, far, sib_own, sib_far, halo_sib, halo_own, sums, stepped, rows):
    step_row((far, own, halo_own), (sib_far, sib_own, halo_sib), stepped)
    lane = lax.broadcasted_iota(jnp.int32, (1, TILE[1]), 1)
    out = jnp.zeros((1, TILE[1]), jnp.float32)
    for k, tile in enumerate(gap_sums(stepped)):
        out = jnp.where(lane == k, jnp.sum(tile + sums[k]), out)

    def row(p, carry):
        rows[p] = out
        return carry

    lax.fori_loop(0, rows.shape[0], row, 0, unroll=16)


def combine_kernel(parts, near, far, target_new, knots, new, written):
    core = lax.axis_index("img")
    even = even_sublanes()
    first = jnp.full(TILE, core, jnp.int32) == 0
    terms = [parts[p] for p in range(parts.shape[0])]
    while len(terms) > 1:
        terms = [a + b for a, b in zip(terms[::2], terms[1::2])]
    lane = lax.broadcasted_iota(jnp.int32, TILE, 1)
    l1, l2, l3 = (
        jnp.sqrt(1.0 + jnp.full(TILE, jnp.sum(jnp.where(lane == k, terms[0], 0.0))))
        for k in range(3)
    )
    whole = l1 + l2 + l3
    k1, k2, k3 = l1 / whole, (l1 + l2) / whole, whole / whole
    w0, w1, w2 = k1, k2 - k1, k3 - k2
    main1, main2 = 2.0 * (w0 + w1), 2.0 * (w1 + w2)
    det = main1 * main2 - w1 * w1
    scale = 6.0 / det
    i0, i1, i2 = 1.0 / w0, 1.0 / w1, 1.0 / w2
    bend1 = (
        -main2 * i0 * scale,
        (main2 + w1) * i1 * scale,
        -w1 * i2 * scale,
    )
    bend2 = (
        w1 * i0 * scale,
        -(main1 + w1) * i1 * scale,
        main1 * i2 * scale,
    )
    zero = jnp.zeros(TILE, jnp.float32)
    values, gaps = [], []
    for j in range(2):
        target = jnp.where(first, jnp.float32(j / 3.0), jnp.float32((j + 2) / 3.0))
        below = 1 + sum((k <= target).astype(jnp.int32) for k in (k1, k2, k3)) - 1
        at = jnp.clip(below, 0, 2)
        h = jnp.where(at == 0, w0, jnp.where(at == 1, w1, w2))
        right = jnp.where(at == 0, k1, jnp.where(at == 1, k2, k3))
        a = (right - target) / h
        b = 1.0 - a
        curve = h * h * (1.0 / 6.0)
        ca, cb = (a * a * a - a) * curve, (b * b * b - b) * curve
        v = [jnp.where(at == k, a, jnp.where(at == k - 1, b, zero)) for k in range(4)]
        c1 = jnp.where(at == 1, ca, jnp.where(at == 0, cb, zero))
        c2 = jnp.where(at == 2, ca, jnp.where(at == 1, cb, zero))
        values.append(v)
        gaps.append([c1 * bend1[m] + c2 * bend2[m] for m in range(3)])
    knots[0] = jnp.float32(0.0)
    knots[1] = k1[0, 0]
    knots[2] = k2[0, 0]
    knots[3] = k3[0, 0]

    def resampled(rows, f, z):
        s = [rows[cell(k, f, z)] for k in range(4)]
        d = [s[k + 1] - s[k] for k in range(3)]
        out = []
        for j in range(2):
            v, e = values[j], gaps[j]
            straight = (v[0] * s[0] + v[1] * s[1]) + (v[2] * s[2] + v[3] * s[3])
            out.append(straight + (e[0] * d[0] + e[1] * d[1] + e[2] * d[2]))
        return out

    def store(j, f):
        return pltpu.make_async_copy(new.at[j, f], target_new.at[j, f], written.at[j, f])

    def field(f, carry):
        for z in range(HALF):
            mine, rest = resampled(near, f, z), resampled(far, f, z)
            for j in range(2):
                row0 = jnp.where(first, mine[j], rest[j])
                row1 = jnp.where(first, rest[j], mine[j])
                new[j, f, z] = jnp.where(even, row0, pltpu.roll(row1, 1, 0))
                new[j, f, z + HALF] = jnp.where(even, pltpu.roll(row0, 7, 0), row1)
        for j in range(2):
            store(j, f).start()
        return carry

    lax.fori_loop(0, FIELDS, field, 0)
    for j in range(2):
        for f in range(FIELDS):
            store(j, f).wait()


def in_hbm(x):
    return pltpu.with_memory_space_constraint(x, pltpu.HBM)


def in_vmem(x):
    return pltpu.with_memory_space_constraint(x, pltpu.VMEM)


def vmem(*shape):
    return pltpu.VMEM(shape, jnp.float32)


def per_device(images):
    everyone = ("img",) + STRIP
    strips = lax.axis_size(STRIP)
    tiles = images.reshape(2, FIELDS, PLANES, 2, 4, 128).transpose(0, 1, 2, 4, 3, 5)
    tiles = tiles.reshape(2, FIELDS, PLANES, *TILE)
    packed = (2, FIELDS, HALF) + TILE
    own, far, far_copy, own_copy = pl.pallas_call(
        pack_kernel,
        out_shape=(vmem(*packed),) * 4,
        in_specs=[pl.BlockSpec(memory_space=pl.ANY)],
        out_specs=(VMEM,) * 4,
        scratch_shapes=[
            pltpu.VMEM((2, FIELDS, PLANES) + TILE, jnp.float32),
            pltpu.SemaphoreType.DMA((2, FIELDS)),
        ],
        compiler_params=PARAMS,
    )(in_hbm(tiles))
    right = [(i + 1) % strips for i in range(strips)]
    left = [(i - 1) % strips for i in range(strips)]
    same = [(i, right[i]) for i in range(strips)]
    same += [(strips + i, strips + left[i]) for i in range(strips)]
    cross = [(i, strips + left[i]) for i in range(strips)]
    cross += [(strips + i, right[i]) for i in range(strips)]
    halo_own = lax.ppermute(far_copy, everyone, same)
    halo_sibling = lax.ppermute(own_copy, everyone, cross)
    swap = [(0, 1), (1, 0)]
    sib_far = lax.ppermute(own, "img", swap)
    sib_own = lax.ppermute(far, "img", swap)
    passed_sibling = lax.ppermute(halo_own, "img", swap)
    passed_own = lax.ppermute(halo_sibling, "img", swap)
    cost = pl.CostEstimate(flops=3_000_000, bytes_accessed=3_000_000, transcendentals=0)
    rows = (own, far, sib_own, sib_far)
    near, sums = pl.pallas_call(
        near_kernel,
        out_shape=(vmem(CELLS, *TILE), vmem(3, *TILE)),
        in_specs=[VMEM] * 6,
        out_specs=(VMEM, VMEM),
        compiler_params=PARAMS,
        cost_estimate=cost,
    )(*map(in_vmem, rows + (halo_own, halo_sibling)))
    rest, parts = pl.pallas_call(
        far_kernel,
        out_shape=(vmem(CELLS, *TILE), vmem(strips, 1, TILE[1])),
        in_specs=[VMEM] * 7,
        out_specs=(VMEM, VMEM),
        compiler_params=PARAMS,
        cost_estimate=cost,
    )(*map(in_vmem, rows + (passed_sibling, passed_own, sums)))
    parts = lax.all_to_all(parts, STRIP, 0, 0, tiled=True)
    parts = parts.reshape(strips // TILE[0], *TILE)
    new, knots = pl.pallas_call(
        combine_kernel,
        out_shape=(
            pltpu.HBM((2, FIELDS, PLANES) + TILE, jnp.float32),
            jax.ShapeDtypeStruct((4,), jnp.float32),
        ),
        in_specs=[VMEM] * 3,
        out_specs=(
            pl.BlockSpec(memory_space=pl.ANY),
            pl.BlockSpec(memory_space=pltpu.SMEM),
        ),
        scratch_shapes=[
            pltpu.VMEM((2, FIELDS, PLANES) + TILE, jnp.float32),
            pltpu.SemaphoreType.DMA((2, FIELDS)),
        ],
        compiler_params=PARAMS,
    )(in_vmem(parts), in_vmem(near), in_vmem(rest))
    new = new.reshape(2, FIELDS, PLANES, 4, 2, 128).transpose(0, 1, 2, 4, 3, 5)
    return new.reshape(2, FIELDS, PLANES, 2, 512), knots


def solution(mesh):
    fine = Mesh(mesh.devices.reshape(2, 8, 8, 4), ("img",) + STRIP)
    spec = P("img", None, None, STRIP, None)
    return jax.shard_map(
        per_device, mesh=fine, in_specs=(spec,), out_specs=(spec, P()), check_vma=False
    )
```

```python
import jax
import jax.numpy as jnp
from jax import lax
from jax.experimental import pallas as pl
from jax.experimental.pallas import tpu as pltpu
from jax.sharding import Mesh, PartitionSpec as P

KAPPA_PHASE = 1.0
KAPPA_SOLUTE = 0.6
BARRIER = 1.5
COUPLING = 2.0
TIME_STEP = 0.05
EQUILIBRIUM = ((0.8, 0.1), (0.1, 0.8), (0.1, 0.1), (0.45, 0.45))
STRIP = ("z", "y", "x")
FIELDS, PLANES = 6, 16
HALF = PLANES // 2
CELLS = 4 * FIELDS * HALF
TILE = (8, 128)
VMEM = pl.BlockSpec(memory_space=pltpu.VMEM)
PARAMS = pltpu.CompilerParams(vmem_limit_bytes=48 * 1024 * 1024)


def cell(k, f, z):
    return (k * FIELDS + f) * HALF + z


def even_sublanes():
    return lax.broadcasted_iota(jnp.int32, TILE, 0) % 2 == 0


def pack_kernel(source, own, far, far_copy, own_copy, images, arrived):
    core = lax.axis_index("img")
    even = even_sublanes()
    first = jnp.full(TILE, core, jnp.int32) == 0

    def fetch(k, f):
        return pltpu.make_async_copy(source.at[k, f], images.at[k, f], arrived.at[k, f])

    for k in range(2):
        for f in range(FIELDS):
            fetch(k, f).start()

    def field(i, carry):
        k, f = i // FIELDS, i % FIELDS
        fetch(k, f).wait()
        for z in range(HALF):
            low, high = images[k, f, z], images[k, f, z + HALF]
            row0 = jnp.where(even, low, pltpu.roll(high, 1, 0))
            row1 = jnp.where(even, pltpu.roll(low, 7, 0), high)
            mine = jnp.where(first, row0, row1)
            rest = jnp.where(first, row1, row0)
            own[k, f, z] = mine
            far[k, f, z] = rest
            own_copy[k, f, z] = mine
            far_copy[k, f, z] = rest
        return carry

    lax.fori_loop(0, 2 * FIELDS, field, 0)


def step_image(center, beside, halo, j, stepped, g):
    even = even_sublanes()
    lane = lax.broadcasted_iota(jnp.int32, TILE, 1)
    at_first, at_last = lane == 0, lane == 127
    for z in range(HALF):
        cells, sums = [], []
        for f in range(FIELDS):
            c = center[j, f, z]
            if z < HALF - 1:
                raised = center[j, f, z + 1]
            else:
                raised = jnp.where(even, pltpu.roll(center[j, f, 0], 7, 0), c)
            if z > 0:
                lowered = center[j, f, z - 1]
            else:
                lowered = jnp.where(even, c, pltpu.roll(center[j, f, HALF - 1], 1, 0))
            ahead = pltpu.roll(c, 127, 1)
            ahead = jnp.where(at_last, pltpu.roll(ahead, 6, 0), ahead)
            behind = pltpu.roll(c, 1, 1)
            behind = jnp.where(at_first, pltpu.roll(behind, 2, 0), behind)
            around = (beside[j, f, z] + halo[j, f, z]) + (raised + lowered) + (ahead + behind)
            cells.append(c)
            sums.append(around)
        squares = [cells[i] * cells[i] for i in range(4)]
        total = (squares[0] + squares[1]) + (squares[2] + squares[3])
        pulls = []
        for s in range(2):
            value = cells[4 + s]
            for i in range(4):
                value = value - EQUILIBRIUM[i][s] * cells[i]
            pulls.append((TIME_STEP * COUPLING) * value)
        for i in range(4):
            gain = (1.0 - 6.0 * TIME_STEP * KAPPA_PHASE) - (TIME_STEP * 2.0 * BARRIER) * (
                total - squares[i]
            )
            out = gain * cells[i] + (TIME_STEP * KAPPA_PHASE) * sums[i]
            out = out + (EQUILIBRIUM[i][0] * pulls[0] + EQUILIBRIUM[i][1] * pulls[1])
            stepped[cell(g, i, z)] = out
        for s in range(2):
            out = (1.0 - 6.0 * TIME_STEP * KAPPA_SOLUTE) * cells[4 + s]
            out = out + (TIME_STEP * KAPPA_SOLUTE) * sums[4 + s] - pulls[s]
            stepped[cell(g, 4 + s, z)] = out


def step_row(mine, theirs, stepped):
    core = lax.axis_index("img")

    def one(j, carry):
        step_image(*mine, j, stepped, 2 * core + j)
        return carry

    def other(j, carry):
        step_image(*theirs, j, stepped, 2 * (1 - core) + j)
        return carry

    lax.fori_loop(0, 2, one, 0)
    lax.fori_loop(0, 2, other, 0)


def gap_sums(stepped):
    def gather(f, sums):
        new = []
        for k in range(3):
            terms = []
            for z in range(HALF):
                gap = stepped[cell(k + 1, f, z)] - stepped[cell(k, f, z)]
                terms.append(gap * gap)
            while len(terms) > 1:
                terms = [a + b for a, b in zip(terms[::2], terms[1::2])]
            new.append(sums[k] + terms[0])
        return tuple(new)

    zero = jnp.zeros(TILE, jnp.float32)
    return lax.fori_loop(0, FIELDS, gather, (zero, zero, zero))


def near_kernel(own, far, sib_own, sib_far, halo_own, halo_sib, stepped, sums):
    step_row((own, far, halo_own), (sib_own, sib_far, halo_sib), stepped)
    for k, tile in enumerate(gap_sums(stepped)):
        sums[k] = tile


def far_kernel(own, far, sib_own, sib_far, halo_sib, halo_own, sums, stepped, rows):
    step_row((far, own, halo_own), (sib_far, sib_own, halo_sib), stepped)
    lane = lax.broadcasted_iota(jnp.int32, (1, TILE[1]), 1)
    out = jnp.zeros((1, TILE[1]), jnp.float32)
    for k, tile in enumerate(gap_sums(stepped)):
        out = jnp.where(lane == k, jnp.sum(tile + sums[k]), out)

    def row(p, carry):
        rows[p] = out
        return carry

    lax.fori_loop(0, rows.shape[0], row, 0, unroll=16)


def total_tile(parts):
    terms = [parts[p] for p in range(parts.shape[0])]
    while len(terms) > 1:
        terms = [a + b for a, b in zip(terms[::2], terms[1::2])]
    return terms[0]


def resum_kernel(parts, rows):
    total = jnp.sum(total_tile(parts), axis=0, keepdims=True)
    for p in range(rows.shape[0]):
        rows[p] = total


def combine_kernel(parts, near, far, new, knots):
    core = lax.axis_index("img")
    even = even_sublanes()
    first = jnp.full(TILE, core, jnp.int32) == 0
    total = total_tile(parts)
    lane = lax.broadcasted_iota(jnp.int32, TILE, 1)
    l1, l2, l3 = (
        jnp.sqrt(1.0 + jnp.full(TILE, jnp.sum(jnp.where(lane == k, total, 0.0))))
        for k in range(3)
    )
    whole = l1 + l2 + l3
    k1, k2, k3 = l1 / whole, (l1 + l2) / whole, whole / whole
    w0, w1, w2 = k1, k2 - k1, k3 - k2
    main1, main2 = 2.0 * (w0 + w1), 2.0 * (w1 + w2)
    det = main1 * main2 - w1 * w1
    scale = 6.0 / det
    i0, i1, i2 = 1.0 / w0, 1.0 / w1, 1.0 / w2
    bend1 = (
        -main2 * i0 * scale,
        (main2 + w1) * i1 * scale,
        -w1 * i2 * scale,
    )
    bend2 = (
        w1 * i0 * scale,
        -(main1 + w1) * i1 * scale,
        main1 * i2 * scale,
    )
    zero = jnp.zeros(TILE, jnp.float32)
    values, gaps = [], []
    for j in range(2):
        target = jnp.where(first, jnp.float32(j / 3.0), jnp.float32((j + 2) / 3.0))
        below = 1 + sum((k <= target).astype(jnp.int32) for k in (k1, k2, k3)) - 1
        at = jnp.clip(below, 0, 2)
        h = jnp.where(at == 0, w0, jnp.where(at == 1, w1, w2))
        right = jnp.where(at == 0, k1, jnp.where(at == 1, k2, k3))
        a = (right - target) / h
        b = 1.0 - a
        curve = h * h * (1.0 / 6.0)
        ca, cb = (a * a * a - a) * curve, (b * b * b - b) * curve
        v = [jnp.where(at == k, a, jnp.where(at == k - 1, b, zero)) for k in range(4)]
        c1 = jnp.where(at == 1, ca, jnp.where(at == 0, cb, zero))
        c2 = jnp.where(at == 2, ca, jnp.where(at == 1, cb, zero))
        values.append(v)
        gaps.append([c1 * bend1[m] + c2 * bend2[m] for m in range(3)])
    knots[0] = jnp.float32(0.0)
    knots[1] = k1[0, 0]
    knots[2] = k2[0, 0]
    knots[3] = k3[0, 0]

    def resampled(rows, f, z):
        s = [rows[cell(k, f, z)] for k in range(4)]
        d = [s[k + 1] - s[k] for k in range(3)]
        out = []
        for j in range(2):
            v, e = values[j], gaps[j]
            straight = (v[0] * s[0] + v[1] * s[1]) + (v[2] * s[2] + v[3] * s[3])
            out.append(straight + (e[0] * d[0] + e[1] * d[1] + e[2] * d[2]))
        return out

    def field(f, carry):
        for z in range(HALF):
            mine, rest = resampled(near, f, z), resampled(far, f, z)
            for j in range(2):
                row0 = jnp.where(first, mine[j], rest[j])
                row1 = jnp.where(first, rest[j], mine[j])
                new[j, f, z] = jnp.where(even, row0, pltpu.roll(row1, 1, 0))
                new[j, f, z + HALF] = jnp.where(even, pltpu.roll(row0, 7, 0), row1)
        return carry

    lax.fori_loop(0, FIELDS, field, 0)


def in_hbm(x):
    return pltpu.with_memory_space_constraint(x, pltpu.HBM)


def in_vmem(x):
    return pltpu.with_memory_space_constraint(x, pltpu.VMEM)


def vmem(*shape):
    return pltpu.VMEM(shape, jnp.float32)


def per_device(images):
    everyone = ("img",) + STRIP
    strips = lax.axis_size(STRIP)
    plane, depth = lax.axis_size(("y", "x")), lax.axis_size("z")
    tiles = images.reshape(2, FIELDS, PLANES, 2, 4, 128).transpose(0, 1, 2, 4, 3, 5)
    tiles = tiles.reshape(2, FIELDS, PLANES, *TILE)
    packed = (2, FIELDS, HALF) + TILE
    own, far, far_copy, own_copy = pl.pallas_call(
        pack_kernel,
        out_shape=(vmem(*packed),) * 4,
        in_specs=[pl.BlockSpec(memory_space=pl.ANY)],
        out_specs=(VMEM,) * 4,
        scratch_shapes=[
            pltpu.VMEM((2, FIELDS, PLANES) + TILE, jnp.float32),
            pltpu.SemaphoreType.DMA((2, FIELDS)),
        ],
        compiler_params=PARAMS,
    )(in_hbm(tiles))
    right = [(i + 1) % strips for i in range(strips)]
    left = [(i - 1) % strips for i in range(strips)]
    same = [(i, right[i]) for i in range(strips)]
    same += [(strips + i, strips + left[i]) for i in range(strips)]
    cross = [(i, strips + left[i]) for i in range(strips)]
    cross += [(strips + i, right[i]) for i in range(strips)]
    halo_own = lax.ppermute(far_copy, everyone, same)
    halo_sibling = lax.ppermute(own_copy, everyone, cross)
    swap = [(0, 1), (1, 0)]
    sib_far = lax.ppermute(own, "img", swap)
    sib_own = lax.ppermute(far, "img", swap)
    passed_sibling = lax.ppermute(halo_own, "img", swap)
    passed_own = lax.ppermute(halo_sibling, "img", swap)
    cost = pl.CostEstimate(flops=3_000_000, bytes_accessed=3_000_000, transcendentals=0)
    rows = (own, far, sib_own, sib_far)
    near, sums = pl.pallas_call(
        near_kernel,
        out_shape=(vmem(CELLS, *TILE), vmem(3, *TILE)),
        in_specs=[VMEM] * 6,
        out_specs=(VMEM, VMEM),
        compiler_params=PARAMS,
        cost_estimate=cost,
    )(*map(in_vmem, rows + (halo_own, halo_sibling)))
    rest, parts = pl.pallas_call(
        far_kernel,
        out_shape=(vmem(CELLS, *TILE), vmem(plane, 1, TILE[1])),
        in_specs=[VMEM] * 7,
        out_specs=(VMEM, VMEM),
        compiler_params=PARAMS,
        cost_estimate=cost,
    )(*map(in_vmem, rows + (passed_sibling, passed_own, sums)))
    parts = lax.all_to_all(parts, ("y", "x"), 0, 0, tiled=True)
    parts = pl.pallas_call(
        resum_kernel,
        out_shape=vmem(depth, 1, TILE[1]),
        in_specs=[VMEM],
        out_specs=VMEM,
        compiler_params=PARAMS,
    )(in_vmem(parts.reshape(-1, *TILE)))
    parts = lax.all_to_all(parts, "z", 0, 0, tiled=True)
    parts = parts.reshape(-1, *TILE)
    new, knots = pl.pallas_call(
        combine_kernel,
        out_shape=(
            jax.ShapeDtypeStruct((2, FIELDS, PLANES) + TILE, jnp.float32),
            jax.ShapeDtypeStruct((4,), jnp.float32),
        ),
        in_specs=[VMEM] * 3,
        out_specs=(VMEM, pl.BlockSpec(memory_space=pltpu.SMEM)),
        compiler_params=PARAMS,
    )(in_vmem(parts), in_vmem(near), in_vmem(rest))
    new = new.reshape(2, FIELDS, PLANES, 4, 2, 128).transpose(0, 1, 2, 4, 3, 5)
    return new.reshape(2, FIELDS, PLANES, 2, 512), knots


def solution(mesh):
    fine = Mesh(mesh.devices.reshape(2, 8, 8, 4), ("img",) + STRIP)
    spec = P("img", None, None, STRIP, None)
    return jax.shard_map(
        per_device, mesh=fine, in_specs=(spec,), out_specs=(spec, P()), check_vma=False
    )
```

```python
import jax
import jax.numpy as jnp
from jax import lax
from jax.experimental import pallas as pl
from jax.experimental.pallas import tpu as pltpu
from jax.sharding import Mesh, PartitionSpec as P

KAPPA_PHASE = 1.0
KAPPA_SOLUTE = 0.6
BARRIER = 1.5
COUPLING = 2.0
TIME_STEP = 0.05
EQUILIBRIUM = ((0.8, 0.1), (0.1, 0.8), (0.1, 0.1), (0.45, 0.45))
STRIP = ("z", "y", "x")
FIELDS, PLANES = 6, 16
HALF = PLANES // 2
CELLS = 2 * FIELDS * HALF
TILE = (8, 128)
VMEM = pl.BlockSpec(memory_space=pltpu.VMEM)
PARAMS = pltpu.CompilerParams(vmem_limit_bytes=48 * 1024 * 1024)


def cell(k, f, z):
    return (k * FIELDS + f) * HALF + z


def even_sublanes():
    return lax.broadcasted_iota(jnp.int32, TILE, 0) % 2 == 0


def pack_kernel(source, own, far, far_copy, own_copy, images, arrived):
    core = lax.axis_index("img")
    even = even_sublanes()
    first = jnp.full(TILE, core, jnp.int32) == 0

    def fetch(k, f):
        return pltpu.make_async_copy(source.at[k, f], images.at[k, f], arrived.at[k, f])

    for k in range(2):
        for f in range(FIELDS):
            fetch(k, f).start()

    def field(i, carry):
        k, f = i // FIELDS, i % FIELDS
        fetch(k, f).wait()
        for z in range(HALF):
            low, high = images[k, f, z], images[k, f, z + HALF]
            row0 = jnp.where(even, low, pltpu.roll(high, 1, 0))
            row1 = jnp.where(even, pltpu.roll(low, 7, 0), high)
            mine = jnp.where(first, row0, row1)
            rest = jnp.where(first, row1, row0)
            own[k, f, z] = mine
            far[k, f, z] = rest
            own_copy[k, f, z] = mine
            far_copy[k, f, z] = rest
        return carry

    lax.fori_loop(0, 2 * FIELDS, field, 0)


def step_image(center, beside, halo, j, stepped, g):
    even = even_sublanes()
    lane = lax.broadcasted_iota(jnp.int32, TILE, 1)
    at_first, at_last = lane == 0, lane == 127
    for z in range(HALF):
        cells, sums = [], []
        for f in range(FIELDS):
            c = center[j, f, z]
            if z < HALF - 1:
                raised = center[j, f, z + 1]
            else:
                raised = jnp.where(even, pltpu.roll(center[j, f, 0], 7, 0), c)
            if z > 0:
                lowered = center[j, f, z - 1]
            else:
                lowered = jnp.where(even, c, pltpu.roll(center[j, f, HALF - 1], 1, 0))
            ahead = pltpu.roll(c, 127, 1)
            ahead = jnp.where(at_last, pltpu.roll(ahead, 6, 0), ahead)
            behind = pltpu.roll(c, 1, 1)
            behind = jnp.where(at_first, pltpu.roll(behind, 2, 0), behind)
            around = (beside[j, f, z] + halo[j, f, z]) + (raised + lowered) + (ahead + behind)
            cells.append(c)
            sums.append(around)
        squares = [cells[i] * cells[i] for i in range(4)]
        total = (squares[0] + squares[1]) + (squares[2] + squares[3])
        pulls = []
        for s in range(2):
            value = cells[4 + s]
            for i in range(4):
                value = value - EQUILIBRIUM[i][s] * cells[i]
            pulls.append((TIME_STEP * COUPLING) * value)
        for i in range(4):
            gain = (1.0 - 6.0 * TIME_STEP * KAPPA_PHASE) - (TIME_STEP * 2.0 * BARRIER) * (
                total - squares[i]
            )
            out = gain * cells[i] + (TIME_STEP * KAPPA_PHASE) * sums[i]
            out = out + (EQUILIBRIUM[i][0] * pulls[0] + EQUILIBRIUM[i][1] * pulls[1])
            stepped[cell(g, i, z)] = out
        for s in range(2):
            out = (1.0 - 6.0 * TIME_STEP * KAPPA_SOLUTE) * cells[4 + s]
            out = out + (TIME_STEP * KAPPA_SOLUTE) * sums[4 + s] - pulls[s]
            stepped[cell(g, 4 + s, z)] = out


def own_kernel(own, far, halo, stepped):
    def one(j, carry):
        step_image(own, far, halo, j, stepped, j)
        return carry

    lax.fori_loop(0, 2, one, 0)


def sibling_kernel(own, far, halo, mine, stepped):
    core = lax.axis_index("img")

    def one(j, carry):
        step_image(own, far, halo, j, stepped, j)
        return carry

    lax.fori_loop(0, 2, one, 0)

    def gather(f, sums):
        pairs = (
            (mine, 1, mine, 0),
            (mine, 1 - core, stepped, core),
            (stepped, 1, stepped, 0),
        )
        new = []
        for total, (one, k, other, m) in zip(sums, pairs):
            terms = []
            for z in range(HALF):
                gap = one[cell(k, f, z)] - other[cell(m, f, z)]
                terms.append(gap * gap)
            while len(terms) > 1:
                terms = [a + b for a, b in zip(terms[::2], terms[1::2])]
            new.append(total + terms[0])
        return tuple(new)

    zero = jnp.zeros(TILE, jnp.float32)
    own_gap, cross_gap, other_gap = lax.fori_loop(0, FIELDS, gather, (zero, zero, zero))
    lane = lax.broadcasted_iota(jnp.int32, TILE, 1)
    out = jnp.where(lane == 2 * core, jnp.sum(own_gap), zero)
    out = jnp.where(lane == 1, jnp.sum(cross_gap), out)
    stepped[CELLS] = jnp.where(lane == 2 - 2 * core, jnp.sum(other_gap), out)


def add_kernel(near, rest, rows):
    total = near[CELLS, 0:1, :] + rest[CELLS, 0:1, :]

    def row(p, carry):
        rows[p] = total
        return carry

    lax.fori_loop(0, rows.shape[0], row, 0, unroll=16)


def total_tile(parts):
    terms = [parts[p] for p in range(parts.shape[0])]
    while len(terms) > 1:
        terms = [a + b for a, b in zip(terms[::2], terms[1::2])]
    return terms[0]


def combine_kernel(parts, near_own, near_sib, far_own, far_sib, new, knots):
    core = lax.axis_index("img")
    even = even_sublanes()
    first = jnp.full(TILE, core, jnp.int32) == 0
    total = total_tile(parts)
    lane = lax.broadcasted_iota(jnp.int32, TILE, 1)
    l1, l2, l3 = (
        jnp.sqrt(1.0 + jnp.full(TILE, jnp.sum(jnp.where(lane == k, total, 0.0))))
        for k in range(3)
    )
    whole = l1 + l2 + l3
    k1, k2, k3 = l1 / whole, (l1 + l2) / whole, whole / whole
    w0, w1, w2 = k1, k2 - k1, k3 - k2
    main1, main2 = 2.0 * (w0 + w1), 2.0 * (w1 + w2)
    det = main1 * main2 - w1 * w1
    scale = 6.0 / det
    i0, i1, i2 = 1.0 / w0, 1.0 / w1, 1.0 / w2
    bend1 = (
        -main2 * i0 * scale,
        (main2 + w1) * i1 * scale,
        -w1 * i2 * scale,
    )
    bend2 = (
        w1 * i0 * scale,
        -(main1 + w1) * i1 * scale,
        main1 * i2 * scale,
    )
    zero = jnp.zeros(TILE, jnp.float32)
    values, gaps = [], []
    for j in range(2):
        target = jnp.where(first, jnp.float32(j / 3.0), jnp.float32((j + 2) / 3.0))
        below = 1 + sum((k <= target).astype(jnp.int32) for k in (k1, k2, k3)) - 1
        at = jnp.clip(below, 0, 2)
        h = jnp.where(at == 0, w0, jnp.where(at == 1, w1, w2))
        right = jnp.where(at == 0, k1, jnp.where(at == 1, k2, k3))
        a = (right - target) / h
        b = 1.0 - a
        curve = h * h * (1.0 / 6.0)
        ca, cb = (a * a * a - a) * curve, (b * b * b - b) * curve
        v = [jnp.where(at == k, a, jnp.where(at == k - 1, b, zero)) for k in range(4)]
        c1 = jnp.where(at == 1, ca, jnp.where(at == 0, cb, zero))
        c2 = jnp.where(at == 2, ca, jnp.where(at == 1, cb, zero))
        values.append(v)
        gaps.append([c1 * bend1[m] + c2 * bend2[m] for m in range(3)])
    knots[0] = jnp.float32(0.0)
    knots[1] = k1[0, 0]
    knots[2] = k2[0, 0]
    knots[3] = k3[0, 0]

    def resampled(rows, f, z):
        s = [rows[k // 2][cell(k % 2, f, z)] for k in range(4)]
        d = [s[k + 1] - s[k] for k in range(3)]
        out = []
        for j in range(2):
            v, e = values[j], gaps[j]
            straight = (v[0] * s[0] + v[1] * s[1]) + (v[2] * s[2] + v[3] * s[3])
            out.append(straight + (e[0] * d[0] + e[1] * d[1] + e[2] * d[2]))
        return out

    def write(even_rows, odd_rows):
        def field(f, carry):
            for z in range(HALF):
                row0, row1 = resampled(even_rows, f, z), resampled(odd_rows, f, z)
                for j in range(2):
                    new[j, f, z] = jnp.where(even, row0[j], pltpu.roll(row1[j], 1, 0))
                    new[j, f, z + HALF] = jnp.where(even, pltpu.roll(row0[j], 7, 0), row1[j])
            return carry

        lax.fori_loop(0, FIELDS, field, 0)

    @pl.when(core == 0)
    def _():
        write((near_own, near_sib), (far_own, far_sib))

    @pl.when(core == 1)
    def _():
        write((far_sib, far_own), (near_sib, near_own))


def in_hbm(x):
    return pltpu.with_memory_space_constraint(x, pltpu.HBM)


def in_vmem(x):
    return pltpu.with_memory_space_constraint(x, pltpu.VMEM)


def vmem(*shape):
    return pltpu.VMEM(shape, jnp.float32)


def per_device(images):
    everyone = ("img",) + STRIP
    strips = lax.axis_size(STRIP)
    tiles = images.reshape(2, FIELDS, PLANES, 2, 4, 128).transpose(0, 1, 2, 4, 3, 5)
    tiles = tiles.reshape(2, FIELDS, PLANES, *TILE)
    packed = (2, FIELDS, HALF) + TILE
    own, far, far_copy, own_copy = pl.pallas_call(
        pack_kernel,
        out_shape=(vmem(*packed),) * 4,
        in_specs=[pl.BlockSpec(memory_space=pl.ANY)],
        out_specs=(VMEM,) * 4,
        scratch_shapes=[
            pltpu.VMEM((2, FIELDS, PLANES) + TILE, jnp.float32),
            pltpu.SemaphoreType.DMA((2, FIELDS)),
        ],
        compiler_params=PARAMS,
    )(in_hbm(tiles))
    right = [(i + 1) % strips for i in range(strips)]
    left = [(i - 1) % strips for i in range(strips)]
    same = [(i, right[i]) for i in range(strips)]
    same += [(strips + i, strips + left[i]) for i in range(strips)]
    cross = [(i, strips + left[i]) for i in range(strips)]
    cross += [(strips + i, right[i]) for i in range(strips)]
    halo_own = lax.ppermute(far_copy, everyone, same)
    halo_sibling = lax.ppermute(own_copy, everyone, cross)
    swap = [(0, 1), (1, 0)]
    sib_far = lax.ppermute(own, "img", swap)
    sib_own = lax.ppermute(far, "img", swap)
    cost = pl.CostEstimate(flops=1_500_000, bytes_accessed=1_500_000, transcendentals=0)
    near_own = pl.pallas_call(
        own_kernel,
        out_shape=vmem(CELLS, *TILE),
        in_specs=[VMEM] * 3,
        out_specs=VMEM,
        compiler_params=PARAMS,
        cost_estimate=cost,
    )(*map(in_vmem, (own, far, halo_own)))
    far_sib = lax.ppermute(near_own, "img", swap)
    near_sib = pl.pallas_call(
        sibling_kernel,
        out_shape=vmem(CELLS + 1, *TILE),
        in_specs=[VMEM] * 4,
        out_specs=VMEM,
        compiler_params=PARAMS,
        cost_estimate=cost,
    )(*map(in_vmem, (sib_own, sib_far, halo_sibling, near_own)))
    near_sib, far_sib = lax.optimization_barrier((near_sib, far_sib))
    far_own = lax.ppermute(near_sib, "img", swap)
    parts = pl.pallas_call(
        add_kernel,
        out_shape=vmem(strips, 1, TILE[1]),
        in_specs=[VMEM] * 2,
        out_specs=VMEM,
        compiler_params=PARAMS,
    )(in_vmem(near_sib), in_vmem(far_own))
    parts = lax.all_to_all(parts, STRIP, 0, 0, tiled=True)
    parts = parts.reshape(-1, *TILE)
    new, knots = pl.pallas_call(
        combine_kernel,
        out_shape=(
            jax.ShapeDtypeStruct((2, FIELDS, PLANES) + TILE, jnp.float32),
            jax.ShapeDtypeStruct((4,), jnp.float32),
        ),
        in_specs=[VMEM] * 5,
        out_specs=(VMEM, pl.BlockSpec(memory_space=pltpu.SMEM)),
        compiler_params=PARAMS,
    )(*map(in_vmem, (parts, near_own, near_sib, far_own, far_sib)))
    new = new.reshape(2, FIELDS, PLANES, 4, 2, 128).transpose(0, 1, 2, 4, 3, 5)
    return new.reshape(2, FIELDS, PLANES, 2, 512), knots


def solution(mesh):
    fine = Mesh(mesh.devices.reshape(2, 8, 8, 4), ("img",) + STRIP)
    spec = P("img", None, None, STRIP, None)
    return jax.shard_map(
        per_device, mesh=fine, in_specs=(spec,), out_specs=(spec, P()), check_vma=False
    )
```

```python
import jax
import jax.numpy as jnp
from jax import lax
from jax.experimental import pallas as pl
from jax.experimental.pallas import tpu as pltpu
from jax.sharding import Mesh, PartitionSpec as P

KAPPA_PHASE = 1.0
KAPPA_SOLUTE = 0.6
BARRIER = 1.5
COUPLING = 2.0
TIME_STEP = 0.05
EQUILIBRIUM = ((0.8, 0.1), (0.1, 0.8), (0.1, 0.1), (0.45, 0.45))
STRIP = ("z", "y", "x")
FIELDS, PLANES = 6, 16
HALF = PLANES // 2
CELLS = 2 * FIELDS * HALF
PAD = 8
TILE = (8, 128)
VMEM = pl.BlockSpec(memory_space=pltpu.VMEM)
PARAMS = pltpu.CompilerParams(vmem_limit_bytes=48 * 1024 * 1024)


def cell(k, f, z):
    return (k * FIELDS + f) * HALF + z


def even_sublanes():
    return lax.broadcasted_iota(jnp.int32, TILE, 0) % 2 == 0


def pack_kernel(source, own, far, far_copy, own_copy, images, arrived):
    core = lax.axis_index("img")
    even = even_sublanes()
    first = jnp.full(TILE, core, jnp.int32) == 0

    def fetch(k, f):
        return pltpu.make_async_copy(source.at[k, f], images.at[k, f], arrived.at[k, f])

    for k in range(2):
        for f in range(FIELDS):
            fetch(k, f).start()

    def field(i, carry):
        k, f = i // FIELDS, i % FIELDS
        fetch(k, f).wait()
        for z in range(HALF):
            low, high = images[k, f, z], images[k, f, z + HALF]
            row0 = jnp.where(even, low, pltpu.roll(high, 1, 0))
            row1 = jnp.where(even, pltpu.roll(low, 7, 0), high)
            mine = jnp.where(first, row0, row1)
            rest = jnp.where(first, row1, row0)
            own[k, f, z] = mine
            far[k, f, z] = rest
            own_copy[k, f, z] = mine
            far_copy[k, f, z] = rest
        return carry

    lax.fori_loop(0, 2 * FIELDS, field, 0)


def step_image(center, beside, halo, j, stepped, g):
    even = even_sublanes()
    lane = lax.broadcasted_iota(jnp.int32, TILE, 1)
    at_first, at_last = lane == 0, lane == 127
    for z in range(HALF):
        cells, sums = [], []
        for f in range(FIELDS):
            c = center[j, f, z]
            if z < HALF - 1:
                raised = center[j, f, z + 1]
            else:
                raised = jnp.where(even, pltpu.roll(center[j, f, 0], 7, 0), c)
            if z > 0:
                lowered = center[j, f, z - 1]
            else:
                lowered = jnp.where(even, c, pltpu.roll(center[j, f, HALF - 1], 1, 0))
            ahead = pltpu.roll(c, 127, 1)
            ahead = jnp.where(at_last, pltpu.roll(ahead, 6, 0), ahead)
            behind = pltpu.roll(c, 1, 1)
            behind = jnp.where(at_first, pltpu.roll(behind, 2, 0), behind)
            around = (beside[j, f, z] + halo[j, f, z]) + (raised + lowered) + (ahead + behind)
            cells.append(c)
            sums.append(around)
        squares = [cells[i] * cells[i] for i in range(4)]
        total = (squares[0] + squares[1]) + (squares[2] + squares[3])
        pulls = []
        for s in range(2):
            value = cells[4 + s]
            for i in range(4):
                value = value - EQUILIBRIUM[i][s] * cells[i]
            pulls.append((TIME_STEP * COUPLING) * value)
        for i in range(4):
            gain = (1.0 - 6.0 * TIME_STEP * KAPPA_PHASE) - (TIME_STEP * 2.0 * BARRIER) * (
                total - squares[i]
            )
            out = gain * cells[i] + (TIME_STEP * KAPPA_PHASE) * sums[i]
            out = out + (EQUILIBRIUM[i][0] * pulls[0] + EQUILIBRIUM[i][1] * pulls[1])
            stepped[cell(g, i, z)] = out
        for s in range(2):
            out = (1.0 - 6.0 * TIME_STEP * KAPPA_SOLUTE) * cells[4 + s]
            out = out + (TIME_STEP * KAPPA_SOLUTE) * sums[4 + s] - pulls[s]
            stepped[cell(g, 4 + s, z)] = out


def own_kernel(own, far, halo, stepped):
    def one(j, carry):
        step_image(own, far, halo, j, stepped, j)
        return carry

    lax.fori_loop(0, 2, one, 0)
    for p in range(CELLS, stepped.shape[0]):
        stepped[p] = jnp.zeros(TILE, jnp.float32)


def sibling_kernel(own, far, halo, mine, stepped):
    core = lax.axis_index("img")

    def one(j, carry):
        step_image(own, far, halo, j, stepped, j)
        return carry

    lax.fori_loop(0, 2, one, 0)

    def gather(f, sums):
        pairs = (
            (mine, 1, mine, 0),
            (mine, 1 - core, stepped, core),
            (stepped, 1, stepped, 0),
        )
        new = []
        for total, (one, k, other, m) in zip(sums, pairs):
            terms = []
            for z in range(HALF):
                gap = one[cell(k, f, z)] - other[cell(m, f, z)]
                terms.append(gap * gap)
            while len(terms) > 1:
                terms = [a + b for a, b in zip(terms[::2], terms[1::2])]
            new.append(total + terms[0])
        return tuple(new)

    zero = jnp.zeros(TILE, jnp.float32)
    own_gap, cross_gap, other_gap = lax.fori_loop(0, FIELDS, gather, (zero, zero, zero))
    lane = lax.broadcasted_iota(jnp.int32, TILE, 1)
    out = jnp.where(lane == 2 * core, jnp.sum(own_gap), zero)
    out = jnp.where(lane == 1, jnp.sum(cross_gap), out)
    stepped[CELLS] = jnp.where(lane == 2 - 2 * core, jnp.sum(other_gap), out)


def add_kernel(near, rest, rows):
    total = near[CELLS, 0:1, :] + rest[CELLS, 0:1, :]

    def row(p, carry):
        rows[p] = total
        return carry

    lax.fori_loop(0, rows.shape[0], row, 0, unroll=16)


def total_tile(parts):
    terms = [parts[p] for p in range(parts.shape[0])]
    while len(terms) > 1:
        terms = [a + b for a, b in zip(terms[::2], terms[1::2])]
    return terms[0]


def combine_kernel(parts, near_own, near_sib, far_own, far_sib, new, knots):
    core = lax.axis_index("img")
    even = even_sublanes()
    first = jnp.full(TILE, core, jnp.int32) == 0
    total = total_tile(parts)
    lane = lax.broadcasted_iota(jnp.int32, TILE, 1)
    l1, l2, l3 = (
        jnp.sqrt(1.0 + jnp.full(TILE, jnp.sum(jnp.where(lane == k, total, 0.0))))
        for k in range(3)
    )
    whole = l1 + l2 + l3
    k1, k2, k3 = l1 / whole, (l1 + l2) / whole, whole / whole
    w0, w1, w2 = k1, k2 - k1, k3 - k2
    main1, main2 = 2.0 * (w0 + w1), 2.0 * (w1 + w2)
    det = main1 * main2 - w1 * w1
    scale = 6.0 / det
    i0, i1, i2 = 1.0 / w0, 1.0 / w1, 1.0 / w2
    bend1 = (
        -main2 * i0 * scale,
        (main2 + w1) * i1 * scale,
        -w1 * i2 * scale,
    )
    bend2 = (
        w1 * i0 * scale,
        -(main1 + w1) * i1 * scale,
        main1 * i2 * scale,
    )
    zero = jnp.zeros(TILE, jnp.float32)
    values, gaps = [], []
    for j in range(2):
        target = jnp.where(first, jnp.float32(j / 3.0), jnp.float32((j + 2) / 3.0))
        below = 1 + sum((k <= target).astype(jnp.int32) for k in (k1, k2, k3)) - 1
        at = jnp.clip(below, 0, 2)
        h = jnp.where(at == 0, w0, jnp.where(at == 1, w1, w2))
        right = jnp.where(at == 0, k1, jnp.where(at == 1, k2, k3))
        a = (right - target) / h
        b = 1.0 - a
        curve = h * h * (1.0 / 6.0)
        ca, cb = (a * a * a - a) * curve, (b * b * b - b) * curve
        v = [jnp.where(at == k, a, jnp.where(at == k - 1, b, zero)) for k in range(4)]
        c1 = jnp.where(at == 1, ca, jnp.where(at == 0, cb, zero))
        c2 = jnp.where(at == 2, ca, jnp.where(at == 1, cb, zero))
        values.append(v)
        gaps.append([c1 * bend1[m] + c2 * bend2[m] for m in range(3)])
    knots[0] = jnp.float32(0.0)
    knots[1] = k1[0, 0]
    knots[2] = k2[0, 0]
    knots[3] = k3[0, 0]

    def resampled(rows, f, z):
        s = [rows[k // 2][cell(k % 2, f, z)] for k in range(4)]
        d = [s[k + 1] - s[k] for k in range(3)]
        out = []
        for j in range(2):
            v, e = values[j], gaps[j]
            straight = (v[0] * s[0] + v[1] * s[1]) + (v[2] * s[2] + v[3] * s[3])
            out.append(straight + (e[0] * d[0] + e[1] * d[1] + e[2] * d[2]))
        return out

    def write(even_rows, odd_rows):
        def field(f, carry):
            for z in range(HALF):
                row0, row1 = resampled(even_rows, f, z), resampled(odd_rows, f, z)
                for j in range(2):
                    new[j, f, z] = jnp.where(even, row0[j], pltpu.roll(row1[j], 1, 0))
                    new[j, f, z + HALF] = jnp.where(even, pltpu.roll(row0[j], 7, 0), row1[j])
            return carry

        lax.fori_loop(0, FIELDS, field, 0)

    @pl.when(core == 0)
    def _():
        write((near_own, near_sib), (far_own, far_sib))

    @pl.when(core == 1)
    def _():
        write((far_sib, far_own), (near_sib, near_own))


def in_hbm(x):
    return pltpu.with_memory_space_constraint(x, pltpu.HBM)


def in_vmem(x):
    return pltpu.with_memory_space_constraint(x, pltpu.VMEM)


def vmem(*shape):
    return pltpu.VMEM(shape, jnp.float32)


def per_device(images):
    everyone = ("img",) + STRIP
    strips = lax.axis_size(STRIP)
    tiles = images.reshape(2, FIELDS, PLANES, 2, 4, 128).transpose(0, 1, 2, 4, 3, 5)
    tiles = tiles.reshape(2, FIELDS, PLANES, *TILE)
    packed = (2, FIELDS, HALF) + TILE
    own, far, far_copy, own_copy = pl.pallas_call(
        pack_kernel,
        out_shape=(vmem(*packed),) * 4,
        in_specs=[pl.BlockSpec(memory_space=pl.ANY)],
        out_specs=(VMEM,) * 4,
        scratch_shapes=[
            pltpu.VMEM((2, FIELDS, PLANES) + TILE, jnp.float32),
            pltpu.SemaphoreType.DMA((2, FIELDS)),
        ],
        compiler_params=PARAMS,
    )(in_hbm(tiles))
    right = [(i + 1) % strips for i in range(strips)]
    left = [(i - 1) % strips for i in range(strips)]
    same = [(i, right[i]) for i in range(strips)]
    same += [(strips + i, strips + left[i]) for i in range(strips)]
    cross = [(i, strips + left[i]) for i in range(strips)]
    cross += [(strips + i, right[i]) for i in range(strips)]
    halo_own = lax.ppermute(far_copy, everyone, same)
    halo_sibling = lax.ppermute(own_copy, everyone, cross)
    swap = [(0, 1), (1, 0)]
    sib_far = lax.ppermute(own, "img", swap)
    sib_own = lax.ppermute(far, "img", swap)
    cost = pl.CostEstimate(flops=1_500_000, bytes_accessed=1_500_000, transcendentals=0)
    near_own = pl.pallas_call(
        own_kernel,
        out_shape=vmem(CELLS + PAD, *TILE),
        in_specs=[VMEM] * 3,
        out_specs=VMEM,
        compiler_params=PARAMS,
        cost_estimate=cost,
    )(*map(in_vmem, (own, far, halo_own)))
    far_sib = lax.ppermute(near_own, "img", swap)
    near_sib = pl.pallas_call(
        sibling_kernel,
        out_shape=vmem(CELLS + 1, *TILE),
        in_specs=[VMEM] * 4,
        out_specs=VMEM,
        compiler_params=PARAMS,
        cost_estimate=cost,
    )(*map(in_vmem, (sib_own, sib_far, halo_sibling, near_own)))
    far_own = lax.ppermute(near_sib, "img", swap)
    far_own, far_sib = lax.optimization_barrier((far_own, far_sib))
    parts = pl.pallas_call(
        add_kernel,
        out_shape=vmem(strips, 1, TILE[1]),
        in_specs=[VMEM] * 2,
        out_specs=VMEM,
        compiler_params=PARAMS,
    )(in_vmem(near_sib), in_vmem(far_own))
    parts = lax.all_to_all(parts, STRIP, 0, 0, tiled=True)
    parts = parts.reshape(-1, *TILE)
    new, knots = pl.pallas_call(
        combine_kernel,
        out_shape=(
            jax.ShapeDtypeStruct((2, FIELDS, PLANES) + TILE, jnp.float32),
            jax.ShapeDtypeStruct((4,), jnp.float32),
        ),
        in_specs=[VMEM] * 5,
        out_specs=(VMEM, pl.BlockSpec(memory_space=pltpu.SMEM)),
        compiler_params=PARAMS,
    )(*map(in_vmem, (parts, near_own, near_sib, far_own, far_sib)))
    new = new.reshape(2, FIELDS, PLANES, 4, 2, 128).transpose(0, 1, 2, 4, 3, 5)
    return new.reshape(2, FIELDS, PLANES, 2, 512), knots


def solution(mesh):
    fine = Mesh(mesh.devices.reshape(2, 8, 8, 4), ("img",) + STRIP)
    spec = P("img", None, None, STRIP, None)
    return jax.shard_map(
        per_device, mesh=fine, in_specs=(spec,), out_specs=(spec, P()), check_vma=False
    )
```

```python
import jax
import jax.numpy as jnp
from jax import lax
from jax.experimental import pallas as pl
from jax.experimental.pallas import tpu as pltpu
from jax.sharding import Mesh, PartitionSpec as P

KAPPA_PHASE = 1.0
KAPPA_SOLUTE = 0.6
BARRIER = 1.5
COUPLING = 2.0
TIME_STEP = 0.05
EQUILIBRIUM = ((0.8, 0.1), (0.1, 0.8), (0.1, 0.1), (0.45, 0.45))
STRIP = ("z", "y", "x")
FIELDS, PLANES = 6, 16
HALF = PLANES // 2
CELLS = 2 * FIELDS * HALF
PAD = 8
TILE = (8, 128)
VMEM = pl.BlockSpec(memory_space=pltpu.VMEM)
PARAMS = pltpu.CompilerParams(vmem_limit_bytes=48 * 1024 * 1024)


def cell(k, f, z):
    return (k * FIELDS + f) * HALF + z


def even_sublanes():
    return lax.broadcasted_iota(jnp.int32, TILE, 0) % 2 == 0


def pack_kernel(source, own, far, images, arrived):
    core = lax.axis_index("img")
    even = even_sublanes()
    first = jnp.full(TILE, core, jnp.int32) == 0

    def fetch(k, f):
        return pltpu.make_async_copy(source.at[k, f], images.at[k, f], arrived.at[k, f])

    for k in range(2):
        for f in range(FIELDS):
            fetch(k, f).start()

    def field(i, carry):
        k, f = i // FIELDS, i % FIELDS
        fetch(k, f).wait()
        for z in range(HALF):
            low, high = images[k, f, z], images[k, f, z + HALF]
            row0 = jnp.where(even, low, pltpu.roll(high, 1, 0))
            row1 = jnp.where(even, pltpu.roll(low, 7, 0), high)
            own[k, f, z] = jnp.where(first, row0, row1)
            far[k, f, z] = jnp.where(first, row1, row0)
        return carry

    lax.fori_loop(0, 2 * FIELDS, field, 0)


def step_image(center, beside, halo, j, stepped, g):
    even = even_sublanes()
    lane = lax.broadcasted_iota(jnp.int32, TILE, 1)
    at_first, at_last = lane == 0, lane == 127
    for z in range(HALF):
        cells, sums = [], []
        for f in range(FIELDS):
            c = center[j, f, z]
            if z < HALF - 1:
                raised = center[j, f, z + 1]
            else:
                raised = jnp.where(even, pltpu.roll(center[j, f, 0], 7, 0), c)
            if z > 0:
                lowered = center[j, f, z - 1]
            else:
                lowered = jnp.where(even, c, pltpu.roll(center[j, f, HALF - 1], 1, 0))
            ahead = pltpu.roll(c, 127, 1)
            ahead = jnp.where(at_last, pltpu.roll(ahead, 6, 0), ahead)
            behind = pltpu.roll(c, 1, 1)
            behind = jnp.where(at_first, pltpu.roll(behind, 2, 0), behind)
            around = (beside[j, f, z] + halo[j, f, z]) + (raised + lowered) + (ahead + behind)
            cells.append(c)
            sums.append(around)
        squares = [cells[i] * cells[i] for i in range(4)]
        total = (squares[0] + squares[1]) + (squares[2] + squares[3])
        pulls = []
        for s in range(2):
            value = cells[4 + s]
            for i in range(4):
                value = value - EQUILIBRIUM[i][s] * cells[i]
            pulls.append((TIME_STEP * COUPLING) * value)
        for i in range(4):
            gain = (1.0 - 6.0 * TIME_STEP * KAPPA_PHASE) - (TIME_STEP * 2.0 * BARRIER) * (
                total - squares[i]
            )
            out = gain * cells[i] + (TIME_STEP * KAPPA_PHASE) * sums[i]
            out = out + (EQUILIBRIUM[i][0] * pulls[0] + EQUILIBRIUM[i][1] * pulls[1])
            stepped[cell(g, i, z)] = out
        for s in range(2):
            out = (1.0 - 6.0 * TIME_STEP * KAPPA_SOLUTE) * cells[4 + s]
            out = out + (TIME_STEP * KAPPA_SOLUTE) * sums[4 + s] - pulls[s]
            stepped[cell(g, 4 + s, z)] = out


def own_kernel(own, far, halo, stepped):
    def one(j, carry):
        step_image(own, far, halo, j, stepped, j)
        return carry

    lax.fori_loop(0, 2, one, 0)
    for p in range(CELLS, stepped.shape[0]):
        stepped[p] = jnp.zeros(TILE, jnp.float32)


def sibling_kernel(own, far, halo, mine, stepped):
    core = lax.axis_index("img")

    def one(j, carry):
        step_image(own, far, halo, j, stepped, j)
        return carry

    lax.fori_loop(0, 2, one, 0)

    def gather(f, sums):
        pairs = (
            (mine, 1, mine, 0),
            (mine, 1 - core, stepped, core),
            (stepped, 1, stepped, 0),
        )
        new = []
        for total, (one, k, other, m) in zip(sums, pairs):
            terms = []
            for z in range(HALF):
                gap = one[cell(k, f, z)] - other[cell(m, f, z)]
                terms.append(gap * gap)
            while len(terms) > 1:
                terms = [a + b for a, b in zip(terms[::2], terms[1::2])]
            new.append(total + terms[0])
        return tuple(new)

    zero = jnp.zeros(TILE, jnp.float32)
    own_gap, cross_gap, other_gap = lax.fori_loop(0, FIELDS, gather, (zero, zero, zero))
    lane = lax.broadcasted_iota(jnp.int32, TILE, 1)
    out = jnp.where(lane == 2 * core, jnp.sum(own_gap), zero)
    out = jnp.where(lane == 1, jnp.sum(cross_gap), out)
    stepped[CELLS] = jnp.where(lane == 2 - 2 * core, jnp.sum(other_gap), out)


def add_kernel(near, rest, rows):
    total = near[CELLS, 0:1, :] + rest[CELLS, 0:1, :]

    def row(p, carry):
        rows[p] = total
        return carry

    lax.fori_loop(0, rows.shape[0], row, 0, unroll=16)


def total_tile(parts):
    terms = [parts[p] for p in range(parts.shape[0])]
    while len(terms) > 1:
        terms = [a + b for a, b in zip(terms[::2], terms[1::2])]
    return terms[0]


def combine_kernel(parts, near_own, near_sib, far_own, far_sib, new, knots):
    core = lax.axis_index("img")
    even = even_sublanes()
    first = jnp.full(TILE, core, jnp.int32) == 0
    total = total_tile(parts)
    lane = lax.broadcasted_iota(jnp.int32, TILE, 1)
    l1, l2, l3 = (
        jnp.sqrt(1.0 + jnp.full(TILE, jnp.sum(jnp.where(lane == k, total, 0.0))))
        for k in range(3)
    )
    whole = l1 + l2 + l3
    k1, k2, k3 = l1 / whole, (l1 + l2) / whole, whole / whole
    w0, w1, w2 = k1, k2 - k1, k3 - k2
    main1, main2 = 2.0 * (w0 + w1), 2.0 * (w1 + w2)
    det = main1 * main2 - w1 * w1
    scale = 6.0 / det
    i0, i1, i2 = 1.0 / w0, 1.0 / w1, 1.0 / w2
    bend1 = (
        -main2 * i0 * scale,
        (main2 + w1) * i1 * scale,
        -w1 * i2 * scale,
    )
    bend2 = (
        w1 * i0 * scale,
        -(main1 + w1) * i1 * scale,
        main1 * i2 * scale,
    )
    zero = jnp.zeros(TILE, jnp.float32)
    values, gaps = [], []
    for j in range(2):
        target = jnp.where(first, jnp.float32(j / 3.0), jnp.float32((j + 2) / 3.0))
        below = 1 + sum((k <= target).astype(jnp.int32) for k in (k1, k2, k3)) - 1
        at = jnp.clip(below, 0, 2)
        h = jnp.where(at == 0, w0, jnp.where(at == 1, w1, w2))
        right = jnp.where(at == 0, k1, jnp.where(at == 1, k2, k3))
        a = (right - target) / h
        b = 1.0 - a
        curve = h * h * (1.0 / 6.0)
        ca, cb = (a * a * a - a) * curve, (b * b * b - b) * curve
        v = [jnp.where(at == k, a, jnp.where(at == k - 1, b, zero)) for k in range(4)]
        c1 = jnp.where(at == 1, ca, jnp.where(at == 0, cb, zero))
        c2 = jnp.where(at == 2, ca, jnp.where(at == 1, cb, zero))
        values.append(v)
        gaps.append([c1 * bend1[m] + c2 * bend2[m] for m in range(3)])
    knots[0] = jnp.float32(0.0)
    knots[1] = k1[0, 0]
    knots[2] = k2[0, 0]
    knots[3] = k3[0, 0]

    def resampled(rows, f, z):
        s = [rows[k // 2][cell(k % 2, f, z)] for k in range(4)]
        d = [s[k + 1] - s[k] for k in range(3)]
        out = []
        for j in range(2):
            v, e = values[j], gaps[j]
            straight = (v[0] * s[0] + v[1] * s[1]) + (v[2] * s[2] + v[3] * s[3])
            out.append(straight + (e[0] * d[0] + e[1] * d[1] + e[2] * d[2]))
        return out

    def write(even_rows, odd_rows):
        def field(f, carry):
            for z in range(HALF):
                row0, row1 = resampled(even_rows, f, z), resampled(odd_rows, f, z)
                for j in range(2):
                    new[j, f, z] = jnp.where(even, row0[j], pltpu.roll(row1[j], 1, 0))
                    new[j, f, z + HALF] = jnp.where(even, pltpu.roll(row0[j], 7, 0), row1[j])
            return carry

        lax.fori_loop(0, FIELDS, field, 0)

    @pl.when(core == 0)
    def _():
        write((near_own, near_sib), (far_own, far_sib))

    @pl.when(core == 1)
    def _():
        write((far_sib, far_own), (near_sib, near_own))


def in_hbm(x):
    return pltpu.with_memory_space_constraint(x, pltpu.HBM)


def in_vmem(x):
    return pltpu.with_memory_space_constraint(x, pltpu.VMEM)


def vmem(*shape):
    return pltpu.VMEM(shape, jnp.float32)


def per_device(images):
    everyone = ("img",) + STRIP
    strips = lax.axis_size(STRIP)
    tiles = images.reshape(2, FIELDS, PLANES, 2, 4, 128).transpose(0, 1, 2, 4, 3, 5)
    tiles = tiles.reshape(2, FIELDS, PLANES, *TILE)
    packed = (2, FIELDS, HALF) + TILE
    own, far = pl.pallas_call(
        pack_kernel,
        out_shape=(vmem(*packed),) * 2,
        in_specs=[pl.BlockSpec(memory_space=pl.ANY)],
        out_specs=(VMEM,) * 2,
        scratch_shapes=[
            pltpu.VMEM((2, FIELDS, PLANES) + TILE, jnp.float32),
            pltpu.SemaphoreType.DMA((2, FIELDS)),
        ],
        compiler_params=PARAMS,
    )(in_hbm(tiles))
    right = [(i + 1) % strips for i in range(strips)]
    left = [(i - 1) % strips for i in range(strips)]
    same = [(i, right[i]) for i in range(strips)]
    same += [(strips + i, strips + left[i]) for i in range(strips)]
    cross = [(i, strips + left[i]) for i in range(strips)]
    cross += [(strips + i, right[i]) for i in range(strips)]
    halo_own = lax.ppermute(far, everyone, same)
    halo_sibling = lax.ppermute(own, everyone, cross)
    swap = [(0, 1), (1, 0)]
    sib_far = lax.ppermute(own, "img", swap)
    sib_own = lax.ppermute(far, "img", swap)
    cost = pl.CostEstimate(flops=1_500_000, bytes_accessed=1_500_000, transcendentals=0)
    near_own = pl.pallas_call(
        own_kernel,
        out_shape=vmem(CELLS + PAD, *TILE),
        in_specs=[VMEM] * 3,
        out_specs=VMEM,
        compiler_params=PARAMS,
        cost_estimate=cost,
    )(*map(in_vmem, (own, far, halo_own)))
    far_sib = lax.ppermute(near_own, "img", swap)
    near_sib = pl.pallas_call(
        sibling_kernel,
        out_shape=vmem(CELLS + 1, *TILE),
        in_specs=[VMEM] * 4,
        out_specs=VMEM,
        compiler_params=PARAMS,
        cost_estimate=cost,
    )(*map(in_vmem, (sib_own, sib_far, halo_sibling, near_own)))
    far_own = lax.ppermute(near_sib, "img", swap)
    far_own, far_sib = lax.optimization_barrier((far_own, far_sib))
    parts = pl.pallas_call(
        add_kernel,
        out_shape=vmem(strips, 1, TILE[1]),
        in_specs=[VMEM] * 2,
        out_specs=VMEM,
        compiler_params=PARAMS,
    )(in_vmem(near_sib), in_vmem(far_own))
    parts = lax.all_to_all(parts, STRIP, 0, 0, tiled=True)
    parts = parts.reshape(-1, *TILE)
    new, knots = pl.pallas_call(
        combine_kernel,
        out_shape=(
            jax.ShapeDtypeStruct((2, FIELDS, PLANES) + TILE, jnp.float32),
            jax.ShapeDtypeStruct((4,), jnp.float32),
        ),
        in_specs=[VMEM] * 5,
        out_specs=(VMEM, pl.BlockSpec(memory_space=pltpu.SMEM)),
        compiler_params=PARAMS,
    )(*map(in_vmem, (parts, near_own, near_sib, far_own, far_sib)))
    new = new.reshape(2, FIELDS, PLANES, 4, 2, 128).transpose(0, 1, 2, 4, 3, 5)
    return new.reshape(2, FIELDS, PLANES, 2, 512), knots


def solution(mesh):
    fine = Mesh(mesh.devices.reshape(2, 8, 8, 4), ("img",) + STRIP)
    spec = P("img", None, None, STRIP, None)
    return jax.shard_map(
        per_device, mesh=fine, in_specs=(spec,), out_specs=(spec, P()), check_vma=False
    )
```

```python
import jax
import jax.numpy as jnp
from jax import lax
from jax.experimental import pallas as pl
from jax.experimental.pallas import tpu as pltpu
from jax.sharding import Mesh, PartitionSpec as P

KAPPA_PHASE = 1.0
KAPPA_SOLUTE = 0.6
BARRIER = 1.5
COUPLING = 2.0
TIME_STEP = 0.05
EQUILIBRIUM = ((0.8, 0.1), (0.1, 0.8), (0.1, 0.1), (0.45, 0.45))
STRIP = ("z", "y", "x")
FIELDS, PLANES = 6, 16
HALF = PLANES // 2
PART = FIELDS // 2
CELLS = 2 * FIELDS * HALF
PAD = 8
TILE = (8, 128)
VMEM = pl.BlockSpec(memory_space=pltpu.VMEM)
PARAMS = pltpu.CompilerParams(vmem_limit_bytes=48 * 1024 * 1024)


def cell(k, f, z):
    return (k * FIELDS + f) * HALF + z


def even_sublanes():
    return lax.broadcasted_iota(jnp.int32, TILE, 0) % 2 == 0


def pack_kernel(source, own, far, far_copy, own_copy, images, arrived):
    core = lax.axis_index("img")
    even = even_sublanes()
    first = jnp.full(TILE, core, jnp.int32) == 0

    def fetch(k, half):
        part = (k, pl.ds(half * PART, PART))
        return pltpu.make_async_copy(source.at[part], images.at[part], arrived.at[k, half])

    for k in range(2):
        for half in range(2):
            fetch(k, half).start()

    def field(i, carry):
        k, f = i // FIELDS, i % FIELDS

        @pl.when(f % PART == 0)
        def _():
            fetch(k, f // PART).wait()

        for z in range(HALF):
            low, high = images[k, f, z], images[k, f, z + HALF]
            row0 = jnp.where(even, low, pltpu.roll(high, 1, 0))
            row1 = jnp.where(even, pltpu.roll(low, 7, 0), high)
            mine = jnp.where(first, row0, row1)
            rest = jnp.where(first, row1, row0)
            own[k, f, z] = mine
            far[k, f, z] = rest
            own_copy[k, f, z] = mine
            far_copy[k, f, z] = rest
        return carry

    lax.fori_loop(0, 2 * FIELDS, field, 0)


def step_image(center, beside, halo, j, stepped, g):
    even = even_sublanes()
    lane = lax.broadcasted_iota(jnp.int32, TILE, 1)
    at_first, at_last = lane == 0, lane == 127
    for z in range(HALF):
        cells, sums = [], []
        for f in range(FIELDS):
            c = center[j, f, z]
            if z < HALF - 1:
                raised = center[j, f, z + 1]
            else:
                raised = jnp.where(even, pltpu.roll(center[j, f, 0], 7, 0), c)
            if z > 0:
                lowered = center[j, f, z - 1]
            else:
                lowered = jnp.where(even, c, pltpu.roll(center[j, f, HALF - 1], 1, 0))
            ahead = pltpu.roll(c, 127, 1)
            ahead = jnp.where(at_last, pltpu.roll(ahead, 6, 0), ahead)
            behind = pltpu.roll(c, 1, 1)
            behind = jnp.where(at_first, pltpu.roll(behind, 2, 0), behind)
            around = (beside[j, f, z] + halo[j, f, z]) + (raised + lowered) + (ahead + behind)
            cells.append(c)
            sums.append(around)
        squares = [cells[i] * cells[i] for i in range(4)]
        total = (squares[0] + squares[1]) + (squares[2] + squares[3])
        pulls = []
        for s in range(2):
            value = cells[4 + s]
            for i in range(4):
                value = value - EQUILIBRIUM[i][s] * cells[i]
            pulls.append((TIME_STEP * COUPLING) * value)
        for i in range(4):
            gain = (1.0 - 6.0 * TIME_STEP * KAPPA_PHASE) - (TIME_STEP * 2.0 * BARRIER) * (
                total - squares[i]
            )
            out = gain * cells[i] + (TIME_STEP * KAPPA_PHASE) * sums[i]
            out = out + (EQUILIBRIUM[i][0] * pulls[0] + EQUILIBRIUM[i][1] * pulls[1])
            stepped[cell(g, i, z)] = out
        for s in range(2):
            out = (1.0 - 6.0 * TIME_STEP * KAPPA_SOLUTE) * cells[4 + s]
            out = out + (TIME_STEP * KAPPA_SOLUTE) * sums[4 + s] - pulls[s]
            stepped[cell(g, 4 + s, z)] = out


def own_kernel(own, far, halo, stepped):
    def one(j, carry):
        step_image(own, far, halo, j, stepped, j)
        return carry

    lax.fori_loop(0, 2, one, 0)
    for p in range(CELLS, stepped.shape[0]):
        stepped[p] = jnp.zeros(TILE, jnp.float32)


def sibling_kernel(own, far, halo, mine, stepped):
    core = lax.axis_index("img")

    def one(j, carry):
        step_image(own, far, halo, j, stepped, j)
        return carry

    lax.fori_loop(0, 2, one, 0)

    def gather(f, sums):
        pairs = (
            (mine, 1, mine, 0),
            (mine, 1 - core, stepped, core),
            (stepped, 1, stepped, 0),
        )
        new = []
        for total, (one, k, other, m) in zip(sums, pairs):
            terms = []
            for z in range(HALF):
                gap = one[cell(k, f, z)] - other[cell(m, f, z)]
                terms.append(gap * gap)
            while len(terms) > 1:
                terms = [a + b for a, b in zip(terms[::2], terms[1::2])]
            new.append(total + terms[0])
        return tuple(new)

    zero = jnp.zeros(TILE, jnp.float32)
    own_gap, cross_gap, other_gap = lax.fori_loop(0, FIELDS, gather, (zero, zero, zero))
    lane = lax.broadcasted_iota(jnp.int32, TILE, 1)
    out = jnp.where(lane == 2 * core, jnp.sum(own_gap), zero)
    out = jnp.where(lane == 1, jnp.sum(cross_gap), out)
    stepped[CELLS] = jnp.where(lane == 2 - 2 * core, jnp.sum(other_gap), out)


def add_kernel(near, rest, rows):
    total = near[CELLS, 0:1, :] + rest[CELLS, 0:1, :]

    def row(p, carry):
        rows[p] = total
        return carry

    lax.fori_loop(0, rows.shape[0], row, 0, unroll=16)


def total_tile(parts):
    terms = [parts[p] for p in range(parts.shape[0])]
    while len(terms) > 1:
        terms = [a + b for a, b in zip(terms[::2], terms[1::2])]
    return terms[0]


def combine_kernel(parts, near_own, near_sib, far_own, far_sib, new, knots):
    core = lax.axis_index("img")
    even = even_sublanes()
    first = jnp.full(TILE, core, jnp.int32) == 0
    total = total_tile(parts)
    lane = lax.broadcasted_iota(jnp.int32, TILE, 1)
    l1, l2, l3 = (
        jnp.sqrt(1.0 + jnp.full(TILE, jnp.sum(jnp.where(lane == k, total, 0.0))))
        for k in range(3)
    )
    whole = l1 + l2 + l3
    k1, k2, k3 = l1 / whole, (l1 + l2) / whole, whole / whole
    w0, w1, w2 = k1, k2 - k1, k3 - k2
    main1, main2 = 2.0 * (w0 + w1), 2.0 * (w1 + w2)
    det = main1 * main2 - w1 * w1
    scale = 6.0 / det
    i0, i1, i2 = 1.0 / w0, 1.0 / w1, 1.0 / w2
    bend1 = (
        -main2 * i0 * scale,
        (main2 + w1) * i1 * scale,
        -w1 * i2 * scale,
    )
    bend2 = (
        w1 * i0 * scale,
        -(main1 + w1) * i1 * scale,
        main1 * i2 * scale,
    )
    zero = jnp.zeros(TILE, jnp.float32)
    gaps = []
    for j in range(2):
        target = jnp.where(first, jnp.float32(j / 3.0), jnp.float32((j + 2) / 3.0))
        below = 1 + sum((k <= target).astype(jnp.int32) for k in (k1, k2, k3)) - 1
        at = jnp.clip(below, 0, 2)
        h = jnp.where(at == 0, w0, jnp.where(at == 1, w1, w2))
        right = jnp.where(at == 0, k1, jnp.where(at == 1, k2, k3))
        a = (right - target) / h
        b = 1.0 - a
        curve = h * h * (1.0 / 6.0)
        ca, cb = (a * a * a - a) * curve, (b * b * b - b) * curve
        v = [jnp.where(at == k, a, jnp.where(at == k - 1, b, zero)) for k in range(4)]
        c1 = jnp.where(at == 1, ca, jnp.where(at == 0, cb, zero))
        c2 = jnp.where(at == 2, ca, jnp.where(at == 1, cb, zero))
        above = (v[1] + v[2] + v[3], v[2] + v[3], v[3])
        gaps.append([above[m] + (c1 * bend1[m] + c2 * bend2[m]) for m in range(3)])
    knots[0] = jnp.float32(0.0)
    knots[1] = k1[0, 0]
    knots[2] = k2[0, 0]
    knots[3] = k3[0, 0]

    def resampled(rows, f, z):
        s = [rows[k // 2][cell(k % 2, f, z)] for k in range(4)]
        d = [s[k + 1] - s[k] for k in range(3)]
        out = []
        for j in range(2):
            g = gaps[j]
            out.append((s[0] + g[0] * d[0]) + (g[1] * d[1] + g[2] * d[2]))
        return out

    def write(even_rows, odd_rows):
        def field(f, carry):
            for z in range(HALF):
                row0, row1 = resampled(even_rows, f, z), resampled(odd_rows, f, z)
                for j in range(2):
                    new[j, f, z] = jnp.where(even, row0[j], pltpu.roll(row1[j], 1, 0))
                    new[j, f, z + HALF] = jnp.where(even, pltpu.roll(row0[j], 7, 0), row1[j])
            return carry

        lax.fori_loop(0, FIELDS, field, 0)

    @pl.when(core == 0)
    def _():
        write((near_own, near_sib), (far_own, far_sib))

    @pl.when(core == 1)
    def _():
        write((far_sib, far_own), (near_sib, near_own))


def in_hbm(x):
    return pltpu.with_memory_space_constraint(x, pltpu.HBM)


def in_vmem(x):
    return pltpu.with_memory_space_constraint(x, pltpu.VMEM)


def vmem(*shape):
    return pltpu.VMEM(shape, jnp.float32)


def per_device(images):
    everyone = ("img",) + STRIP
    strips = lax.axis_size(STRIP)
    tiles = images.reshape(2, FIELDS, PLANES, 2, 4, 128).transpose(0, 1, 2, 4, 3, 5)
    tiles = tiles.reshape(2, FIELDS, PLANES, *TILE)
    packed = (2, FIELDS, HALF) + TILE
    own, far, far_copy, own_copy = pl.pallas_call(
        pack_kernel,
        out_shape=(vmem(*packed),) * 4,
        in_specs=[pl.BlockSpec(memory_space=pl.ANY)],
        out_specs=(VMEM,) * 4,
        scratch_shapes=[
            pltpu.VMEM((2, FIELDS, PLANES) + TILE, jnp.float32),
            pltpu.SemaphoreType.DMA((2, 2)),
        ],
        compiler_params=PARAMS,
    )(in_hbm(tiles))
    right = [(i + 1) % strips for i in range(strips)]
    left = [(i - 1) % strips for i in range(strips)]
    same = [(i, right[i]) for i in range(strips)]
    same += [(strips + i, strips + left[i]) for i in range(strips)]
    cross = [(i, strips + left[i]) for i in range(strips)]
    cross += [(strips + i, right[i]) for i in range(strips)]
    halo_own = lax.ppermute(far_copy, everyone, same)
    halo_sibling = lax.ppermute(own_copy, everyone, cross)
    swap = [(0, 1), (1, 0)]
    sib_far = lax.ppermute(own, "img", swap)
    sib_own = lax.ppermute(far, "img", swap)
    cost = pl.CostEstimate(flops=1_500_000, bytes_accessed=1_500_000, transcendentals=0)
    near_own = pl.pallas_call(
        own_kernel,
        out_shape=vmem(CELLS + PAD, *TILE),
        in_specs=[VMEM] * 3,
        out_specs=VMEM,
        compiler_params=PARAMS,
        cost_estimate=cost,
    )(*map(in_vmem, (own, far, halo_own)))
    far_sib = lax.ppermute(near_own, "img", swap)
    near_sib = pl.pallas_call(
        sibling_kernel,
        out_shape=vmem(CELLS + 1, *TILE),
        in_specs=[VMEM] * 4,
        out_specs=VMEM,
        compiler_params=PARAMS,
        cost_estimate=cost,
    )(*map(in_vmem, (sib_own, sib_far, halo_sibling, near_own)))
    far_own = lax.ppermute(near_sib, "img", swap)
    far_own, far_sib = lax.optimization_barrier((far_own, far_sib))
    parts = pl.pallas_call(
        add_kernel,
        out_shape=vmem(strips, 1, TILE[1]),
        in_specs=[VMEM] * 2,
        out_specs=VMEM,
        compiler_params=PARAMS,
    )(in_vmem(near_sib), in_vmem(far_own))
    parts = lax.all_to_all(parts, STRIP, 0, 0, tiled=True)
    parts = parts.reshape(-1, *TILE)
    new, knots = pl.pallas_call(
        combine_kernel,
        out_shape=(
            jax.ShapeDtypeStruct((2, FIELDS, PLANES) + TILE, jnp.float32),
            jax.ShapeDtypeStruct((4,), jnp.float32),
        ),
        in_specs=[VMEM] * 5,
        out_specs=(VMEM, pl.BlockSpec(memory_space=pltpu.SMEM)),
        compiler_params=PARAMS,
    )(*map(in_vmem, (parts, near_own, near_sib, far_own, far_sib)))
    new = new.reshape(2, FIELDS, PLANES, 4, 2, 128).transpose(0, 1, 2, 4, 3, 5)
    return new.reshape(2, FIELDS, PLANES, 2, 512), knots


def solution(mesh):
    fine = Mesh(mesh.devices.reshape(2, 8, 8, 4), ("img",) + STRIP)
    spec = P("img", None, None, STRIP, None)
    return jax.shard_map(
        per_device, mesh=fine, in_specs=(spec,), out_specs=(spec, P()), check_vma=False
    )
```

```python
import jax
import jax.numpy as jnp
from jax import lax
from jax.experimental import pallas as pl
from jax.experimental.pallas import tpu as pltpu
from jax.sharding import Mesh, PartitionSpec as P

KAPPA_PHASE = 1.0
KAPPA_SOLUTE = 0.6
BARRIER = 1.5
COUPLING = 2.0
TIME_STEP = 0.05
EQUILIBRIUM = ((0.8, 0.1), (0.1, 0.8), (0.1, 0.1), (0.45, 0.45))
STRIP = ("z", "y", "x")
FIELDS, PLANES = 6, 16
HALF = PLANES // 2
PART = 1
CELLS = 2 * FIELDS * HALF
PAD = 8
TILE = (8, 128)
VMEM = pl.BlockSpec(memory_space=pltpu.VMEM)
PARAMS = pltpu.CompilerParams(vmem_limit_bytes=48 * 1024 * 1024)


def cell(k, f, z):
    return (k * FIELDS + f) * HALF + z


def even_sublanes():
    return lax.broadcasted_iota(jnp.int32, TILE, 0) % 2 == 0


def pack_kernel(source, own, far, far_copy, own_copy, images, arrived):
    core = lax.axis_index("img")
    even = even_sublanes()
    first = jnp.full(TILE, core, jnp.int32) == 0

    def fetch(k, half):
        part = (k, pl.ds(half * PART, PART))
        return pltpu.make_async_copy(source.at[part], images.at[part], arrived.at[k, half])

    for k in range(2):
        for half in range(FIELDS // PART):
            fetch(k, half).start()

    def field(i, carry):
        k, f = i // FIELDS, i % FIELDS

        @pl.when(f % PART == 0)
        def _():
            fetch(k, f // PART).wait()

        for z in range(HALF):
            low, high = images[k, f, z], images[k, f, z + HALF]
            row0 = jnp.where(even, low, pltpu.roll(high, 1, 0))
            row1 = jnp.where(even, pltpu.roll(low, 7, 0), high)
            mine = jnp.where(first, row0, row1)
            rest = jnp.where(first, row1, row0)
            own[k, f, z] = mine
            far[k, f, z] = rest
            own_copy[k, f, z] = mine
            far_copy[k, f, z] = rest
        return carry

    lax.fori_loop(0, 2 * FIELDS, field, 0)


def step_image(center, beside, halo, j, stepped, g):
    even = even_sublanes()
    lane = lax.broadcasted_iota(jnp.int32, TILE, 1)
    at_first, at_last = lane == 0, lane == 127
    for z in range(HALF):
        cells, sums = [], []
        for f in range(FIELDS):
            c = center[j, f, z]
            if z < HALF - 1:
                raised = center[j, f, z + 1]
            else:
                raised = jnp.where(even, pltpu.roll(center[j, f, 0], 7, 0), c)
            if z > 0:
                lowered = center[j, f, z - 1]
            else:
                lowered = jnp.where(even, c, pltpu.roll(center[j, f, HALF - 1], 1, 0))
            ahead = pltpu.roll(c, 127, 1)
            ahead = jnp.where(at_last, pltpu.roll(ahead, 6, 0), ahead)
            behind = pltpu.roll(c, 1, 1)
            behind = jnp.where(at_first, pltpu.roll(behind, 2, 0), behind)
            around = (beside[j, f, z] + halo[j, f, z]) + (raised + lowered) + (ahead + behind)
            cells.append(c)
            sums.append(around)
        squares = [cells[i] * cells[i] for i in range(4)]
        total = (squares[0] + squares[1]) + (squares[2] + squares[3])
        pulls = []
        for s in range(2):
            value = cells[4 + s]
            for i in range(4):
                value = value - EQUILIBRIUM[i][s] * cells[i]
            pulls.append((TIME_STEP * COUPLING) * value)
        for i in range(4):
            gain = (1.0 - 6.0 * TIME_STEP * KAPPA_PHASE) - (TIME_STEP * 2.0 * BARRIER) * (
                total - squares[i]
            )
            out = gain * cells[i] + (TIME_STEP * KAPPA_PHASE) * sums[i]
            out = out + (EQUILIBRIUM[i][0] * pulls[0] + EQUILIBRIUM[i][1] * pulls[1])
            stepped[cell(g, i, z)] = out
        for s in range(2):
            out = (1.0 - 6.0 * TIME_STEP * KAPPA_SOLUTE) * cells[4 + s]
            out = out + (TIME_STEP * KAPPA_SOLUTE) * sums[4 + s] - pulls[s]
            stepped[cell(g, 4 + s, z)] = out


def own_kernel(own, far, halo, stepped):
    def one(j, carry):
        step_image(own, far, halo, j, stepped, j)
        return carry

    lax.fori_loop(0, 2, one, 0)
    for p in range(CELLS, stepped.shape[0]):
        stepped[p] = jnp.zeros(TILE, jnp.float32)


def sibling_kernel(own, far, halo, mine, stepped):
    core = lax.axis_index("img")

    def one(j, carry):
        step_image(own, far, halo, j, stepped, j)
        return carry

    lax.fori_loop(0, 2, one, 0)

    def gather(f, sums):
        pairs = (
            (mine, 1, mine, 0),
            (mine, 1 - core, stepped, core),
            (stepped, 1, stepped, 0),
        )
        new = []
        for total, (one, k, other, m) in zip(sums, pairs):
            terms = []
            for z in range(HALF):
                gap = one[cell(k, f, z)] - other[cell(m, f, z)]
                terms.append(gap * gap)
            while len(terms) > 1:
                terms = [a + b for a, b in zip(terms[::2], terms[1::2])]
            new.append(total + terms[0])
        return tuple(new)

    zero = jnp.zeros(TILE, jnp.float32)
    own_gap, cross_gap, other_gap = lax.fori_loop(0, FIELDS, gather, (zero, zero, zero))
    lane = lax.broadcasted_iota(jnp.int32, TILE, 1)
    out = jnp.where(lane == 2 * core, jnp.sum(own_gap), zero)
    out = jnp.where(lane == 1, jnp.sum(cross_gap), out)
    stepped[CELLS] = jnp.where(lane == 2 - 2 * core, jnp.sum(other_gap), out)


def add_kernel(near, rest, rows):
    total = near[CELLS, 0:1, :] + rest[CELLS, 0:1, :]

    def row(p, carry):
        rows[p] = total
        return carry

    lax.fori_loop(0, rows.shape[0], row, 0, unroll=16)


def total_tile(parts):
    terms = [parts[p] for p in range(parts.shape[0])]
    while len(terms) > 1:
        terms = [a + b for a, b in zip(terms[::2], terms[1::2])]
    return terms[0]


def combine_kernel(parts, near_own, near_sib, far_own, far_sib, new, knots):
    core = lax.axis_index("img")
    even = even_sublanes()
    first = jnp.full(TILE, core, jnp.int32) == 0
    total = total_tile(parts)
    lane = lax.broadcasted_iota(jnp.int32, TILE, 1)
    l1, l2, l3 = (
        jnp.sqrt(1.0 + jnp.full(TILE, jnp.sum(jnp.where(lane == k, total, 0.0))))
        for k in range(3)
    )
    whole = l1 + l2 + l3
    k1, k2, k3 = l1 / whole, (l1 + l2) / whole, whole / whole
    w0, w1, w2 = k1, k2 - k1, k3 - k2
    main1, main2 = 2.0 * (w0 + w1), 2.0 * (w1 + w2)
    det = main1 * main2 - w1 * w1
    scale = 6.0 / det
    i0, i1, i2 = 1.0 / w0, 1.0 / w1, 1.0 / w2
    bend1 = (
        -main2 * i0 * scale,
        (main2 + w1) * i1 * scale,
        -w1 * i2 * scale,
    )
    bend2 = (
        w1 * i0 * scale,
        -(main1 + w1) * i1 * scale,
        main1 * i2 * scale,
    )
    zero = jnp.zeros(TILE, jnp.float32)
    gaps = []
    for j in range(2):
        target = jnp.where(first, jnp.float32(j / 3.0), jnp.float32((j + 2) / 3.0))
        below = 1 + sum((k <= target).astype(jnp.int32) for k in (k1, k2, k3)) - 1
        at = jnp.clip(below, 0, 2)
        h = jnp.where(at == 0, w0, jnp.where(at == 1, w1, w2))
        right = jnp.where(at == 0, k1, jnp.where(at == 1, k2, k3))
        a = (right - target) / h
        b = 1.0 - a
        curve = h * h * (1.0 / 6.0)
        ca, cb = (a * a * a - a) * curve, (b * b * b - b) * curve
        v = [jnp.where(at == k, a, jnp.where(at == k - 1, b, zero)) for k in range(4)]
        c1 = jnp.where(at == 1, ca, jnp.where(at == 0, cb, zero))
        c2 = jnp.where(at == 2, ca, jnp.where(at == 1, cb, zero))
        above = (v[1] + v[2] + v[3], v[2] + v[3], v[3])
        gaps.append([above[m] + (c1 * bend1[m] + c2 * bend2[m]) for m in range(3)])
    knots[0] = jnp.float32(0.0)
    knots[1] = k1[0, 0]
    knots[2] = k2[0, 0]
    knots[3] = k3[0, 0]

    def resampled(rows, f, z):
        s = [rows[k // 2][cell(k % 2, f, z)] for k in range(4)]
        d = [s[k + 1] - s[k] for k in range(3)]
        out = []
        for j in range(2):
            g = gaps[j]
            out.append((s[0] + g[0] * d[0]) + (g[1] * d[1] + g[2] * d[2]))
        return out

    def write(even_rows, odd_rows):
        def field(f, carry):
            for z in range(HALF):
                row0, row1 = resampled(even_rows, f, z), resampled(odd_rows, f, z)
                for j in range(2):
                    new[j, f, z] = jnp.where(even, row0[j], pltpu.roll(row1[j], 1, 0))
                    new[j, f, z + HALF] = jnp.where(even, pltpu.roll(row0[j], 7, 0), row1[j])
            return carry

        lax.fori_loop(0, FIELDS, field, 0)

    @pl.when(core == 0)
    def _():
        write((near_own, near_sib), (far_own, far_sib))

    @pl.when(core == 1)
    def _():
        write((far_sib, far_own), (near_sib, near_own))


def in_hbm(x):
    return pltpu.with_memory_space_constraint(x, pltpu.HBM)


def in_vmem(x):
    return pltpu.with_memory_space_constraint(x, pltpu.VMEM)


def vmem(*shape):
    return pltpu.VMEM(shape, jnp.float32)


def per_device(images):
    everyone = ("img",) + STRIP
    strips = lax.axis_size(STRIP)
    tiles = images.reshape(2, FIELDS, PLANES, 2, 4, 128).transpose(0, 1, 2, 4, 3, 5)
    tiles = tiles.reshape(2, FIELDS, PLANES, *TILE)
    packed = (2, FIELDS, HALF) + TILE
    own, far, far_copy, own_copy = pl.pallas_call(
        pack_kernel,
        out_shape=(vmem(*packed),) * 4,
        in_specs=[pl.BlockSpec(memory_space=pl.ANY)],
        out_specs=(VMEM,) * 4,
        scratch_shapes=[
            pltpu.VMEM((2, FIELDS, PLANES) + TILE, jnp.float32),
            pltpu.SemaphoreType.DMA((2, FIELDS // PART)),
        ],
        compiler_params=PARAMS,
    )(in_hbm(tiles))
    right = [(i + 1) % strips for i in range(strips)]
    left = [(i - 1) % strips for i in range(strips)]
    same = [(i, right[i]) for i in range(strips)]
    same += [(strips + i, strips + left[i]) for i in range(strips)]
    cross = [(i, strips + left[i]) for i in range(strips)]
    cross += [(strips + i, right[i]) for i in range(strips)]
    halo_own = lax.ppermute(far_copy, everyone, same)
    halo_sibling = lax.ppermute(own_copy, everyone, cross)
    swap = [(0, 1), (1, 0)]
    sib_far = lax.ppermute(own, "img", swap)
    sib_own = lax.ppermute(far, "img", swap)
    cost = pl.CostEstimate(flops=1_500_000, bytes_accessed=1_500_000, transcendentals=0)
    near_own = pl.pallas_call(
        own_kernel,
        out_shape=vmem(CELLS + PAD, *TILE),
        in_specs=[VMEM] * 3,
        out_specs=VMEM,
        compiler_params=PARAMS,
        cost_estimate=cost,
    )(*map(in_vmem, (own, far, halo_own)))
    far_sib = lax.ppermute(near_own, "img", swap)
    near_sib = pl.pallas_call(
        sibling_kernel,
        out_shape=vmem(CELLS + 1, *TILE),
        in_specs=[VMEM] * 4,
        out_specs=VMEM,
        compiler_params=PARAMS,
        cost_estimate=cost,
    )(*map(in_vmem, (sib_own, sib_far, halo_sibling, near_own)))
    far_own = lax.ppermute(near_sib, "img", swap)
    far_own, far_sib = lax.optimization_barrier((far_own, far_sib))
    parts = pl.pallas_call(
        add_kernel,
        out_shape=vmem(strips, 1, TILE[1]),
        in_specs=[VMEM] * 2,
        out_specs=VMEM,
        compiler_params=PARAMS,
    )(in_vmem(near_sib), in_vmem(far_own))
    parts = lax.all_to_all(parts, STRIP[::-1], 0, 0, tiled=True)
    parts = parts.reshape(-1, *TILE)
    new, knots = pl.pallas_call(
        combine_kernel,
        out_shape=(
            jax.ShapeDtypeStruct((2, FIELDS, PLANES) + TILE, jnp.float32),
            jax.ShapeDtypeStruct((4,), jnp.float32),
        ),
        in_specs=[VMEM] * 5,
        out_specs=(VMEM, pl.BlockSpec(memory_space=pltpu.SMEM)),
        compiler_params=PARAMS,
    )(*map(in_vmem, (parts, near_own, near_sib, far_own, far_sib)))
    new = new.reshape(2, FIELDS, PLANES, 4, 2, 128).transpose(0, 1, 2, 4, 3, 5)
    return new.reshape(2, FIELDS, PLANES, 2, 512), knots


def solution(mesh):
    fine = Mesh(mesh.devices.reshape(2, 8, 8, 4), ("img",) + STRIP)
    spec = P("img", None, None, STRIP, None)
    return jax.shard_map(
        per_device, mesh=fine, in_specs=(spec,), out_specs=(spec, P()), check_vma=False
    )
```

```python
import jax
import jax.numpy as jnp
from jax import lax
from jax.experimental import pallas as pl
from jax.experimental.pallas import tpu as pltpu
from jax.sharding import Mesh, PartitionSpec as P

KAPPA_PHASE = 1.0
KAPPA_SOLUTE = 0.6
BARRIER = 1.5
COUPLING = 2.0
TIME_STEP = 0.05
EQUILIBRIUM = ((0.8, 0.1), (0.1, 0.8), (0.1, 0.1), (0.45, 0.45))
STRIP = ("z", "y", "x")
FIELDS, PLANES = 6, 16
HALF = PLANES // 2
PART = 1
CELLS = 2 * FIELDS * HALF
PAD = 8
TILE = (8, 128)
VMEM = pl.BlockSpec(memory_space=pltpu.VMEM)
PARAMS = pltpu.CompilerParams(vmem_limit_bytes=48 * 1024 * 1024)


def cell(k, f, z):
    return (k * FIELDS + f) * HALF + z


def even_sublanes():
    return lax.broadcasted_iota(jnp.int32, TILE, 0) % 2 == 0


def pack_kernel(source, own, far, far_copy, own_copy, images, arrived):
    core = lax.axis_index("img")
    even = even_sublanes()
    first = jnp.full(TILE, core, jnp.int32) == 0

    def fetch(k, half):
        part = (k, pl.ds(half * PART, PART))
        return pltpu.make_async_copy(source.at[part], images.at[part], arrived.at[k, half])

    for k in range(2):
        for half in range(FIELDS // PART):
            fetch(k, half).start()

    def field(i, carry):
        k, f = i // FIELDS, i % FIELDS

        @pl.when(f % PART == 0)
        def _():
            fetch(k, f // PART).wait()

        for z in range(HALF):
            low, high = images[k, f, z], images[k, f, z + HALF]
            row0 = jnp.where(even, low, pltpu.roll(high, 1, 0))
            row1 = jnp.where(even, pltpu.roll(low, 7, 0), high)
            mine = jnp.where(first, row0, row1)
            rest = jnp.where(first, row1, row0)
            own[k, f, z] = mine
            far[k, f, z] = rest
            own_copy[k, f, z] = mine
            far_copy[k, f, z] = rest
        return carry

    lax.fori_loop(0, 2 * FIELDS, field, 0)


def step_image(center, beside, halo, j, stepped, g):
    even = even_sublanes()
    lane = lax.broadcasted_iota(jnp.int32, TILE, 1)
    at_first, at_last = lane == 0, lane == 127
    for z in range(HALF):
        cells, sums = [], []
        for f in range(FIELDS):
            c = center[j, f, z]
            if z < HALF - 1:
                raised = center[j, f, z + 1]
            else:
                raised = jnp.where(even, pltpu.roll(center[j, f, 0], 7, 0), c)
            if z > 0:
                lowered = center[j, f, z - 1]
            else:
                lowered = jnp.where(even, c, pltpu.roll(center[j, f, HALF - 1], 1, 0))
            ahead = pltpu.roll(c, 127, 1)
            ahead = jnp.where(at_last, pltpu.roll(ahead, 6, 0), ahead)
            behind = pltpu.roll(c, 1, 1)
            behind = jnp.where(at_first, pltpu.roll(behind, 2, 0), behind)
            around = (beside[j, f, z] + halo[j, f, z]) + (raised + lowered) + (ahead + behind)
            cells.append(c)
            sums.append(around)
        squares = [cells[i] * cells[i] for i in range(4)]
        total = (squares[0] + squares[1]) + (squares[2] + squares[3])
        pulls = []
        for s in range(2):
            value = cells[4 + s]
            for i in range(4):
                value = value - EQUILIBRIUM[i][s] * cells[i]
            pulls.append((TIME_STEP * COUPLING) * value)
        for i in range(4):
            gain = (1.0 - 6.0 * TIME_STEP * KAPPA_PHASE) - (TIME_STEP * 2.0 * BARRIER) * (
                total - squares[i]
            )
            out = gain * cells[i] + (TIME_STEP * KAPPA_PHASE) * sums[i]
            out = out + (EQUILIBRIUM[i][0] * pulls[0] + EQUILIBRIUM[i][1] * pulls[1])
            stepped[cell(g, i, z)] = out
        for s in range(2):
            out = (1.0 - 6.0 * TIME_STEP * KAPPA_SOLUTE) * cells[4 + s]
            out = out + (TIME_STEP * KAPPA_SOLUTE) * sums[4 + s] - pulls[s]
            stepped[cell(g, 4 + s, z)] = out


def gap_square(one, k, other, m, f):
    terms = []
    for z in range(HALF):
        gap = one[cell(k, f, z)] - other[cell(m, f, z)]
        terms.append(gap * gap)
    while len(terms) > 1:
        terms = [a + b for a, b in zip(terms[::2], terms[1::2])]
    return terms[0]


def own_kernel(own, far, halo, stepped):
    def one(j, carry):
        step_image(own, far, halo, j, stepped, j)
        return carry

    lax.fori_loop(0, 2, one, 0)
    zero = jnp.zeros(TILE, jnp.float32)
    stepped[CELLS] = lax.fori_loop(
        0, FIELDS, lambda f, total: total + gap_square(stepped, 1, stepped, 0, f), zero
    )
    for p in range(CELLS + 1, stepped.shape[0]):
        stepped[p] = zero


def sibling_kernel(own, far, halo, mine, stepped):
    core = lax.axis_index("img")

    def one(j, carry):
        step_image(own, far, halo, j, stepped, j)
        return carry

    lax.fori_loop(0, 2, one, 0)

    def gather(f, sums):
        cross = gap_square(mine, 1 - core, stepped, core, f)
        return (sums[0] + cross, sums[1] + gap_square(stepped, 1, stepped, 0, f))

    zero = jnp.zeros(TILE, jnp.float32)
    cross_gap, other_gap = lax.fori_loop(0, FIELDS, gather, (zero, zero))
    own_gap = mine[CELLS]
    lane = lax.broadcasted_iota(jnp.int32, TILE, 1)
    out = jnp.where(lane == 2 * core, jnp.sum(own_gap), zero)
    out = jnp.where(lane == 1, jnp.sum(cross_gap), out)
    stepped[CELLS] = jnp.where(lane == 2 - 2 * core, jnp.sum(other_gap), out)


def add_kernel(near, rest, rows):
    total = near[CELLS, 0:1, :] + rest[CELLS, 0:1, :]

    def row(p, carry):
        rows[p] = total
        return carry

    lax.fori_loop(0, rows.shape[0], row, 0, unroll=16)


def total_tile(parts):
    terms = [parts[p] for p in range(parts.shape[0])]
    while len(terms) > 1:
        terms = [a + b for a, b in zip(terms[::2], terms[1::2])]
    return terms[0]


def combine_kernel(
    parts, near_own, near_sib, far_own, far_sib, target_new, knots, new, written
):
    core = lax.axis_index("img")
    even = even_sublanes()
    first = jnp.full(TILE, core, jnp.int32) == 0
    total = total_tile(parts)
    lane = lax.broadcasted_iota(jnp.int32, TILE, 1)
    l1, l2, l3 = (
        jnp.sqrt(1.0 + jnp.full(TILE, jnp.sum(jnp.where(lane == k, total, 0.0))))
        for k in range(3)
    )
    whole = l1 + l2 + l3
    k1, k2, k3 = l1 / whole, (l1 + l2) / whole, whole / whole
    w0, w1, w2 = k1, k2 - k1, k3 - k2
    main1, main2 = 2.0 * (w0 + w1), 2.0 * (w1 + w2)
    det = main1 * main2 - w1 * w1
    scale = 6.0 / det
    i0, i1, i2 = 1.0 / w0, 1.0 / w1, 1.0 / w2
    bend1 = (
        -main2 * i0 * scale,
        (main2 + w1) * i1 * scale,
        -w1 * i2 * scale,
    )
    bend2 = (
        w1 * i0 * scale,
        -(main1 + w1) * i1 * scale,
        main1 * i2 * scale,
    )
    zero = jnp.zeros(TILE, jnp.float32)
    gaps = []
    for j in range(2):
        target = jnp.where(first, jnp.float32(j / 3.0), jnp.float32((j + 2) / 3.0))
        below = 1 + sum((k <= target).astype(jnp.int32) for k in (k1, k2, k3)) - 1
        at = jnp.clip(below, 0, 2)
        h = jnp.where(at == 0, w0, jnp.where(at == 1, w1, w2))
        right = jnp.where(at == 0, k1, jnp.where(at == 1, k2, k3))
        a = (right - target) / h
        b = 1.0 - a
        curve = h * h * (1.0 / 6.0)
        ca, cb = (a * a * a - a) * curve, (b * b * b - b) * curve
        v = [jnp.where(at == k, a, jnp.where(at == k - 1, b, zero)) for k in range(4)]
        c1 = jnp.where(at == 1, ca, jnp.where(at == 0, cb, zero))
        c2 = jnp.where(at == 2, ca, jnp.where(at == 1, cb, zero))
        above = (v[1] + v[2] + v[3], v[2] + v[3], v[3])
        gaps.append([above[m] + (c1 * bend1[m] + c2 * bend2[m]) for m in range(3)])
    knots[0] = jnp.float32(0.0)
    knots[1] = k1[0, 0]
    knots[2] = k2[0, 0]
    knots[3] = k3[0, 0]

    def resampled(rows, f, z):
        s = [rows[k // 2][cell(k % 2, f, z)] for k in range(4)]
        d = [s[k + 1] - s[k] for k in range(3)]
        out = []
        for j in range(2):
            g = gaps[j]
            out.append((s[0] + g[0] * d[0]) + (g[1] * d[1] + g[2] * d[2]))
        return out

    def store(j, half):
        part = (j, pl.ds(half * (FIELDS // 2), FIELDS // 2))
        return pltpu.make_async_copy(new.at[part], target_new.at[part], written.at[j, half])

    def write(even_rows, odd_rows):
        def field(f, carry):
            for z in range(HALF):
                row0, row1 = resampled(even_rows, f, z), resampled(odd_rows, f, z)
                for j in range(2):
                    new[j, f, z] = jnp.where(even, row0[j], pltpu.roll(row1[j], 1, 0))
                    new[j, f, z + HALF] = jnp.where(even, pltpu.roll(row0[j], 7, 0), row1[j])
            return carry

        for half in range(2):
            lax.fori_loop(half * (FIELDS // 2), (half + 1) * (FIELDS // 2), field, 0)
            for j in range(2):
                store(j, half).start()

    @pl.when(core == 0)
    def _():
        write((near_own, near_sib), (far_own, far_sib))

    @pl.when(core == 1)
    def _():
        write((far_sib, far_own), (near_sib, near_own))

    for half in range(2):
        for j in range(2):
            store(j, half).wait()


def in_hbm(x):
    return pltpu.with_memory_space_constraint(x, pltpu.HBM)


def in_vmem(x):
    return pltpu.with_memory_space_constraint(x, pltpu.VMEM)


def vmem(*shape):
    return pltpu.VMEM(shape, jnp.float32)


def per_device(images):
    everyone = ("img",) + STRIP
    strips = lax.axis_size(STRIP)
    tiles = images.reshape(2, FIELDS, PLANES, 2, 4, 128).transpose(0, 1, 2, 4, 3, 5)
    tiles = tiles.reshape(2, FIELDS, PLANES, *TILE)
    packed = (2, FIELDS, HALF) + TILE
    own, far, far_copy, own_copy = pl.pallas_call(
        pack_kernel,
        out_shape=(vmem(*packed),) * 4,
        in_specs=[pl.BlockSpec(memory_space=pl.ANY)],
        out_specs=(VMEM,) * 4,
        scratch_shapes=[
            pltpu.VMEM((2, FIELDS, PLANES) + TILE, jnp.float32),
            pltpu.SemaphoreType.DMA((2, FIELDS // PART)),
        ],
        compiler_params=PARAMS,
    )(in_hbm(tiles))
    right = [(i + 1) % strips for i in range(strips)]
    left = [(i - 1) % strips for i in range(strips)]
    same = [(i, right[i]) for i in range(strips)]
    same += [(strips + i, strips + left[i]) for i in range(strips)]
    cross = [(i, strips + left[i]) for i in range(strips)]
    cross += [(strips + i, right[i]) for i in range(strips)]
    halo_own = lax.ppermute(far_copy, everyone, same)
    halo_sibling = lax.ppermute(own_copy, everyone, cross)
    swap = [(0, 1), (1, 0)]
    sib_far = lax.ppermute(own, "img", swap)
    sib_own = lax.ppermute(far, "img", swap)
    cost = pl.CostEstimate(flops=1_500_000, bytes_accessed=1_500_000, transcendentals=0)
    near_own = pl.pallas_call(
        own_kernel,
        out_shape=vmem(CELLS + PAD, *TILE),
        in_specs=[VMEM] * 3,
        out_specs=VMEM,
        compiler_params=PARAMS,
        cost_estimate=cost,
    )(*map(in_vmem, (own, far, halo_own)))
    far_sib = lax.ppermute(near_own, "img", swap)
    near_sib = pl.pallas_call(
        sibling_kernel,
        out_shape=vmem(CELLS + 1, *TILE),
        in_specs=[VMEM] * 4,
        out_specs=VMEM,
        compiler_params=PARAMS,
        cost_estimate=cost,
    )(*map(in_vmem, (sib_own, sib_far, halo_sibling, near_own)))
    far_own = lax.ppermute(near_sib, "img", swap)
    far_own, far_sib = lax.optimization_barrier((far_own, far_sib))
    parts = pl.pallas_call(
        add_kernel,
        out_shape=vmem(strips, 1, TILE[1]),
        in_specs=[VMEM] * 2,
        out_specs=VMEM,
        compiler_params=PARAMS,
    )(in_vmem(near_sib), in_vmem(far_own))
    parts = lax.all_to_all(parts, STRIP, 0, 0, tiled=True)
    parts = parts.reshape(-1, *TILE)
    new, knots = pl.pallas_call(
        combine_kernel,
        out_shape=(
            jax.ShapeDtypeStruct((2, FIELDS, PLANES) + TILE, jnp.float32),
            jax.ShapeDtypeStruct((4,), jnp.float32),
        ),
        in_specs=[VMEM] * 5,
        out_specs=(
            pl.BlockSpec(memory_space=pl.ANY),
            pl.BlockSpec(memory_space=pltpu.SMEM),
        ),
        scratch_shapes=[
            pltpu.VMEM((2, FIELDS, PLANES) + TILE, jnp.float32),
            pltpu.SemaphoreType.DMA((2, 2)),
        ],
        compiler_params=PARAMS,
    )(*map(in_vmem, (parts, near_own, near_sib, far_own, far_sib)))
    new = new.reshape(2, FIELDS, PLANES, 4, 2, 128).transpose(0, 1, 2, 4, 3, 5)
    return new.reshape(2, FIELDS, PLANES, 2, 512), knots


def solution(mesh):
    fine = Mesh(mesh.devices.reshape(2, 8, 8, 4), ("img",) + STRIP)
    spec = P("img", None, None, STRIP, None)
    return jax.shard_map(
        per_device, mesh=fine, in_specs=(spec,), out_specs=(spec, P()), check_vma=False
    )
```

```python
import jax
import jax.numpy as jnp
from jax import lax
from jax.experimental import pallas as pl
from jax.experimental.pallas import tpu as pltpu
from jax.sharding import Mesh, PartitionSpec as P

KAPPA_PHASE = 1.0
KAPPA_SOLUTE = 0.6
BARRIER = 1.5
COUPLING = 2.0
TIME_STEP = 0.05
EQUILIBRIUM = ((0.8, 0.1), (0.1, 0.8), (0.1, 0.1), (0.45, 0.45))
STRIP = ("z", "y", "x")
FIELDS, PLANES = 6, 16
HALF = PLANES // 2
PART = 1
CELLS = 2 * FIELDS * HALF
PAD = 8
TILE = (8, 128)
VMEM = pl.BlockSpec(memory_space=pltpu.VMEM)
PARAMS = pltpu.CompilerParams(vmem_limit_bytes=48 * 1024 * 1024)


def cell(k, f, z):
    return (k * FIELDS + f) * HALF + z


def even_sublanes():
    return lax.broadcasted_iota(jnp.int32, TILE, 0) % 2 == 0


def pack_kernel(source, own, far, far_copy, own_copy, images, arrived):
    core = lax.axis_index("img")
    even = even_sublanes()
    first = jnp.full(TILE, core, jnp.int32) == 0

    def fetch(k, half):
        part = (k, pl.ds(half * PART, PART))
        return pltpu.make_async_copy(source.at[part], images.at[part], arrived.at[k, half])

    for k in range(2):
        for half in range(FIELDS // PART):
            fetch(k, half).start()

    def field(i, carry):
        k, f = i // FIELDS, i % FIELDS

        @pl.when(f % PART == 0)
        def _():
            fetch(k, f // PART).wait()

        for z in range(HALF):
            low, high = images[k, f, z], images[k, f, z + HALF]
            row0 = jnp.where(even, low, pltpu.roll(high, 1, 0))
            row1 = jnp.where(even, pltpu.roll(low, 7, 0), high)
            mine = jnp.where(first, row0, row1)
            rest = jnp.where(first, row1, row0)
            own[k, f, z] = mine
            far[k, f, z] = rest
            own_copy[k, f, z] = mine
            far_copy[k, f, z] = rest
        return carry

    lax.fori_loop(0, 2 * FIELDS, field, 0)


def step_image(center, beside, halo, j, stepped, g):
    even = even_sublanes()
    lane = lax.broadcasted_iota(jnp.int32, TILE, 1)
    at_first, at_last = lane == 0, lane == 127
    for z in range(HALF):
        cells, sums = [], []
        for f in range(FIELDS):
            c = center[j, f, z]
            if z < HALF - 1:
                raised = center[j, f, z + 1]
            else:
                raised = jnp.where(even, pltpu.roll(center[j, f, 0], 7, 0), c)
            if z > 0:
                lowered = center[j, f, z - 1]
            else:
                lowered = jnp.where(even, c, pltpu.roll(center[j, f, HALF - 1], 1, 0))
            ahead = pltpu.roll(c, 127, 1)
            ahead = jnp.where(at_last, pltpu.roll(ahead, 6, 0), ahead)
            behind = pltpu.roll(c, 1, 1)
            behind = jnp.where(at_first, pltpu.roll(behind, 2, 0), behind)
            around = (beside[j, f, z] + halo[j, f, z]) + (raised + lowered) + (ahead + behind)
            cells.append(c)
            sums.append(around)
        squares = [cells[i] * cells[i] for i in range(4)]
        total = (squares[0] + squares[1]) + (squares[2] + squares[3])
        pulls = []
        for s in range(2):
            value = cells[4 + s]
            for i in range(4):
                value = value - EQUILIBRIUM[i][s] * cells[i]
            pulls.append((TIME_STEP * COUPLING) * value)
        for i in range(4):
            gain = (1.0 - 6.0 * TIME_STEP * KAPPA_PHASE) - (TIME_STEP * 2.0 * BARRIER) * (
                total - squares[i]
            )
            out = gain * cells[i] + (TIME_STEP * KAPPA_PHASE) * sums[i]
            out = out + (EQUILIBRIUM[i][0] * pulls[0] + EQUILIBRIUM[i][1] * pulls[1])
            stepped[cell(g, i, z)] = out
        for s in range(2):
            out = (1.0 - 6.0 * TIME_STEP * KAPPA_SOLUTE) * cells[4 + s]
            out = out + (TIME_STEP * KAPPA_SOLUTE) * sums[4 + s] - pulls[s]
            stepped[cell(g, 4 + s, z)] = out


def gap_square(one, k, other, m, f):
    terms = []
    for z in range(HALF):
        gap = one[cell(k, f, z)] - other[cell(m, f, z)]
        terms.append(gap * gap)
    while len(terms) > 1:
        terms = [a + b for a, b in zip(terms[::2], terms[1::2])]
    return terms[0]


def own_kernel(own, far, halo, stepped):
    def one(j, carry):
        step_image(own, far, halo, j, stepped, j)
        return carry

    lax.fori_loop(0, 2, one, 0)
    zero = jnp.zeros(TILE, jnp.float32)
    stepped[CELLS] = lax.fori_loop(
        0, FIELDS, lambda f, total: total + gap_square(stepped, 1, stepped, 0, f), zero
    )
    for p in range(CELLS + 1, stepped.shape[0]):
        stepped[p] = zero


def sibling_kernel(own, far, halo, mine, stepped):
    core = lax.axis_index("img")

    def one(j, carry):
        step_image(own, far, halo, j, stepped, j)
        return carry

    lax.fori_loop(0, 2, one, 0)

    def gather(f, sums):
        cross = gap_square(mine, 1 - core, stepped, core, f)
        return (sums[0] + cross, sums[1] + gap_square(stepped, 1, stepped, 0, f))

    zero = jnp.zeros(TILE, jnp.float32)
    cross_gap, other_gap = lax.fori_loop(0, FIELDS, gather, (zero, zero))
    own_gap = mine[CELLS]
    lane = lax.broadcasted_iota(jnp.int32, TILE, 1)
    out = jnp.where(lane == 2 * core, jnp.sum(own_gap), zero)
    out = jnp.where(lane == 1, jnp.sum(cross_gap), out)
    stepped[CELLS] = jnp.where(lane == 2 - 2 * core, jnp.sum(other_gap), out)


def add_kernel(near, rest, rows):
    total = near[CELLS, 0:1, :] + rest[CELLS, 0:1, :]

    def row(p, carry):
        rows[p] = total
        return carry

    lax.fori_loop(0, rows.shape[0], row, 0, unroll=16)


def total_tile(parts):
    terms = [parts[p] for p in range(parts.shape[0])]
    while len(terms) > 1:
        terms = [a + b for a, b in zip(terms[::2], terms[1::2])]
    return terms[0]


def combine_kernel(parts, near_own, near_sib, far_own, far_sib, new, knots):
    core = lax.axis_index("img")
    even = even_sublanes()
    first = jnp.full(TILE, core, jnp.int32) == 0
    total = total_tile(parts)
    lane = lax.broadcasted_iota(jnp.int32, TILE, 1)
    l1, l2, l3 = (
        jnp.sqrt(1.0 + jnp.full(TILE, jnp.sum(jnp.where(lane == k, total, 0.0))))
        for k in range(3)
    )
    whole = l1 + l2 + l3
    k1, k2, k3 = l1 / whole, (l1 + l2) / whole, whole / whole
    w0, w1, w2 = k1, k2 - k1, k3 - k2
    main1, main2 = 2.0 * (w0 + w1), 2.0 * (w1 + w2)
    det = main1 * main2 - w1 * w1
    scale = 6.0 / det
    i0, i1, i2 = 1.0 / w0, 1.0 / w1, 1.0 / w2
    bend1 = (
        -main2 * i0 * scale,
        (main2 + w1) * i1 * scale,
        -w1 * i2 * scale,
    )
    bend2 = (
        w1 * i0 * scale,
        -(main1 + w1) * i1 * scale,
        main1 * i2 * scale,
    )
    zero = jnp.zeros(TILE, jnp.float32)
    gaps = []
    for j in range(2):
        target = jnp.where(first, jnp.float32(j / 3.0), jnp.float32((j + 2) / 3.0))
        below = 1 + sum((k <= target).astype(jnp.int32) for k in (k1, k2, k3)) - 1
        at = jnp.clip(below, 0, 2)
        h = jnp.where(at == 0, w0, jnp.where(at == 1, w1, w2))
        right = jnp.where(at == 0, k1, jnp.where(at == 1, k2, k3))
        a = (right - target) / h
        b = 1.0 - a
        curve = h * h * (1.0 / 6.0)
        ca, cb = (a * a * a - a) * curve, (b * b * b - b) * curve
        v = [jnp.where(at == k, a, jnp.where(at == k - 1, b, zero)) for k in range(4)]
        c1 = jnp.where(at == 1, ca, jnp.where(at == 0, cb, zero))
        c2 = jnp.where(at == 2, ca, jnp.where(at == 1, cb, zero))
        above = (v[1] + v[2] + v[3], v[2] + v[3], v[3])
        gaps.append([above[m] + (c1 * bend1[m] + c2 * bend2[m]) for m in range(3)])
    knots[0] = jnp.float32(0.0)
    knots[1] = k1[0, 0]
    knots[2] = k2[0, 0]
    knots[3] = k3[0, 0]

    def resampled(rows, f, z):
        s = [rows[k // 2][cell(k % 2, f, z)] for k in range(4)]
        d = [s[k + 1] - s[k] for k in range(3)]
        out = []
        for j in range(2):
            g = gaps[j]
            out.append((s[0] + g[0] * d[0]) + (g[1] * d[1] + g[2] * d[2]))
        return out

    def write(even_rows, odd_rows):
        def field(f, carry):
            for z in range(HALF):
                row0, row1 = resampled(even_rows, f, z), resampled(odd_rows, f, z)
                for j in range(2):
                    new[j, f, z] = jnp.where(even, row0[j], pltpu.roll(row1[j], 1, 0))
                    new[j, f, z + HALF] = jnp.where(even, pltpu.roll(row0[j], 7, 0), row1[j])
            return carry

        lax.fori_loop(0, FIELDS, field, 0)

    @pl.when(core == 0)
    def _():
        write((near_own, near_sib), (far_own, far_sib))

    @pl.when(core == 1)
    def _():
        write((far_sib, far_own), (near_sib, near_own))


def in_hbm(x):
    return pltpu.with_memory_space_constraint(x, pltpu.HBM)


def in_vmem(x):
    return pltpu.with_memory_space_constraint(x, pltpu.VMEM)


def vmem(*shape):
    return pltpu.VMEM(shape, jnp.float32)


def per_device(images):
    everyone = ("img",) + STRIP
    strips = lax.axis_size(STRIP)
    tiles = images.reshape(2, FIELDS, PLANES, 2, 4, 128).transpose(0, 1, 2, 4, 3, 5)
    tiles = tiles.reshape(2, FIELDS, PLANES, *TILE)
    packed = (2, FIELDS, HALF) + TILE
    own, far, far_copy, own_copy = pl.pallas_call(
        pack_kernel,
        out_shape=(vmem(*packed),) * 4,
        in_specs=[pl.BlockSpec(memory_space=pl.ANY)],
        out_specs=(VMEM,) * 4,
        scratch_shapes=[
            pltpu.VMEM((2, FIELDS, PLANES) + TILE, jnp.float32),
            pltpu.SemaphoreType.DMA((2, FIELDS // PART)),
        ],
        compiler_params=PARAMS,
    )(in_hbm(tiles))
    right = [(i + 1) % strips for i in range(strips)]
    left = [(i - 1) % strips for i in range(strips)]
    same = [(i, right[i]) for i in range(strips)]
    same += [(strips + i, strips + left[i]) for i in range(strips)]
    cross = [(i, strips + left[i]) for i in range(strips)]
    cross += [(strips + i, right[i]) for i in range(strips)]
    halo_own = lax.ppermute(far_copy, everyone, same)
    halo_sibling = lax.ppermute(own_copy, everyone, cross)
    swap = [(0, 1), (1, 0)]
    sib_far = lax.ppermute(own, "img", swap)
    sib_own = lax.ppermute(far, "img", swap)
    cost = pl.CostEstimate(flops=1_500_000, bytes_accessed=1_500_000, transcendentals=0)
    near_own = pl.pallas_call(
        own_kernel,
        out_shape=vmem(CELLS + PAD, *TILE),
        in_specs=[VMEM] * 3,
        out_specs=VMEM,
        compiler_params=PARAMS,
        cost_estimate=cost,
    )(*map(in_vmem, (own, far, halo_own)))
    far_sib = lax.ppermute(near_own, "img", swap)
    near_sib = pl.pallas_call(
        sibling_kernel,
        out_shape=vmem(CELLS + 1, *TILE),
        in_specs=[VMEM] * 4,
        out_specs=VMEM,
        compiler_params=PARAMS,
        cost_estimate=cost,
    )(*map(in_vmem, (sib_own, sib_far, halo_sibling, near_own)))
    far_own = lax.ppermute(near_sib, "img", swap)
    far_own, far_sib = lax.optimization_barrier((far_own, far_sib))
    parts = pl.pallas_call(
        add_kernel,
        out_shape=vmem(strips, 1, TILE[1]),
        in_specs=[VMEM] * 2,
        out_specs=VMEM,
        compiler_params=PARAMS,
    )(in_vmem(near_sib), in_vmem(far_own))
    parts = lax.all_to_all(parts, STRIP, 0, 0, tiled=True)
    parts = parts.reshape(-1, *TILE)
    new, knots = pl.pallas_call(
        combine_kernel,
        out_shape=(
            jax.ShapeDtypeStruct((2, FIELDS, PLANES) + TILE, jnp.float32),
            jax.ShapeDtypeStruct((4,), jnp.float32),
        ),
        in_specs=[VMEM] * 5,
        out_specs=(VMEM, pl.BlockSpec(memory_space=pltpu.SMEM)),
        compiler_params=PARAMS,
    )(*map(in_vmem, (parts, near_own, near_sib, far_own, far_sib)))
    new = new.reshape(2, FIELDS, PLANES, 4, 2, 128).transpose(0, 1, 2, 4, 3, 5)
    return new.reshape(2, FIELDS, PLANES, 2, 512), knots


def solution(mesh):
    fine = Mesh(mesh.devices.reshape(2, 8, 8, 4), ("img",) + STRIP)
    spec = P("img", None, None, STRIP, None)
    return jax.shard_map(
        per_device, mesh=fine, in_specs=(spec,), out_specs=(spec, P()), check_vma=False
    )
```
